32 devices in a mesh: dp: 8 (over y, x, core), seq: 4 (over z).
Axes of the slice: x: 2, y: 2, z: 4, core: 2. Of those that a mesh axis runs over, the one named last changes fastest.
Arguments:
- inputs: bfloat16 [16, 1024, 1408], P('dp', 'seq'), may hold values from -6 to 6
- skipped: bfloat16 [16, 1024, 1408], P('dp', 'seq'), may hold values from -6 to 6
- text_rows: bfloat16 [16, 256, 1024], P('dp', 'seq'), may hold values from -6 to 6
- condition: bfloat16 [16, 1408], P('dp'), may hold values from -6 to 6
- cotangent: bfloat16 [16, 1024, 1408], P('dp', 'seq'), may hold values from -6 to 6
- norm_gains: float32 [7040], replicated, may hold values from 0.1 to 1.9
- skip_weight: bfloat16 [2816, 1408], P('seq', 'dp'), may hold values from -0.109375 to 0.109375
- shift_weight: bfloat16 [1408, 1408], P('seq', 'dp'), may hold values from -0.15625 to 0.15625
- query_key_weight: bfloat16 [1408, 2816], P('seq', 'dp'), may hold values from -0.15625 to 0.15625
- value_weight: bfloat16 [1408, 1408], P('seq', 'dp'), may hold values from -0.15625 to 0.15625
- self_output: bfloat16 [1408, 1408], P('seq', 'dp'), may hold values from -0.875 to 0.875
- cross_query: bfloat16 [1408, 1408], P('seq', 'dp'), may hold values from -0.15625 to 0.15625
- cross_memory: bfloat16 [1024, 2816], P('seq', 'dp'), may hold values from -0.1875 to 0.1875
- cross_output: bfloat16 [1408, 1408], P('seq', 'dp'), may hold values from -0.875 to 0.875
- up_weight: bfloat16 [1408, 6144], P('seq', 'dp'), may hold values from -0.15625 to 0.15625
- down_weight: bfloat16 [6144, 1408], P('seq', 'dp'), may hold values from -0.078125 to 0.078125
Outputs:
- blended_out: bfloat16 [16, 1024, 1408], P('dp', 'seq')
- grad_input: float32 [16, 1024, 1408], P('dp', 'seq')
- grad_skipped: float32 [16, 1024, 1408], P('dp', 'seq')
- grad_text: float32 [16, 256, 1024], P('dp', 'seq')
- grad_gains: float32 [7040], replicated
- grad_skip_weight: float32 [2816, 1408], P('seq', 'dp')
- grad_shift_weight: float32 [1408, 1408], P('seq', 'dp')
- grad_query_key_weight: float32 [1408, 2816], P('seq', 'dp')
- grad_value_weight: float32 [1408, 1408], P('seq', 'dp')
- grad_self_output: float32 [1408, 1408], P('seq', 'dp')
- grad_cross_query: float32 [1408, 1408], P('seq', 'dp')
- grad_cross_memory: float32 [1024, 2816], P('seq', 'dp')
- grad_cross_output: float32 [1408, 1408], P('seq', 'dp')
- grad_up_weight: float32 [1408, 6144], P('seq', 'dp')
- grad_down_weight: float32 [6144, 1408], P('seq', 'dp')
The draws below stay inside these ranges and needn't reach their ends.
All inputs are finite; a program needn't handle non-finite values.
Results may differ from the reference program's by a relative error of at most 0.02.
Values may be sent and summed in bfloat16 or wider, within the bound.
No kernel may reach another device: no remote copies, remote signals or barrier semaphores. Data moves between devices by JAX's collectives and lax.ppermute only.
A program may use at most 384 MiB of HBM per device.

```python
import jax
import jax.numpy as jnp
from jax import lax

D = 1408
H = 16
HD = 88
FF = 6144
TW = 1024
TXT = 256
GRID = 32
LEN = 1024
LATENTS = 16


def block_scale(own_key, extent, shards, smallest, largest):
    factor_of, own = 1.0, jax.random.fold_in(own_key, 6)
    for dim, parts in shards:
        heights = jnp.exp(jax.random.uniform(jax.random.fold_in(own, dim), (parts,), jnp.float32, smallest / len(shards), largest / len(shards)))
        factor_of = factor_of * jnp.repeat(heights, extent[dim] // parts).reshape([-1 if axis == dim else 1 for axis in range(len(extent))])
    return factor_of


def bell_draw(key, extent, width, reach, split=(), kind=jnp.bfloat16):
    loudness = block_scale(key, extent, split, -0.22, 0.18) if split else 1.0
    entries = jax.random.normal(key, extent, jnp.float32) * width * loudness
    return jnp.minimum(jnp.maximum(entries, -reach), reach).astype(kind)


def setup_inputs(seed: int = 0) -> dict:
    key_of = jax.random.split(jax.random.key(seed), 17)
    return {
        "inputs": bell_draw(key_of[0], (LATENTS, LEN, D), 1.0, 6.0, ((0, 8), (1, 4))),
        "skipped": bell_draw(key_of[1], (LATENTS, LEN, D), 1.0, 6.0, ((0, 8), (1, 4))),
        "text_rows": bell_draw(key_of[2], (LATENTS, TXT, TW), 1.0, 6.0, ((0, 8), (1, 4))),
        "condition": bell_draw(key_of[3], (LATENTS, D), 1.0, 6.0, ((0, 8),)),
        "cotangent": bell_draw(key_of[4], (LATENTS, LEN, D), 1.0, 6.0, ((0, 8), (1, 4))),
        "norm_gains": jnp.clip(1.0 + 0.18 * jax.random.normal(key_of[5], (5 * D,), jnp.float32), 0.1, 1.9),
        "skip_weight": bell_draw(key_of[6], (2 * D, D), (2 * D) ** -0.5, 0.109375, ((0, 4), (1, 8))),
        "shift_weight": bell_draw(key_of[7], (D, D), D ** -0.5, 0.15625, ((0, 4), (1, 8))),
        "query_key_weight": bell_draw(key_of[8], (D, 2 * D), D ** -0.5, 0.15625, ((0, 4), (1, 8))),
        "value_weight": bell_draw(key_of[9], (D, D), D ** -0.5, 0.15625, ((0, 4), (1, 8))),
        "self_output": bell_draw(key_of[10], (D, D), (D // 32) ** -0.5, 0.875, ((0, 4), (1, 8))),
        "cross_query": bell_draw(key_of[11], (D, D), D ** -0.5, 0.15625, ((0, 4), (1, 8))),
        "cross_memory": bell_draw(key_of[12], (TW, 2 * D), TW ** -0.5, 0.1875, ((0, 4), (1, 8))),
        "cross_output": bell_draw(key_of[13], (D, D), (D // 32) ** -0.5, 0.875, ((0, 4), (1, 8))),
        "up_weight": bell_draw(key_of[14], (D, FF), D ** -0.5, 0.15625, ((0, 4), (1, 8))),
        "down_weight": bell_draw(key_of[15], (FF, D), FF ** -0.5, 0.078125, ((0, 4), (1, 8))),
    }


@jax.custom_vjp
def low(v):
    return lax.optimization_barrier(v.astype(jnp.bfloat16)).astype(jnp.float32)

@jax.custom_vjp
def low_back(v):
    return v

def low_keep(v):
    return (low(v), None)

def low_pass(kept, grad):
    return (grad,)

def back_keep(v):
    return (v, None)

def back_low(kept, grad):
    return (low(grad),)
low.defvjp(low_keep, low_pass)
low_back.defvjp(back_keep, back_low)
epsilon = 1e-06

def matmul(matrix_a, matrix_b):
    return jnp.dot(matrix_a, matrix_b, precision=lax.Precision.HIGHEST)

def normalize(values):
    center = values - lax.optimization_barrier(jnp.mean(values, axis=-1, keepdims=True))
    spread = lax.optimization_barrier(jnp.mean(center * center, axis=-1, keepdims=True))
    return center * lax.rsqrt(spread + epsilon)

def rotary_tables(token_total):
    position = jnp.arange(token_total, dtype=jnp.int32)
    quarter = HD // 4
    frequency = jnp.power(10000.0, -jnp.arange(quarter, dtype=jnp.float32) / quarter)
    row_angle = (position // GRID).astype(jnp.float32)[:, None, None] * frequency
    col_angle = (position % GRID).astype(jnp.float32)[:, None, None] * frequency
    return (jnp.cos(row_angle), jnp.sin(row_angle), jnp.cos(col_angle), jnp.sin(col_angle))

def rotate(per_head, tables):
    row_cos, row_sin, col_cos, col_sin = tables
    quarter = per_head.shape[-1] // 4
    part_one = per_head[..., :quarter]
    part_two = per_head[..., quarter:2 * quarter]
    part_three = per_head[..., 2 * quarter:3 * quarter]
    part_four = per_head[..., 3 * quarter:]
    return jnp.concatenate([part_one * row_cos - part_two * row_sin, part_two * row_cos + part_one * row_sin, part_three * col_cos - part_four * col_sin, part_four * col_cos + part_three * col_sin], axis=-1)

def attend(queries, key_heads, value_heads):
    scores = low_back(jnp.einsum('qhd,khd->hqk', queries, key_heads, precision=lax.Precision.HIGHEST) * HD ** (-0.5))
    softmaxed = low(jax.nn.softmax(scores, axis=-1))
    blended = jnp.einsum('hqk,khd->qhd', softmaxed, value_heads, precision=lax.Precision.HIGHEST)
    return blended.reshape(blended.shape[0], -1)

def block(weights, gains32, latent_in, latent_skip, latent_text, latent_cond, tables):
    skip_w, shift_w, pair_w, value_w, self_w, cq_w, memory_w, cout_w, up_w, down_w = weights
    gain_skip = gains32[:2 * D]
    gain_one = gains32[2 * D:3 * D]
    gain_two = gains32[3 * D:4 * D]
    gain_three = gains32[4 * D:]
    token_total = latent_in.shape[0]
    text_total = latent_text.shape[0]
    joined = jnp.concatenate([latent_in, latent_skip], axis=-1)
    level_zero = low(normalize(joined) * gain_skip)
    stream_zero = low_back(matmul(level_zero, skip_w))
    cond_act = low(jax.nn.silu(latent_cond))
    shift_row = matmul(cond_act[None, :], shift_w)
    level_one = low(normalize(stream_zero) * gain_one + shift_row)
    projected = low_back(jnp.concatenate([matmul(level_one, pair_w), matmul(level_one, value_w)], axis=-1))
    queries = low(rotate(normalize(projected[:, :D].reshape(token_total, H, HD)), tables))
    key_heads = low(rotate(normalize(projected[:, D:2 * D].reshape(token_total, H, HD)), tables))
    value_heads = low(projected[:, 2 * D:].reshape(token_total, H, HD))
    attended = low(low_back(attend(queries, key_heads, value_heads)))
    stream_one = stream_zero + low_back(matmul(attended, self_w))
    level_two = low(normalize(stream_one) * gain_two)
    cross_proj = low_back(matmul(level_two, cq_w))
    cross_heads = low(normalize(cross_proj.reshape(token_total, H, HD)))
    memory_proj = low_back(matmul(latent_text, memory_w))
    memory_keys = low(normalize(memory_proj[:, :D].reshape(text_total, H, HD)))
    memory_values = low(memory_proj[:, D:].reshape(text_total, H, HD))
    crossed = low(low_back(attend(cross_heads, memory_keys, memory_values)))
    stream_two = stream_one + low_back(matmul(crossed, cout_w))
    level_three = low(normalize(stream_two) * gain_three)
    hidden = low_back(matmul(level_three, up_w))
    activated = low(jax.nn.gelu(hidden, approximate=True))
    return stream_two + matmul(activated, down_w)

def reference(inputs, skipped, text_rows, condition, cotangent, norm_gains, skip_weight, shift_weight, query_key_weight, value_weight, self_output, cross_query, cross_memory, cross_output, up_weight, down_weight):
    weights = (skip_weight.astype(jnp.float32), shift_weight.astype(jnp.float32), query_key_weight.astype(jnp.float32), value_weight.astype(jnp.float32), self_output.astype(jnp.float32), cross_query.astype(jnp.float32), cross_memory.astype(jnp.float32), cross_output.astype(jnp.float32), up_weight.astype(jnp.float32), down_weight.astype(jnp.float32))
    gains32 = norm_gains.astype(jnp.float32)
    cond32 = condition.astype(jnp.float32)
    tables = rotary_tables(GRID * GRID)
    checked = jax.checkpoint(block)

    def whole(weight_set, gain_set, inputs32, skipped32, text32):

        def step(carry, item):
            latent_in, latent_skip, latent_text, latent_cond = item
            return (carry, checked(weight_set, gain_set, latent_in, latent_skip, latent_text, latent_cond, tables))
        _, outputs = lax.scan(step, jnp.zeros((), jnp.float32), (inputs32, skipped32, text32, cond32))
        return outputs
    result, pull = jax.vjp(whole, weights, gains32, inputs.astype(jnp.float32), skipped.astype(jnp.float32), text_rows.astype(jnp.float32))
    grad_weights, grad_gains, grad_in, grad_skip, grad_txt = pull(cotangent.astype(jnp.float32))
    return (result.astype(jnp.bfloat16), grad_in, grad_skip, grad_txt, grad_gains, grad_weights[0], grad_weights[1], grad_weights[2], grad_weights[3], grad_weights[4], grad_weights[5], grad_weights[6], grad_weights[7], grad_weights[8], grad_weights[9])
```

```python
import functools
import math

import jax
import jax.numpy as jnp
from jax import lax
from jax.experimental import pallas as pl
from jax.experimental.pallas import tpu as pltpu
from jax.sharding import Mesh
from jax.sharding import PartitionSpec as P

H = 16
HD = 88
GRID = 32
PAIR = 2 * HD

epsilon = 1e-06
SCALE = HD ** (-0.5)
SCALE_LOG2 = SCALE * math.log2(math.e)

f32 = jnp.float32
bf16 = jnp.bfloat16


def normalize(values, axis):
    center = values - jnp.mean(values, axis=axis, keepdims=True)
    spread = jnp.mean(center * center, axis=axis, keepdims=True)
    return center * lax.rsqrt(spread + epsilon)


def norm_gain(values, gain_vec):
    return normalize(values, 0) * gain_vec[:, None]


def shifted_norm(values, gain_vec, offset):
    return normalize(values, 0) * gain_vec[:, None] + offset[:, None]


def norm_gain_rows(values, gain_vec):
    return normalize(values, -1) * gain_vec


def gelu_tanh(values):
    return jax.nn.gelu(values, approximate=True)


def head_norm(flat):
    return normalize(flat.reshape(H, HD, flat.shape[-1]), 1).reshape(flat.shape)


def rotate(per_head, tables):
    row_cos, row_sin, col_cos, col_sin = tables
    quarter = per_head.shape[1] // 4
    part_one = per_head[:, :quarter]
    part_two = per_head[:, quarter : 2 * quarter]
    part_three = per_head[:, 2 * quarter : 3 * quarter]
    part_four = per_head[:, 3 * quarter :]
    return jnp.concatenate(
        [
            part_one * row_cos - part_two * row_sin,
            part_two * row_cos + part_one * row_sin,
            part_three * col_cos - part_four * col_sin,
            part_four * col_cos + part_three * col_sin,
        ],
        axis=1,
    )


def dot(a, b, dims=((1,), (0,))):
    return lax.dot_general(a, b, (dims, ((), ())), preferred_element_type=f32)


NN = ((1,), (0,))
TN = ((0,), (0,))
NT = ((1,), (1,))


def heads_of(ref):
    pair = ref[...].astype(f32)
    return pair[:HD].astype(bf16), pair[HD:].astype(bf16)


def attend_kernel(blocks, *refs):
    q_ref = refs[0]
    k_refs = refs[1 : 1 + blocks]
    v_refs = refs[1 + blocks : 1 + 2 * blocks]
    o_ref, inv_ref = refs[1 + 2 * blocks :]
    q_heads = heads_of(q_ref)
    k_heads = [heads_of(r) for r in k_refs]
    v_heads = [heads_of(r) for r in v_refs]
    for i in range(2):
        total = None
        summed = None
        for k_pair, v_pair in zip(k_heads, v_heads):
            scores = dot(k_pair[i], q_heads[i], TN)
            probs = jnp.exp2(scores * SCALE_LOG2)
            part_sum = jnp.sum(probs, axis=0, keepdims=True)
            part = dot(v_pair[i], probs.astype(bf16), NN)
            total = part if total is None else total + part
            summed = part_sum if summed is None else summed + part_sum
        inverse = 1.0 / summed
        o_ref[i * HD : (i + 1) * HD, :] = total * inverse
        inv_ref[0, i : i + 1, :] = inverse


def attend(query, keys, values):
    blocks = len(keys)
    tokens = query.shape[1]
    per_key = keys[0].shape[1]
    spec_q = pl.BlockSpec((PAIR, tokens), lambda h: (h, 0))
    spec_k = pl.BlockSpec((PAIR, per_key), lambda h: (h, 0))
    return pl.pallas_call(
        functools.partial(attend_kernel, blocks),
        grid=(H // 2,),
        in_specs=[spec_q] + [spec_k] * (2 * blocks),
        out_specs=[spec_q, pl.BlockSpec((1, 2, tokens), lambda h: (h, 0, 0))],
        out_shape=[
            jax.ShapeDtypeStruct((H * HD, tokens), f32),
            jax.ShapeDtypeStruct((H // 2, 2, tokens), f32),
        ],
        compiler_params=pltpu.CompilerParams(vmem_limit_bytes=48 * 2**20),
        cost_estimate=pl.CostEstimate(
            flops=2 * 2 * H * 128 * tokens * per_key * blocks,
            bytes_accessed=2 * H * HD * (3 * tokens + 2 * per_key * blocks),
            transcendentals=H * tokens * per_key * blocks,
        ),
        name="attend",
    )(query, *keys, *values)


def attend_back_kernel(blocks, *refs):
    q_ref, g_ref, o_ref, inv_ref = refs[:4]
    k_refs = refs[4 : 4 + blocks]
    v_refs = refs[4 + blocks : 4 + 2 * blocks]
    dq_ref = refs[4 + 2 * blocks]
    dk_refs = refs[5 + 2 * blocks : 5 + 3 * blocks]
    dv_refs = refs[5 + 3 * blocks : 5 + 4 * blocks]
    q_heads = heads_of(q_ref)
    g_heads = heads_of(g_ref)
    gated = g_ref[...].astype(f32) * o_ref[...].astype(f32)
    k_heads = [heads_of(r) for r in k_refs]
    v_heads = [heads_of(r) for r in v_refs]
    for i in range(2):
        rows = slice(i * HD, (i + 1) * HD)
        row_dot = jnp.sum(gated[rows], axis=0, keepdims=True)
        inverse = inv_ref[0, i : i + 1, :]
        grad_q = None
        for b in range(blocks):
            k_one, v_one = k_heads[b][i], v_heads[b][i]
            scores = dot(k_one, q_heads[i], TN)
            exact = jnp.exp2(scores * SCALE_LOG2) * inverse
            grad_probs = dot(v_one, g_heads[i], TN)
            grad_scores = (exact * (grad_probs - row_dot)).astype(bf16)
            part = dot(k_one, grad_scores, NN)
            grad_q = part if grad_q is None else grad_q + part
            dk_refs[b][rows, :] = (dot(q_heads[i], grad_scores, NT) * SCALE).astype(
                dk_refs[b].dtype
            )
            dv_refs[b][rows, :] = dot(g_heads[i], exact.astype(bf16), NT).astype(dv_refs[b].dtype)
        dq_ref[rows, :] = grad_q * SCALE


def attend_back(query, grad, out, inverse, keys, values):
    blocks = len(keys)
    tokens = query.shape[1]
    per_key = keys[0].shape[1]
    spec_q = pl.BlockSpec((PAIR, tokens), lambda h: (h, 0))
    spec_k = pl.BlockSpec((PAIR, per_key), lambda h: (h, 0))
    shape_k = jax.ShapeDtypeStruct((H * HD, per_key), f32)
    outs = pl.pallas_call(
        functools.partial(attend_back_kernel, blocks),
        grid=(H // 2,),
        in_specs=[spec_q] * 3
        + [pl.BlockSpec((1, 2, tokens), lambda h: (h, 0, 0))]
        + [spec_k] * (2 * blocks),
        out_specs=[spec_q] + [spec_k] * (2 * blocks),
        out_shape=[jax.ShapeDtypeStruct((H * HD, tokens), f32)] + [shape_k] * (2 * blocks),
        compiler_params=pltpu.CompilerParams(vmem_limit_bytes=56 * 2**20),
        cost_estimate=pl.CostEstimate(
            flops=5 * 2 * H * 128 * tokens * per_key * blocks,
            bytes_accessed=2 * H * HD * (6 * tokens + 6 * per_key * blocks),
            transcendentals=H * tokens * per_key * blocks,
        ),
        name="attend_back",
    )(query, grad, out, inverse, *keys, *values)
    return outs[0], outs[1 : 1 + blocks], outs[1 + blocks :]


def assemble_kernel(heights, layout, *refs):
    count = len(layout)
    place_ref = refs[0]
    pieces = refs[1 : 1 + count]
    wholes = refs[1 + count : 1 + count + len(heights)]
    held = refs[1 + count + len(heights) : -2]
    sem_in, sem_out = refs[-2:]
    loads = [
        pltpu.make_async_copy(piece, room, sem_in.at[i])
        for i, (piece, room) in enumerate(zip(pieces, held))
    ]
    for load in loads:
        load.start()
    stores = []
    for load, room, (rank, low, high) in zip(loads, held, layout):
        load.wait()
        top = 0
        for height, whole in zip(heights, wholes):
            begin, end = max(low, top), min(high, top + height)
            if begin < end:
                row = pl.multiple_of(place_ref[rank] * height, 16) + (begin - top)
                store = pltpu.make_async_copy(
                    room.at[pl.ds(begin - low, end - begin)],
                    whole.at[pl.ds(row, end - begin)],
                    sem_out.at[len(stores)],
                )
                store.start()
                stores.append(store)
            top += height
    for store in stores:
        store.wait()


def assemble(pieces, layout, heights, places):
    width = pieces[0].shape[1]
    total = sum(heights)
    return pl.pallas_call(
        functools.partial(assemble_kernel, heights, layout),
        in_specs=[pl.BlockSpec(memory_space=pltpu.SMEM)]
        + [pl.BlockSpec(memory_space=pl.ANY)] * len(pieces),
        out_specs=[pl.BlockSpec(memory_space=pl.ANY)] * len(heights),
        out_shape=[jax.ShapeDtypeStruct((8 * height, width), bf16) for height in heights],
        scratch_shapes=[pltpu.VMEM(piece.shape, bf16) for piece in pieces]
        + [
            pltpu.SemaphoreType.DMA((len(pieces),)),
            pltpu.SemaphoreType.DMA((len(pieces) * len(heights),)),
        ],
        compiler_params=pltpu.CompilerParams(vmem_limit_bytes=24 * 2**20),
        cost_estimate=pl.CostEstimate(
            flops=0, bytes_accessed=2 * 2 * 8 * total * width, transcendentals=0
        ),
        name="assemble",
    )(places, *pieces)


def outer_kernel(place_ref, dy_ref, dy_other_ref, x_ref, x_other_ref, out_ref):
    out_ref[...] = (
        dot(dy_ref[...], x_ref[...], NT) + dot(dy_other_ref[...], x_other_ref[...], NT)
    ).astype(bf16)


def outer_blocks(places, dy_pair, x_pair, blocks):
    height = dy_pair[0].shape[0] // blocks
    tokens = dy_pair[0].shape[1]
    width = x_pair[0].shape[0]
    count = places.shape[0]
    spec_dy = pl.BlockSpec((height, tokens), lambda i, place: (place[i], 0))
    spec_x = pl.BlockSpec((width, tokens), lambda i, place: (0, 0))
    return pl.pallas_call(
        outer_kernel,
        grid_spec=pltpu.PrefetchScalarGridSpec(
            num_scalar_prefetch=1,
            grid=(count,),
            in_specs=[spec_dy, spec_dy, spec_x, spec_x],
            out_specs=pl.BlockSpec((height, width), lambda i, place: (i, 0)),
        ),
        out_shape=jax.ShapeDtypeStruct((count * height, width), bf16),
        compiler_params=pltpu.CompilerParams(vmem_limit_bytes=56 * 2**20),
        cost_estimate=pl.CostEstimate(
            flops=2 * 2 * count * height * width * tokens,
            bytes_accessed=2 * (2 * tokens * (count * height + width) + count * height * width),
            transcendentals=0,
        ),
        name="outer_blocks",
    )(places, *dy_pair, *x_pair)


def after(value, *others):
    return lax.optimization_barrier((value,) + others)[0]


SWAP = ((0, 1), (1, 0))


def swap(values, axis):
    return lax.ppermute(values, axis, SWAP)


def on_device(
    sizes,
    inputs,
    skipped,
    text_rows,
    condition,
    cotangent,
    norm_gains,
    skip_weight,
    shift_weight,
    query_key_weight,
    value_weight,
    self_output,
    cross_query,
    cross_memory,
    cross_output,
    up_weight,
    down_weight,
):
    outer, inner, cores, seq = sizes
    plane = outer * inner
    square = outer == 2 and inner == 2
    lat_count, local_rows, width = inputs.shape
    text_local = text_rows.shape[1]
    at_a = lax.axis_index("a")
    at_b = lax.axis_index("b")
    at_c = lax.axis_index("c")
    at_z = lax.axis_index("z")
    tokens = lat_count * local_rows

    def route(step):
        return [
            (
                core * seq + z,
                (z // lat_count) * seq + core * lat_count + (z % lat_count + step) % lat_count,
            )
            for core in range(cores)
            for z in range(seq)
        ]

    slot = at_z % lat_count

    def to_latent(values):
        parts = []
        for step in range(lat_count):
            chosen = lax.dynamic_index_in_dim(
                values, (slot + step) % lat_count, 0, keepdims=False
            )
            parts.append(lax.ppermute(chosen, ("c", "z"), route(step)))
        return jnp.concatenate(parts, axis=0)

    def from_latent(rows):
        height = rows.shape[0] // lat_count
        parts = []
        for step in range(lat_count):
            back = [(target, source) for source, target in route(step)]
            parts.append(
                lax.ppermute(rows[step * height : (step + 1) * height], ("c", "z"), back)
            )
        stacked = jnp.stack(parts + parts)
        return lax.dynamic_slice_in_dim(stacked, (lat_count - slot) % lat_count, lat_count, 0)

    places = jnp.stack(
        [
            ((at_a + da) % outer * inner + (at_b + db) % inner) * cores + (at_c + dc) % cores
            for dc in range(2)
            for da in range(2)
            for db in range(2)
        ]
    ).astype(jnp.int32)
    here = {"a": at_a, "b": at_b, "c": at_c}

    def z_shift(values, step):
        return lax.ppermute(values, "z", [(z, (z + step) % seq) for z in range(seq)])

    def z_blocks(values):
        arrived = [values] + [z_shift(values, step) for step in range(1, seq)]
        blocks = []
        for z in range(seq):
            block = arrived[0]
            for step in range(1, seq):
                block = jnp.where(at_z == (z + step) % seq, arrived[step], block)
            blocks.append(block)
        return blocks

    def flip(shards):
        return jnp.concatenate([shard.T for shard in shards], axis=0)

    def z_gather(flipped, direct):
        if direct:
            blocks = z_blocks(flipped)
        else:
            blocks = list(lax.all_gather(flipped, "z", axis=0, tiled=False))
        return jnp.concatenate(blocks, axis=1)

    def gather_rows(values, axes):
        if not square:
            return lax.all_gather(values, axes[::-1], axis=0, tiled=True)
        for axis in axes:
            other = swap(values, axis)
            lower = here[axis] == 0
            values = jnp.concatenate(
                [jnp.where(lower, values, other), jnp.where(lower, other, values)], axis=0
            )
        return values

    def total_of(values):
        if not square:
            return lax.psum(values, ("a", "b", "c", "z"))
        for axis in ("c", "b", "a"):
            values = values + swap(values, axis)
        stride = 1
        while stride < seq:
            values = values + lax.ppermute(values, "z", [(z, z ^ stride) for z in range(seq)])
            stride *= 2
        return values

    def gather(piece, heights):
        if not square:
            starts = [sum(heights[:i]) for i in range(len(heights))]
            return [
                lax.all_gather(piece[s : s + h], ("a", "b", "c"), axis=0, tiled=True)
                for s, h in zip(starts, heights)
            ], piece
        rows = piece.shape[0]
        half = rows // 32 * 16
        over_b = swap(piece, "b")
        over_a = swap(piece, "a")
        low = swap(over_b[:half], "a")
        high = swap(over_a[half:], "b")
        mine = (piece, over_b, over_a, low, high)
        spans = ((0, 0, rows), (1, 0, rows), (2, 0, rows), (3, 0, half), (3, half, rows))
        others = tuple(swap(part, "c") for part in mine)
        layout = spans + tuple((rank + 4, begin, end) for rank, begin, end in spans)
        return assemble(mine + others, layout, heights, places), (over_a, over_b)

    def blocks_of(dy_pair, x_pair):
        if square:
            return outer_blocks(places[:4][::-1], dy_pair, x_pair, plane * cores)
        kept = []
        for dy in dy_pair:
            cube = dy.reshape(plane, cores, -1, dy.shape[1])
            kept.append(
                lax.dynamic_index_in_dim(cube, at_c, 1, keepdims=False).reshape(-1, dy.shape[1])
            )
        return (dot(kept[0], x_pair[0], NT) + dot(kept[1], x_pair[1], NT)).astype(bf16)

    def scatter(grads, direct):
        if not square:
            cubes = [grad.reshape(plane, -1, grad.shape[1]) for grad in grads]
            summed = [
                lax.psum_scatter(cube, ("a", "b"), scatter_dimension=0, tiled=True)[0]
                for cube in cubes
            ]
            return z_scatter(summed, False)
        heights = [grad.shape[0] // 4 for grad in grads]

        def rank(i):
            return jnp.concatenate(
                [grad[i * h : (i + 1) * h] for grad, h in zip(grads, heights)], axis=0
            )

        far, over_a, over_b, own = rank(0), rank(1), rank(2), rank(3)
        rows = own.shape[0]
        half = rows // 32 * 16
        low = swap(far[:half], "b")
        high = swap(far[half:], "a")
        over_a = jnp.concatenate([over_a[:half] + low, over_a[half:]], axis=0)
        over_b = jnp.concatenate([over_b[:half], over_b[half:] + high], axis=0)
        got_a = swap(over_a, "a")
        got_b = swap(over_b, "b")
        total = (own.astype(f32) + got_a.astype(f32) + got_b.astype(f32)).astype(bf16)
        starts = [sum(heights[:i]) for i in range(len(heights))]
        return z_scatter([total[s : s + h] for s, h in zip(starts, heights)], direct)

    def z_scatter(outs, direct):
        heights = [out.shape[0] for out in outs]
        joined = jnp.concatenate(outs, axis=0)
        cut = joined.reshape(joined.shape[0], seq, -1).transpose(1, 0, 2)
        if direct:
            owned = lax.dynamic_index_in_dim(cut, at_z, 0, keepdims=False).astype(f32)
            for step in range(1, seq):
                block = lax.dynamic_index_in_dim(cut, (at_z + step) % seq, 0, keepdims=False)
                owned = owned + z_shift(block, step).astype(f32)
        else:
            owned = lax.psum_scatter(cut, "z", scatter_dimension=0, tiled=True)[0].astype(f32)
        results = []
        start = 0
        for height in heights:
            results.append(owned[start : start + height].T)
            start += height
        return results

    gain_skip = norm_gains[: 2 * width]
    gain_one = norm_gains[2 * width : 3 * width]
    gain_two = norm_gains[3 * width : 4 * width]
    gain_three = norm_gains[4 * width :]

    skip_piece = z_gather(flip([skip_weight]), True)
    pair_piece = z_gather(
        after(flip([query_key_weight, value_weight, shift_weight]), skip_piece), True
    )
    self_piece = z_gather(
        after(flip([self_output, cross_query, cross_output]), skip_piece), False
    )
    chip_in = to_latent(after(inputs, pair_piece))
    chip_skip = to_latent(after(skipped, pair_piece))
    memory_piece = z_gather(after(flip([cross_memory]), chip_skip), True)
    up_piece = z_gather(after(flip([up_weight]), pair_piece, self_piece), False)
    chip_text = to_latent(after(text_rows, memory_piece)).T
    down_piece = z_gather(after(flip([down_weight]), up_piece), False)
    chip_grad = to_latent(after(cotangent, chip_text)).T

    (skip_t,), ready = gather(skip_piece, [skip_weight.shape[1]])
    (pair_t, value_t, shift_t), ready = gather(
        after(pair_piece, *ready),
        [query_key_weight.shape[1], value_weight.shape[1], shift_weight.shape[1]],
    )
    (self_t, cq_t, cout_t), ready = gather(
        after(self_piece, *ready),
        [self_output.shape[1], cross_query.shape[1], cross_output.shape[1]],
    )
    (memory_t,), ready = gather(after(memory_piece, *ready), [cross_memory.shape[1]])
    (up_t,), ready = gather(after(up_piece, *ready), [up_weight.shape[1]])
    (down_t,), ready = gather(after(down_piece, *ready), [down_weight.shape[1]])

    quarter = HD // 4
    frequency = jnp.power(10000.0, -jnp.arange(quarter, dtype=f32) / quarter)
    position = jnp.concatenate(
        [
            (at_c * lat_count + (slot - step) % lat_count) * local_rows
            + jnp.arange(local_rows, dtype=jnp.int32)
            for step in range(lat_count)
        ]
    )
    row_angle = (position // GRID).astype(f32)[None, :] * frequency[:, None]
    col_angle = (position % GRID).astype(f32)[None, :] * frequency[:, None]
    tables = (jnp.cos(row_angle), jnp.sin(row_angle), jnp.cos(col_angle), jnp.sin(col_angle))

    def prepare(flat):
        cube = flat.reshape(H, HD, flat.shape[-1])
        return rotate(normalize(cube, 1), tables).reshape(flat.shape)

    cond_pair = (condition, swap(condition, "c"))
    same_core = at_z // lat_count == at_c
    cond_two = jnp.where(same_core, cond_pair[0], cond_pair[1])
    chip_cond = lax.dynamic_index_in_dim(cond_two, slot, 0, keepdims=False)
    shift = dot(shift_t, jax.nn.silu(chip_cond.astype(f32)).astype(bf16)[:, None], NN)[:, 0]

    joined = jnp.concatenate([chip_in.T, chip_skip.T], axis=0).astype(f32)
    level_zero = norm_gain(joined, gain_skip).astype(bf16)
    stream_zero = dot(skip_t, level_zero)
    level_one = shifted_norm(stream_zero, gain_one, shift).astype(bf16)
    pair_proj = dot(pair_t, level_one)
    value_proj = dot(value_t, level_one).astype(bf16)
    query_flat = pair_proj[:width]
    key_flat = pair_proj[width:]
    query = prepare(query_flat).astype(bf16)
    key = prepare(key_flat).astype(bf16)
    keys = [key, swap(key, "c")]
    values = [value_proj, swap(value_proj, "c")]
    attended, self_inverse = attend(query, keys, values)
    attended = attended.astype(bf16)
    stream_one = stream_zero + dot(self_t, attended)
    level_two = norm_gain(stream_one, gain_two).astype(bf16)
    cross_proj = dot(cq_t, level_two)
    cross = head_norm(cross_proj).astype(bf16)
    memory_proj = dot(memory_t, chip_text)
    memory_key_flat = memory_proj[:width]
    memory_key = head_norm(memory_key_flat).astype(bf16)
    memory_value = memory_proj[width:].astype(bf16)
    text_keys = [memory_key, swap(memory_key, "c")]
    text_values = [memory_value, swap(memory_value, "c")]
    crossed, cross_inverse = attend(cross, text_keys, text_values)
    crossed = crossed.astype(bf16)
    stream_two = stream_one + dot(cout_t, crossed)
    level_three = norm_gain(stream_two, gain_three).astype(bf16)
    hidden = dot(up_t, level_three)
    activated = gelu_tanh(hidden).astype(bf16)
    blended = (stream_two + dot(down_t, activated)).astype(bf16)
    blended_out = from_latent(blended.T)

    def with_other(values):
        return values, swap(values, "c")

    zero_pair = with_other(level_zero)
    one_pair = with_other(level_one)
    attended_pair = with_other(attended)
    two_pair = with_other(level_two)
    text_pair = with_other(chip_text)
    crossed_pair = with_other(crossed)
    three_pair = with_other(level_three)
    activated_pair = with_other(activated)

    down_blocks = blocks_of(with_other(chip_grad), activated_pair)
    (grad_down,) = scatter([down_blocks], False)
    grad_act = dot(down_t, chip_grad, TN)
    _, gelu_pull = jax.vjp(gelu_tanh, hidden)
    grad_hidden = gelu_pull(grad_act)[0].astype(bf16)
    up_blocks = blocks_of(with_other(grad_hidden), three_pair)
    (grad_up,) = scatter([up_blocks], False)
    grad_level_three = dot(up_t, after(grad_hidden, down_blocks), TN)
    _, pull_three = jax.vjp(norm_gain, stream_two, gain_three)
    grad_from_three, grad_gain_three = pull_three(grad_level_three)
    grad_stream_two = chip_grad.astype(f32) + grad_from_three
    cross_back = grad_stream_two.astype(bf16)
    grad_crossed = dot(cout_t, after(cross_back, up_blocks), TN).astype(bf16)
    grad_cross, grad_tk, grad_tv = attend_back(
        cross, grad_crossed, crossed, cross_inverse, text_keys, text_values
    )
    grad_memory_key = grad_tk[0] + swap(grad_tk[1].astype(bf16), "c").astype(f32)
    grad_memory_value = grad_tv[0] + swap(grad_tv[1].astype(bf16), "c").astype(f32)
    _, pull_memory = jax.vjp(head_norm, memory_key_flat)
    grad_memory_proj = jnp.concatenate(
        [pull_memory(grad_memory_key)[0], grad_memory_value], axis=0
    ).astype(bf16)
    grad_text_rows = dot(grad_memory_proj, memory_t, TN).astype(bf16)
    grad_text = from_latent(grad_text_rows).astype(f32)
    _, pull_cq = jax.vjp(head_norm, cross_proj)
    grad_cq_flat = pull_cq(grad_cross)[0].astype(bf16)
    grad_level_two = dot(cq_t, grad_cq_flat, TN)
    _, pull_two = jax.vjp(norm_gain, stream_one, gain_two)
    grad_from_two, grad_gain_two = pull_two(grad_level_two)
    grad_stream_one = grad_stream_two + grad_from_two
    self_back = grad_stream_one.astype(bf16)
    grad_attended = dot(self_t, self_back, TN).astype(bf16)
    grad_q, grad_k, grad_v = attend_back(
        query, grad_attended, attended, self_inverse, keys, values
    )
    grad_key = grad_k[0] + swap(grad_k[1].astype(bf16), "c").astype(f32)
    grad_value_proj = (grad_v[0] + swap(grad_v[1].astype(bf16), "c").astype(f32)).astype(bf16)
    _, pull_query = jax.vjp(prepare, query_flat)
    _, pull_key = jax.vjp(prepare, key_flat)
    grad_pair_proj = jnp.concatenate([pull_query(grad_q)[0], pull_key(grad_key)[0]], axis=0).astype(
        bf16
    )
    grad_level_one = dot(pair_t, grad_pair_proj, TN) + dot(value_t, grad_value_proj, TN)
    _, pull_one = jax.vjp(shifted_norm, stream_zero, gain_one, shift)
    grad_from_one, grad_gain_one, grad_shift_part = pull_one(grad_level_one)
    skip_back = (grad_stream_one + grad_from_one).astype(bf16)

    (grad_memory,) = scatter([blocks_of(with_other(grad_memory_proj), text_pair)], True)
    grad_cout, grad_cq, grad_self = scatter(
        [
            blocks_of(with_other(cross_back), crossed_pair),
            blocks_of(with_other(grad_cq_flat), two_pair),
            blocks_of(with_other(self_back), attended_pair),
        ],
        False,
    )
    grad_pair, grad_value = scatter(
        [
            blocks_of(with_other(grad_pair_proj), one_pair),
            blocks_of(with_other(grad_value_proj), one_pair),
        ],
        False,
    )
    (grad_skip_w,) = scatter([blocks_of(with_other(skip_back), zero_pair)], True)

    cond_act = jax.nn.silu(gather_rows(condition, ("c", "b", "a")).astype(f32)).astype(bf16)
    block_in, block_out = shift_weight.shape
    cond_block = lax.dynamic_slice_in_dim(cond_act, at_z * block_in, block_in, 1).astype(f32)
    shift_latent = grad_shift_part + swap(grad_shift_part, "c")
    shift_column = jnp.concatenate(z_blocks(shift_latent[None, :]), axis=0)
    shift_grads = gather_rows(shift_column, ("b", "a"))
    own_columns = ((at_a * inner + at_b) * cores + at_c) * block_out
    grad_shift = jnp.dot(
        cond_block.T,
        lax.dynamic_slice_in_dim(shift_grads, own_columns, block_out, 1),
        precision=lax.Precision.HIGHEST,
    )

    skip_back_rows = from_latent(skip_back.T).reshape(tokens, width)
    grad_level_zero = dot(skip_back_rows, skip_t, NN)
    joined_rows = jnp.concatenate([inputs, skipped], axis=-1).astype(f32).reshape(tokens, -1)
    _, pull_zero = jax.vjp(norm_gain_rows, joined_rows, gain_skip)
    grad_joined, grad_gain_skip = pull_zero(grad_level_zero)
    grad_input = grad_joined[:, :width].reshape(inputs.shape)
    grad_skipped = grad_joined[:, width:].reshape(inputs.shape)
    grad_gains = total_of(
        jnp.concatenate([grad_gain_skip, grad_gain_one, grad_gain_two, grad_gain_three])
    )
    return (
        blended_out,
        grad_input,
        grad_skipped,
        grad_text,
        grad_gains,
        grad_skip_w,
        grad_shift,
        grad_pair,
        grad_value,
        grad_self,
        grad_cq,
        grad_memory,
        grad_cout,
        grad_up,
        grad_down,
    )


def solution(mesh):
    dp, seq = mesh.shape["dp"], mesh.shape["seq"]
    inner, cores = 2, 2
    sizes = (dp // (inner * cores), inner, cores, seq)
    split = Mesh(mesh.devices.reshape(sizes), ("a", "b", "c", "z"))
    rows = P(("a", "b", "c"), "z", None)
    blocks = P("z", ("a", "b", "c"))
    return jax.shard_map(
        functools.partial(on_device, sizes),
        mesh=split,
        in_specs=(rows, rows, rows, P(("a", "b", "c"), None), rows, P()) + (blocks,) * 10,
        out_specs=(rows, rows, rows, rows, P()) + (blocks,) * 10,
        check_vma=False,
    )
```

```python
import functools
import math

import jax
import jax.numpy as jnp
from jax import lax
from jax.experimental import pallas as pl
from jax.experimental.pallas import tpu as pltpu
from jax.sharding import Mesh
from jax.sharding import PartitionSpec as P

H = 16
HD = 88
GRID = 32
PAIR = 2 * HD

epsilon = 1e-06
SCALE = HD ** (-0.5)
SCALE_LOG2 = SCALE * math.log2(math.e)

f32 = jnp.float32
bf16 = jnp.bfloat16


def normalize(values, axis):
    center = values - jnp.mean(values, axis=axis, keepdims=True)
    spread = jnp.mean(center * center, axis=axis, keepdims=True)
    return center * lax.rsqrt(spread + epsilon)


def norm_gain(values, gain_vec):
    return normalize(values, 0) * gain_vec[:, None]


def shifted_norm(values, gain_vec, offset):
    return normalize(values, 0) * gain_vec[:, None] + offset[:, None]


def norm_gain_rows(values, gain_vec):
    return normalize(values, -1) * gain_vec


def gelu_tanh(values):
    return jax.nn.gelu(values, approximate=True)


def head_norm(flat):
    return normalize(flat.reshape(H, HD, flat.shape[-1]), 1).reshape(flat.shape)


def rotate(per_head, tables):
    row_cos, row_sin, col_cos, col_sin = tables
    quarter = per_head.shape[1] // 4
    part_one = per_head[:, :quarter]
    part_two = per_head[:, quarter : 2 * quarter]
    part_three = per_head[:, 2 * quarter : 3 * quarter]
    part_four = per_head[:, 3 * quarter :]
    return jnp.concatenate(
        [
            part_one * row_cos - part_two * row_sin,
            part_two * row_cos + part_one * row_sin,
            part_three * col_cos - part_four * col_sin,
            part_four * col_cos + part_three * col_sin,
        ],
        axis=1,
    )


def dot(a, b, dims=((1,), (0,))):
    return lax.dot_general(a, b, (dims, ((), ())), preferred_element_type=f32)


NN = ((1,), (0,))
TN = ((0,), (0,))
NT = ((1,), (1,))


def heads_of(ref):
    pair = ref[...].astype(f32)
    return pair[:HD].astype(bf16), pair[HD:].astype(bf16)


def attend_kernel(blocks, *refs):
    q_ref = refs[0]
    k_refs = refs[1 : 1 + blocks]
    v_refs = refs[1 + blocks : 1 + 2 * blocks]
    o_ref, inv_ref = refs[1 + 2 * blocks :]
    q_heads = heads_of(q_ref)
    k_heads = [heads_of(r) for r in k_refs]
    v_heads = [heads_of(r) for r in v_refs]
    outs = []
    for i in range(2):
        total = None
        summed = None
        for k_pair, v_pair in zip(k_heads, v_heads):
            scores = dot(k_pair[i], q_heads[i], TN)
            probs = jnp.exp2(scores * SCALE_LOG2)
            part_sum = jnp.sum(probs, axis=0, keepdims=True)
            part = dot(v_pair[i], probs.astype(bf16), NN)
            total = part if total is None else total + part
            summed = part_sum if summed is None else summed + part_sum
        inverse = 1.0 / summed
        outs.append(total * inverse)
        inv_ref[0, i : i + 1, :] = inverse
    o_ref[...] = jnp.concatenate(outs, axis=0).astype(bf16)


def attend(query, keys, values):
    blocks = len(keys)
    tokens = query.shape[1]
    per_key = keys[0].shape[1]
    spec_q = pl.BlockSpec((PAIR, tokens), lambda h: (h, 0))
    spec_k = pl.BlockSpec((PAIR, per_key), lambda h: (h, 0))
    return pl.pallas_call(
        functools.partial(attend_kernel, blocks),
        grid=(H // 2,),
        in_specs=[spec_q] + [spec_k] * (2 * blocks),
        out_specs=[spec_q, pl.BlockSpec((1, 2, tokens), lambda h: (h, 0, 0))],
        out_shape=[
            jax.ShapeDtypeStruct((H * HD, tokens), bf16),
            jax.ShapeDtypeStruct((H // 2, 2, tokens), f32),
        ],
        compiler_params=pltpu.CompilerParams(vmem_limit_bytes=48 * 2**20),
        cost_estimate=pl.CostEstimate(
            flops=2 * 2 * H * 128 * tokens * per_key * blocks,
            bytes_accessed=2 * H * HD * (3 * tokens + 2 * per_key * blocks),
            transcendentals=H * tokens * per_key * blocks,
        ),
        name="attend",
    )(query, *keys, *values)


def attend_back_kernel(blocks, *refs):
    q_ref, g_ref, o_ref, inv_ref = refs[:4]
    k_refs = refs[4 : 4 + blocks]
    v_refs = refs[4 + blocks : 4 + 2 * blocks]
    dq_ref = refs[4 + 2 * blocks]
    dk_refs = refs[5 + 2 * blocks : 5 + 3 * blocks]
    dv_refs = refs[5 + 3 * blocks : 5 + 4 * blocks]
    q_heads = heads_of(q_ref)
    g_heads = heads_of(g_ref)
    gated = g_ref[...].astype(f32) * o_ref[...].astype(f32)
    k_heads = [heads_of(r) for r in k_refs]
    v_heads = [heads_of(r) for r in v_refs]
    grad_queries = []
    grad_keys = [[] for _ in range(blocks)]
    grad_values = [[] for _ in range(blocks)]
    for i in range(2):
        row_dot = jnp.sum(gated[i * HD : (i + 1) * HD], axis=0, keepdims=True)
        inverse = inv_ref[0, i : i + 1, :]
        grad_q = None
        for b in range(blocks):
            k_one, v_one = k_heads[b][i], v_heads[b][i]
            scores = dot(k_one, q_heads[i], TN)
            exact = jnp.exp2(scores * SCALE_LOG2) * inverse
            grad_probs = dot(v_one, g_heads[i], TN)
            grad_scores = (exact * (grad_probs - row_dot)).astype(bf16)
            part = dot(k_one, grad_scores, NN)
            grad_q = part if grad_q is None else grad_q + part
            grad_keys[b].append(dot(q_heads[i], grad_scores, NT) * SCALE)
            grad_values[b].append(dot(g_heads[i], exact.astype(bf16), NT))
        grad_queries.append(grad_q * SCALE)
    dq_ref[...] = jnp.concatenate(grad_queries, axis=0)
    for b in range(blocks):
        dk_refs[b][...] = jnp.concatenate(grad_keys[b], axis=0).astype(dk_refs[b].dtype)
        dv_refs[b][...] = jnp.concatenate(grad_values[b], axis=0).astype(dv_refs[b].dtype)


def attend_back(query, grad, out, inverse, keys, values):
    blocks = len(keys)
    tokens = query.shape[1]
    per_key = keys[0].shape[1]
    spec_q = pl.BlockSpec((PAIR, tokens), lambda h: (h, 0))
    spec_k = pl.BlockSpec((PAIR, per_key), lambda h: (h, 0))
    shapes_k = [jax.ShapeDtypeStruct((H * HD, per_key), kind) for kind in (f32, bf16)]
    outs = pl.pallas_call(
        functools.partial(attend_back_kernel, blocks),
        grid=(H // 2,),
        in_specs=[spec_q] * 3
        + [pl.BlockSpec((1, 2, tokens), lambda h: (h, 0, 0))]
        + [spec_k] * (2 * blocks),
        out_specs=[spec_q] + [spec_k] * (2 * blocks),
        out_shape=[jax.ShapeDtypeStruct((H * HD, tokens), f32)] + shapes_k * 2,
        compiler_params=pltpu.CompilerParams(vmem_limit_bytes=56 * 2**20),
        cost_estimate=pl.CostEstimate(
            flops=5 * 2 * H * 128 * tokens * per_key * blocks,
            bytes_accessed=2 * H * HD * (6 * tokens + 6 * per_key * blocks),
            transcendentals=H * tokens * per_key * blocks,
        ),
        name="attend_back",
    )(query, grad, out, inverse, *keys, *values)
    return outs[0], outs[1 : 1 + blocks], outs[1 + blocks :]


def assemble_kernel(heights, layout, *refs):
    count = len(layout)
    place_ref = refs[0]
    pieces = refs[1 : 1 + count]
    wholes = refs[1 + count : 1 + count + len(heights)]
    held = refs[1 + count + len(heights) : -2]
    sem_in, sem_out = refs[-2:]
    loads = [
        pltpu.make_async_copy(piece, room, sem_in.at[i])
        for i, (piece, room) in enumerate(zip(pieces, held))
    ]
    for load in loads:
        load.start()
    stores = []
    for load, room, (rank, low, high) in zip(loads, held, layout):
        load.wait()
        top = 0
        for height, whole in zip(heights, wholes):
            begin, end = max(low, top), min(high, top + height)
            if begin < end:
                row = pl.multiple_of(place_ref[rank] * height, 16) + (begin - top)
                store = pltpu.make_async_copy(
                    room.at[pl.ds(begin - low, end - begin)],
                    whole.at[pl.ds(row, end - begin)],
                    sem_out.at[len(stores)],
                )
                store.start()
                stores.append(store)
            top += height
    for store in stores:
        store.wait()


def assemble(pieces, layout, heights, places):
    width = pieces[0].shape[1]
    total = sum(heights)
    return pl.pallas_call(
        functools.partial(assemble_kernel, heights, layout),
        in_specs=[pl.BlockSpec(memory_space=pltpu.SMEM)]
        + [pl.BlockSpec(memory_space=pl.ANY)] * len(pieces),
        out_specs=[pl.BlockSpec(memory_space=pl.ANY)] * len(heights),
        out_shape=[jax.ShapeDtypeStruct((8 * height, width), bf16) for height in heights],
        scratch_shapes=[pltpu.VMEM(piece.shape, bf16) for piece in pieces]
        + [
            pltpu.SemaphoreType.DMA((len(pieces),)),
            pltpu.SemaphoreType.DMA((len(pieces) * len(heights),)),
        ],
        compiler_params=pltpu.CompilerParams(vmem_limit_bytes=24 * 2**20),
        cost_estimate=pl.CostEstimate(
            flops=0, bytes_accessed=2 * 2 * 8 * total * width, transcendentals=0
        ),
        name="assemble",
    )(places, *pieces)


def outer_kernel(heights, sharing, half, place_ref, *refs):
    count = len(heights)
    outs = 5 if half else 1
    dy_refs = refs[: 2 * count]
    x_refs = refs[2 * count : -outs]
    if half:
        low_ref, high_ref, over_a_ref, over_b_ref, own_ref = refs[-outs:]

    def put(rank, top, block):
        if not half:
            refs[-1][rank, top : top + block.shape[0], :] = block
            return
        if rank < 3:
            (own_ref, over_b_ref, over_a_ref)[rank][top : top + block.shape[0], :] = block
            return
        end = top + block.shape[0]
        if top < half:
            low_ref[top : min(end, half), :] = block[: min(end, half) - top]
        if end > half:
            high_ref[max(top, half) - half : end - half, :] = block[max(top, half) - top :]

    top = 0
    for i, (height, x_index) in enumerate(zip(heights, sharing)):
        step = 4 if height <= 176 else 2 if height <= 352 else 1
        for start in range(0, 4, step):
            total = None
            for core in range(2):
                chosen = [
                    dy_refs[2 * i + core][
                        pl.ds(pl.multiple_of(place_ref[rank] * height, 16), height), :
                    ]
                    for rank in range(start, start + step)
                ]
                lhs = chosen[0] if step == 1 else jnp.concatenate(chosen, axis=0)
                part = dot(lhs, x_refs[2 * x_index + core][...], NT)
                total = part if total is None else total + part
            total = total.astype(bf16)
            for n in range(step):
                put(start + n, top, total[n * height : (n + 1) * height])
        top += height


def outer_blocks(places, groups, blocks, split):
    x_pairs = [x_pair for x_pair, _ in groups]
    dy_pairs = [dy for _, group in groups for dy in group]
    sharing = [i for i, (_, group) in enumerate(groups) for _ in group]
    heights = [dy[0].shape[0] // blocks for dy in dy_pairs]
    rows = sum(heights)
    half = rows // 32 * 16 if split else 0
    tokens = dy_pairs[0][0].shape[1]
    width = x_pairs[0][0].shape[0]
    cut = next(c for c in (1408, 1536, 512, 128) if width % c == 0)
    once = pl.Buffered(1)
    dy_specs = [
        pl.BlockSpec(dy.shape, lambda i, place: (0, 0), pipeline_mode=once)
        for pair in dy_pairs
        for dy in pair
    ]
    x_buffers = {"pipeline_mode": once} if cut == width else {}
    x_specs = [pl.BlockSpec((cut, tokens), lambda i, place: (i, 0), **x_buffers)] * (
        2 * len(x_pairs)
    )
    sizes = (half, rows - half, rows, rows, rows)
    if split:
        out_specs = [pl.BlockSpec((size, cut), lambda i, place: (0, i)) for size in sizes]
        out_shape = [jax.ShapeDtypeStruct((size, width), bf16) for size in sizes]
    else:
        out_specs = [pl.BlockSpec((4, rows, cut), lambda i, place: (0, 0, i))]
        out_shape = [jax.ShapeDtypeStruct((4, rows, width), bf16)]
    return pl.pallas_call(
        functools.partial(outer_kernel, heights, sharing, half),
        grid_spec=pltpu.PrefetchScalarGridSpec(
            num_scalar_prefetch=1,
            grid=(width // cut,),
            in_specs=dy_specs + x_specs,
            out_specs=out_specs,
        ),
        out_shape=out_shape,
        compiler_params=pltpu.CompilerParams(vmem_limit_bytes=56 * 2**20),
        cost_estimate=pl.CostEstimate(
            flops=2 * 2 * 4 * rows * width * tokens,
            bytes_accessed=2 * (2 * tokens * (8 * rows + width) + 4 * rows * width),
            transcendentals=0,
        ),
        name="outer_blocks",
    )(places, *[dy for pair in dy_pairs for dy in pair], *[x for pair in x_pairs for x in pair])


def cut_kernel(seq, z_ref, *refs):
    term_refs, out_refs, held = refs[: -seq - 1], refs[-seq - 1 : -1], refs[-1]
    at_z = z_ref[0]
    rows, width = term_refs[0].shape
    part = width // seq

    def chunk(i, _):
        at = pl.ds(pl.multiple_of(i * 16, 16), 16)
        total = term_refs[0][at, :]
        if len(term_refs) > 1:
            total = sum(ref[at, :].astype(f32) for ref in term_refs).astype(bf16)
        for j in range(seq):
            held[j, at, :] = total[:, j * part : (j + 1) * part]
        return 0

    lax.fori_loop(0, rows // 16, chunk, 0)
    for step in range(seq):
        out_refs[step][...] = held[lax.rem(at_z + step, seq)]


def cut_sum(at_z, seq, *terms):
    rows, width = terms[0].shape
    return pl.pallas_call(
        functools.partial(cut_kernel, seq),
        in_specs=[pl.BlockSpec(memory_space=pltpu.SMEM)]
        + [pl.BlockSpec(memory_space=pltpu.VMEM)] * len(terms),
        out_specs=[pl.BlockSpec(memory_space=pltpu.VMEM)] * seq,
        out_shape=[jax.ShapeDtypeStruct((rows, width // seq), bf16)] * seq,
        scratch_shapes=[pltpu.VMEM((seq, rows, width // seq), bf16)],
        compiler_params=pltpu.CompilerParams(vmem_limit_bytes=32 * 2**20),
        cost_estimate=pl.CostEstimate(
            flops=2 * rows * width, bytes_accessed=8 * rows * width, transcendentals=0
        ),
        name="cut_sum",
    )(at_z.reshape(1), *terms)


def join_kernel(seq, z_ref, *refs):
    part_refs, out_ref, held = refs[:seq], refs[seq], refs[seq + 1]
    at_z = z_ref[0]
    rows, width = out_ref.shape
    for step in range(seq):
        held[lax.rem(at_z + seq - step, seq)] = part_refs[step][...]

    def chunk(i, _):
        at = pl.ds(pl.multiple_of(i * 16, 16), 16)
        out_ref[at, :] = jnp.concatenate([held[j, at, :] for j in range(seq)], axis=1)
        return 0

    lax.fori_loop(0, rows // 16, chunk, 0)


def join_parts(at_z, parts):
    seq = len(parts)
    rows, part = parts[0].shape
    return pl.pallas_call(
        functools.partial(join_kernel, seq),
        in_specs=[pl.BlockSpec(memory_space=pltpu.SMEM)]
        + [pl.BlockSpec(memory_space=pltpu.VMEM)] * seq,
        out_specs=pl.BlockSpec(memory_space=pltpu.VMEM),
        out_shape=jax.ShapeDtypeStruct((rows, seq * part), bf16),
        scratch_shapes=[pltpu.VMEM((seq, rows, part), bf16)],
        compiler_params=pltpu.CompilerParams(vmem_limit_bytes=32 * 2**20),
        cost_estimate=pl.CostEstimate(
            flops=0, bytes_accessed=4 * seq * rows * part, transcendentals=0
        ),
        name="join_parts",
    )(at_z.reshape(1), *parts)


def join_gathered_kernel(gathered_ref, out_ref):
    seq = gathered_ref.shape[0]

    def chunk(i, _):
        at = pl.ds(pl.multiple_of(i * 16, 16), 16)
        out_ref[at, :] = jnp.concatenate([gathered_ref[j, at, :] for j in range(seq)], axis=1)
        return 0

    lax.fori_loop(0, out_ref.shape[0] // 16, chunk, 0)


def join_gathered(gathered):
    seq, rows, part = gathered.shape
    return pl.pallas_call(
        join_gathered_kernel,
        in_specs=[pl.BlockSpec(memory_space=pltpu.VMEM)],
        out_specs=pl.BlockSpec(memory_space=pltpu.VMEM),
        out_shape=jax.ShapeDtypeStruct((rows, seq * part), bf16),
        compiler_params=pltpu.CompilerParams(vmem_limit_bytes=32 * 2**20),
        cost_estimate=pl.CostEstimate(
            flops=0, bytes_accessed=4 * seq * rows * part, transcendentals=0
        ),
        name="join_gathered",
    )(gathered)


def stack_kernel(*refs):
    term_refs, out_ref = refs[:-1], refs[-1]
    seq, _, part = out_ref.shape

    def chunk(i, _):
        at = pl.ds(pl.multiple_of(i * 16, 16), 16)
        total = sum(ref[at, :].astype(f32) for ref in term_refs).astype(bf16)
        for j in range(seq):
            out_ref[j, at, :] = total[:, j * part : (j + 1) * part]
        return 0

    lax.fori_loop(0, out_ref.shape[1] // 16, chunk, 0)


def stack_sum(seq, *terms):
    rows, width = terms[0].shape
    return pl.pallas_call(
        stack_kernel,
        in_specs=[pl.BlockSpec(memory_space=pltpu.VMEM)] * len(terms),
        out_specs=pl.BlockSpec(memory_space=pltpu.VMEM),
        out_shape=jax.ShapeDtypeStruct((seq, rows, width // seq), bf16),
        compiler_params=pltpu.CompilerParams(vmem_limit_bytes=32 * 2**20),
        cost_estimate=pl.CostEstimate(
            flops=2 * rows * width, bytes_accessed=8 * rows * width, transcendentals=0
        ),
        name="stack_sum",
    )(*terms)


def gelu_slope(x):
    scale = math.sqrt(2.0 / math.pi)
    bend = 0.044715
    curve = jnp.tanh(scale * (x + bend * x * x * x))
    return 0.5 * (1.0 + curve) + 0.5 * x * (1.0 - curve * curve) * scale * (1.0 + 3.0 * bend * x * x)


def mlp_up_kernel(up_ref, u_ref, hidden_ref, act_ref):
    hidden = dot(up_ref[...], u_ref[0], NN)
    hidden_ref[0] = hidden
    act_ref[0] = gelu_tanh(hidden).astype(bf16)


def mlp_down_kernel(down_ref, act_ref, out_ref):
    out_ref[0] = dot(down_ref[...], act_ref[0], NN).astype(bf16)


def mlp_back_kernel(down_flip_ref, up_flip_ref, grad_ref, hidden_ref, dh_ref, du_ref):
    grad_act = dot(down_flip_ref[...], grad_ref[0], NN)
    grad_hidden = (grad_act * gelu_slope(hidden_ref[0])).astype(bf16)
    dh_ref[0] = grad_hidden
    du_ref[0] = dot(up_flip_ref[...], grad_hidden, NN).astype(bf16)


def mlp_outer_kernel(a_ref, b_ref, out_ref, total_ref):
    step = pl.program_id(0)

    @pl.when(step == 0)
    def _():
        total_ref[...] = jnp.zeros_like(total_ref)

    total_ref[...] += dot(a_ref[0], b_ref[0], NT)

    @pl.when(step == pl.num_programs(0) - 1)
    def _():
        out_ref[...] = total_ref[...].astype(bf16)


def by_device(shape):
    return pl.BlockSpec((1,) + shape, lambda i: (i, 0, 0))


def kept(shape):
    return pl.BlockSpec(shape, lambda i: (0, 0))


def mlp_call(kernel, name, held, streams, outs, whole=None):
    count, _, tokens = streams[0].shape
    params = pltpu.CompilerParams(vmem_limit_bytes=48 * 2**20)
    flops = 2 * count * tokens * sum(x.shape[0] * x.shape[1] for x in held)
    moved = sum(x.size * 2 for x in streams) + sum(count * r * tokens * 3 for r, _ in outs)
    if whole:
        flops = 2 * count * tokens * whole[0] * whole[1]
        out_specs, out_shape = kept(whole), jax.ShapeDtypeStruct(whole, bf16)
        scratch = [pltpu.VMEM(whole, f32)]
    else:
        out_specs = [by_device((rows, tokens)) for rows, _ in outs]
        out_shape = [jax.ShapeDtypeStruct((count, rows, tokens), kind) for rows, kind in outs]
        scratch = []
    return pl.pallas_call(
        kernel,
        grid=(count,),
        in_specs=[kept(x.shape) for x in held] + [by_device(x.shape[1:]) for x in streams],
        out_specs=out_specs,
        out_shape=out_shape,
        scratch_shapes=scratch,
        compiler_params=params,
        cost_estimate=pl.CostEstimate(flops=flops, bytes_accessed=moved, transcendentals=0),
        name=name,
    )(*held, *streams)


def after(value, *others):
    return lax.optimization_barrier((value,) + others)[0]


SWAP = ((0, 1), (1, 0))


def swap(values, axis):
    return lax.ppermute(values, axis, SWAP)


def on_device(
    sizes,
    inputs,
    skipped,
    text_rows,
    condition,
    cotangent,
    norm_gains,
    skip_weight,
    shift_weight,
    query_key_weight,
    value_weight,
    self_output,
    cross_query,
    cross_memory,
    cross_output,
    up_weight,
    down_weight,
):
    outer, inner, cores, seq = sizes
    plane = outer * inner
    square = outer == 2 and inner == 2
    lat_count, local_rows, width = inputs.shape
    text_local = text_rows.shape[1]
    at_a = lax.axis_index("a")
    at_b = lax.axis_index("b")
    at_c = lax.axis_index("c")
    at_z = lax.axis_index("z")
    tokens = lat_count * local_rows

    def route(step):
        return [
            (
                core * seq + z,
                (z // lat_count) * seq + core * lat_count + (z % lat_count + step) % lat_count,
            )
            for core in range(cores)
            for z in range(seq)
        ]

    slot = at_z % lat_count

    def to_latent(values):
        parts = []
        for step in range(lat_count):
            chosen = lax.dynamic_index_in_dim(
                values, (slot + step) % lat_count, 0, keepdims=False
            )
            parts.append(lax.ppermute(chosen, ("c", "z"), route(step)))
        return jnp.concatenate(parts, axis=0)

    def from_latent(rows, *others):
        height = rows.shape[0] // lat_count
        parts = []
        for step in range(lat_count):
            back = [(target, source) for source, target in route(step)]
            parts.append(
                lax.ppermute(rows[step * height : (step + 1) * height], ("c", "z"), back)
            )
        parts = [after(part, *others) for part in parts]
        stacked = jnp.stack(parts + parts)
        return lax.dynamic_slice_in_dim(stacked, (lat_count - slot) % lat_count, lat_count, 0)

    places = jnp.stack(
        [
            ((at_a + da) % outer * inner + (at_b + db) % inner) * cores + (at_c + dc) % cores
            for dc in range(2)
            for da in range(2)
            for db in range(2)
        ]
    ).astype(jnp.int32)
    here = {"a": at_a, "b": at_b, "c": at_c}

    def z_shift(values, step):
        return lax.ppermute(values, "z", [(z, (z + step) % seq) for z in range(seq)])

    def z_send(values):
        return [values] + [z_shift(values, step) for step in range(1, seq)]

    def z_order(arrived):
        blocks = []
        for z in range(seq):
            block = arrived[0]
            for step in range(1, seq):
                block = jnp.where(at_z == (z + step) % seq, arrived[step], block)
            blocks.append(block)
        return blocks

    def z_piece(arrived, *others):
        arrived = [after(part, *others) for part in arrived]
        if square:
            return join_parts(at_z, arrived)
        return jnp.concatenate(z_order(arrived), axis=1)

    def flip(shards):
        return jnp.concatenate([shard.T for shard in shards], axis=0)

    def gather_rows(values, axes):
        if not square:
            return lax.all_gather(values, axes[::-1], axis=0, tiled=True)
        for axis in axes:
            other = swap(values, axis)
            lower = here[axis] == 0
            values = jnp.concatenate(
                [jnp.where(lower, values, other), jnp.where(lower, other, values)], axis=0
            )
        return values

    def total_of(values):
        if not square:
            return lax.psum(values, ("a", "b", "c", "z"))
        held = jnp.zeros((8,) + values.shape, values.dtype)
        for rank in range(8):
            arrived = to_rank(values, rank) if rank else values
            held = lax.dynamic_update_slice(held, arrived[None], (places[rank], 0))
        values = sum(held[i] for i in range(8))
        values = sum(z_order(z_send(values)))
        return values

    def to_rank(values, rank):
        axes = tuple(axis for axis, bit in (("c", 4), ("a", 2), ("b", 1)) if rank & bit)
        axes = tuple(axis for axis in ("a", "b", "c") if axis in axes)
        last = 2 ** len(axes) - 1
        return lax.ppermute(values, axes, [(i, last - i) for i in range(last + 1)])

    def exchange(blocks):
        return [blocks[0]] + [to_rank(blocks[rank], rank) for rank in range(1, 8)]

    def stack_by_device(blocks):
        rows = blocks[0].shape[0]
        layout = tuple((rank, 0, rows) for rank in range(8))
        return assemble(tuple(blocks), layout, [rows], places)[0]

    def hop_one(piece):
        return swap(piece, "b"), swap(piece, "a")

    def halves(over_b, over_a):
        half = over_b.shape[0] // 32 * 16
        return over_b[:half], over_a[half:]

    def hop_two(low, high):
        return swap(low, "a"), swap(high, "b")

    def after_all(parts, *others):
        return tuple(lax.optimization_barrier(tuple(parts) + others)[: len(parts)])

    def to_core(parts):
        return tuple(swap(part, "c") for part in parts)

    def whole_of(mine, others, shards):
        rows = mine[0].shape[0]
        half = mine[3].shape[0]
        spans = ((0, 0, rows), (1, 0, rows), (2, 0, rows), (3, 0, half), (3, half, rows))
        layout = spans + tuple((rank + 4, begin, end) for rank, begin, end in spans)
        return assemble(mine + others, layout, [shard.shape[1] for shard in shards], places)

    def gather_plain(piece, shards):
        heights = [shard.shape[1] for shard in shards]
        starts = [sum(heights[:i]) for i in range(len(heights))]
        return [
            lax.all_gather(piece[s : s + h], ("a", "b", "c"), axis=0, tiled=True)
            for s, h in zip(starts, heights)
        ]

    in_order = jnp.arange(4, dtype=jnp.int32) * cores + at_c

    def outer_of(*groups, split=True):
        if square:
            return outer_blocks(
                places[:4] if split else in_order, groups, plane * cores, split
            )
        outs = []
        for x_pair, dy_pairs in groups:
            for dy_pair in dy_pairs:
                total = 0.0
                for dy, x in zip(dy_pair, x_pair):
                    cube = dy.reshape(plane, cores, -1, dy.shape[1])
                    mine = lax.dynamic_index_in_dim(cube, at_c, 1, keepdims=False)
                    total = total + dot(mine.reshape(-1, dy.shape[1]), x, NT)
                cube = total.astype(bf16).reshape(plane, -1, x_pair[0].shape[0])
                outs.append(
                    lax.psum_scatter(cube, ("a", "b"), scatter_dimension=0, tiled=True)[0]
                )
        return (jnp.concatenate(outs, axis=0),)

    def sum_far(state):
        low, high, over_a, over_b, own = state
        return swap(low, "b"), swap(high, "a"), over_a, over_b, own

    def sum_near(state, *others):
        low, high, over_a, over_b, own = state
        half = low.shape[0]
        low = after(low, *others)
        over_a = lax.dynamic_update_slice(over_a, over_a[:half] + low, (0, 0))
        over_b = lax.dynamic_update_slice(over_b, over_b[half:] + high, (half, 0))
        return own, swap(over_a, "a"), swap(over_b, "b"), (over_a, over_b)

    def sum_z(state, *others):
        own, got_a, got_b, _ = state
        parts = cut_sum(at_z, seq, own, after(got_a, *others), got_b)
        return [parts[0]] + [z_shift(parts[step], step) for step in range(1, seq)]

    def sum_z_one(total, *others):
        parts = cut_sum(at_z, seq, after(total, *others))
        return [parts[0]] + [z_shift(parts[step], step) for step in range(1, seq)]

    def sum_z_offloaded(state, *others):
        own, got_a, got_b, _ = state
        stacked = stack_sum(seq, own, after(got_a, *others), got_b)
        return [lax.psum_scatter(stacked, "z", scatter_dimension=0, tiled=True)[0]], stacked

    def sum_plain(state):
        (total,) = state
        cut = total.reshape(total.shape[0], seq, -1).transpose(1, 0, 2)
        return [
            z_shift(lax.dynamic_index_in_dim(cut, (at_z + step) % seq, 0, keepdims=False), step)
            for step in range(seq)
        ]

    def sum_end(parts, shards, *others):
        owned = sum(after(part, *others).astype(f32) for part in parts)
        results = []
        start = 0
        for shard in shards:
            results.append(owned[start : start + shard.shape[1]].T)
            start += shard.shape[1]
        return results

    gain_skip = norm_gains[: 2 * width]
    gain_one = norm_gains[2 * width : 3 * width]
    gain_two = norm_gains[3 * width : 4 * width]
    gain_three = norm_gains[4 * width :]

    both_in = jnp.concatenate([inputs, skipped], axis=-1)
    skip_set = [skip_weight]
    pair_set = [query_key_weight, value_weight, shift_weight]
    self_set = [self_output, cross_query, cross_output]
    memory_set = [cross_memory]
    up_set = [up_weight]
    down_set = [down_weight]
    skip_flip, pair_flip, self_flip, memory_flip, up_flip, down_flip = (
        flip(one) for one in (skip_set, pair_set, self_set, memory_set, up_set, down_set)
    )
    if square:
        skip_sent = z_send(skip_flip)
        self_flip = after(self_flip, pair_flip)
        up_flip = after(up_flip, self_flip)
        down_flip = after(down_flip, up_flip)
        grad_sent = to_latent(after(cotangent, down_flip))
        pair_sent = lax.all_gather(pair_flip, "z", axis=0, tiled=False)
        self_sent = lax.all_gather(self_flip, "z", axis=0, tiled=False)
        up_sent = lax.all_gather(up_flip, "z", axis=0, tiled=False)
        down_sent = lax.all_gather(down_flip, "z", axis=0, tiled=False)
        skip_piece = z_piece(skip_sent)
        skip_near = hop_one(skip_piece)
        skip_half = halves(*skip_near)
        skip_far = hop_two(*skip_half)
        pair_piece = join_gathered(after(pair_sent, *skip_half))
        pair_near = hop_one(pair_piece)
        memory_sent = z_send(after(memory_flip, pair_piece))
        skip_far = after_all(skip_far, pair_piece)
        skip_mine = (skip_piece,) + skip_near + skip_far
        skip_other = to_core(skip_mine)
        (skip_t,) = whole_of(skip_mine, skip_other, skip_set)
        joined = jnp.concatenate(
            [
                inputs.reshape(tokens, width).T,
                skipped.reshape(tokens, width).T,
            ],
            axis=0,
        ).astype(f32)
        start_zero = dot(skip_t, norm_gain(joined, gain_skip).astype(bf16)).astype(bf16)
        zero_sent = to_latent(start_zero.T.reshape(inputs.shape))
        pair_near = after_all(pair_near, start_zero)
        pair_half = halves(*pair_near)
        pair_far = hop_two(*pair_half)
        memory_piece = z_piece(memory_sent, *pair_half)
        self_piece = join_gathered(after(self_sent, memory_piece))
        pair_far = after_all(pair_far, self_piece)
        pair_mine = (pair_piece,) + pair_near + pair_far
        pair_other = to_core(pair_mine)
        self_near = hop_one(self_piece)
        memory_near = hop_one(memory_piece)
        stream_zero = after(zero_sent, *pair_far).T.astype(f32)
        pair_t, value_t, shift_t = whole_of(pair_mine, pair_other, pair_set)
    else:
        chip_both = to_latent(both_in)
        joined = chip_both.T.astype(f32)
        level_zero = norm_gain(joined, gain_skip).astype(bf16)
        chip_text = to_latent(text_rows).T
        chip_grad = to_latent(cotangent).T
        (skip_t,) = gather_plain(z_piece(z_send(skip_flip)), skip_set)
        pair_t, value_t, shift_t = gather_plain(z_piece(z_send(pair_flip)), pair_set)
        self_t, cq_t, cout_t = gather_plain(z_piece(z_send(self_flip)), self_set)
        (memory_t,) = gather_plain(z_piece(z_send(memory_flip)), memory_set)
        (up_t,) = gather_plain(z_piece(z_send(up_flip)), up_set)
        (down_t,) = gather_plain(z_piece(z_send(down_flip)), down_set)
        stream_zero = dot(skip_t, level_zero)

    quarter = HD // 4
    frequency = jnp.power(10000.0, -jnp.arange(quarter, dtype=f32) / quarter)
    position = jnp.concatenate(
        [
            (at_c * lat_count + (slot - step) % lat_count) * local_rows
            + jnp.arange(local_rows, dtype=jnp.int32)
            for step in range(lat_count)
        ]
    )
    row_angle = (position // GRID).astype(f32)[None, :] * frequency[:, None]
    col_angle = (position % GRID).astype(f32)[None, :] * frequency[:, None]
    tables = (jnp.cos(row_angle), jnp.sin(row_angle), jnp.cos(col_angle), jnp.sin(col_angle))

    def prepare(flat):
        cube = flat.reshape(H, HD, flat.shape[-1])
        return rotate(normalize(cube, 1), tables).reshape(flat.shape)

    cond_pair = (condition, swap(condition, "c"))
    same_core = at_z // lat_count == at_c
    cond_two = jnp.where(same_core, cond_pair[0], cond_pair[1])
    chip_cond = lax.dynamic_index_in_dim(cond_two, slot, 0, keepdims=False)
    shift = dot(shift_t, jax.nn.silu(chip_cond.astype(f32)).astype(bf16)[:, None], NN)[:, 0]

    level_one = shifted_norm(stream_zero, gain_one, shift).astype(bf16)
    pair_proj = dot(pair_t, level_one)
    value_proj = dot(value_t, level_one).astype(bf16)
    query_flat = pair_proj[:width]
    key_flat = pair_proj[width:]
    query = prepare(query_flat).astype(bf16)
    key = prepare(key_flat).astype(bf16)
    keys = [key, swap(key, "c")]
    values = [value_proj, swap(value_proj, "c")]
    query_next = query
    if square:
        self_near = after_all(self_near, query)
        self_half = halves(*self_near)
        self_far = hop_two(*self_half)
        memory_near = after_all(memory_near, *self_half)
        memory_half = halves(*memory_near)
        memory_far = hop_two(*memory_half)
        query_next = after(query, *memory_half)
    attended, self_inverse = attend(query_next, keys, values)
    attended_next = attended
    if square:
        all_plane = ("a", "b", "c")
        up_piece = join_gathered(after(up_sent, attended))
        down_piece = join_gathered(after(down_sent, attended))
        slice_rows = up_weight.shape[1]
        down_blocks = [
            lax.dynamic_slice_in_dim(down_piece, places[rank] * slice_rows, slice_rows, 1)
            for rank in range(8)
        ]
        chip_grad = after(grad_sent, attended).T
        grad_all = lax.all_gather(chip_grad, all_plane, axis=0, tiled=False)
        text_sent = to_latent(after(text_rows, query))
        down_sent = exchange(down_blocks)
        self_far = after_all(self_far, attended)
        self_mine = (self_piece,) + self_near + self_far
        self_other = to_core(self_mine)
        memory_far = after_all(memory_far, *self_far)
        memory_mine = (memory_piece,) + memory_near + memory_far
        memory_other = to_core(memory_mine)
        self_t, cq_t, cout_t = whole_of(self_mine, self_other, self_set)
        (memory_t,) = whole_of(memory_mine, memory_other, memory_set)
        chip_text = after(text_sent, *memory_far).T
    stream_one = stream_zero + dot(self_t, attended_next)
    level_two = norm_gain(stream_one, gain_two).astype(bf16)
    cross_proj = dot(cq_t, level_two)
    cross = head_norm(cross_proj).astype(bf16)
    memory_proj = dot(memory_t, chip_text)
    memory_key_flat = memory_proj[:width]
    memory_key = head_norm(memory_key_flat).astype(bf16)
    memory_value = memory_proj[width:].astype(bf16)
    text_keys = [memory_key, swap(memory_key, "c")]
    text_values = [memory_value, swap(memory_value, "c")]
    crossed, cross_inverse = attend(cross, text_keys, text_values)
    stream_two = stream_one + dot(cout_t, crossed)
    level_three = norm_gain(stream_two, gain_three).astype(bf16)
    if square:
        up_slice = up_piece
        three_all = lax.all_gather(
            after(level_three, grad_all), all_plane, axis=0, tiled=False
        )
        down_slice = stack_by_device([after(part, level_three) for part in down_sent])
        hidden, activated = mlp_call(
            mlp_up_kernel,
            "mlp_up",
            [up_slice],
            [three_all],
            [(slice_rows, f32), (slice_rows, bf16)],
        )
    else:
        hidden = dot(up_t, level_three)
        activated = gelu_tanh(hidden).astype(bf16)

    def with_other(values):
        return values, swap(values, "c")

    one_pair = with_other(level_one)
    attended_pair = with_other(attended)
    two_pair = with_other(level_two)
    text_pair = with_other(chip_text)
    crossed_pair = with_other(crossed)

    if square:
        grad_hidden, part = mlp_call(
            mlp_back_kernel,
            "mlp_back",
            [down_slice.T, up_slice.T],
            [grad_all, hidden],
            [(slice_rows, bf16), (width, bf16)],
        )
        grad_level_three = lax.psum_scatter(part, all_plane, scatter_dimension=0, tiled=True)[0]
        both_sent = to_latent(after(both_in, part))
        down_grad = mlp_call(
            mlp_outer_kernel,
            "mlp_outer",
            [],
            [after(grad_all, part), activated],
            [],
            (width, slice_rows),
        )
        down_parts = exchange(
            [
                lax.dynamic_slice_in_dim(
                    down_grad, places[rank] * (width // 8), width // 8, 0
                )
                for rank in range(8)
            ]
        )
        up_grad = mlp_call(
            mlp_outer_kernel,
            "mlp_outer",
            [],
            [after(grad_hidden, down_grad), three_all],
            [],
            (slice_rows, width),
        )
        up_sum = sum_z_one(up_grad)
        (out_part,) = mlp_call(
            mlp_down_kernel,
            "mlp_down",
            [down_slice],
            [after(activated, up_grad)],
            [(width, bf16)],
        )
        down_whole = stack_by_device([after(part, out_part) for part in down_parts])
        down_cube = down_whole.reshape(seq, -1, slice_rows)
        down_sum = [
            z_shift(
                lax.dynamic_index_in_dim(down_cube, (at_z + step) % seq, 0, keepdims=False), step
            )
            if step
            else lax.dynamic_index_in_dim(down_cube, at_z, 0, keepdims=False)
            for step in range(seq)
        ]
        level_zero = norm_gain(after(both_sent, out_part).T.astype(f32), gain_skip).astype(bf16)
        grad_level_three = after(grad_level_three, level_zero, down_cube).astype(f32)
    else:
        grad_act = dot(down_t, chip_grad, TN)
        _, gelu_pull = jax.vjp(gelu_tanh, hidden)
        grad_hidden = gelu_pull(grad_act)[0].astype(bf16)
        down_outer = outer_of((with_other(activated), [with_other(chip_grad)]))
        up_outer = outer_of((with_other(level_three), [with_other(grad_hidden)]))
        grad_level_three = dot(up_t, grad_hidden, TN)
    zero_pair = with_other(level_zero)
    _, pull_three = jax.vjp(norm_gain, stream_two, gain_three)
    grad_from_three, grad_gain_three = pull_three(grad_level_three)
    grad_stream_two = chip_grad.astype(f32) + grad_from_three
    cross_back = grad_stream_two.astype(bf16)
    grad_crossed = dot(cout_t, cross_back, TN).astype(bf16)
    grad_cross, grad_tk, grad_tv = attend_back(
        cross, grad_crossed, crossed, cross_inverse, text_keys, text_values
    )
    grad_memory_key = grad_tk[0] + swap(grad_tk[1], "c").astype(f32)
    grad_memory_value = grad_tv[0] + swap(grad_tv[1], "c").astype(f32)
    _, pull_memory = jax.vjp(head_norm, memory_key_flat)
    grad_memory_proj = jnp.concatenate(
        [pull_memory(grad_memory_key)[0], grad_memory_value], axis=0
    ).astype(bf16)
    _, pull_cq = jax.vjp(head_norm, cross_proj)
    grad_cq_flat = pull_cq(grad_cross)[0].astype(bf16)
    early = up_sum + down_sum if square else []
    grad_level_two = dot(cq_t, grad_cq_flat, TN)
    _, pull_two = jax.vjp(norm_gain, stream_one, gain_two)
    grad_from_two, grad_gain_two = pull_two(grad_level_two)
    grad_stream_one = grad_stream_two + grad_from_two
    self_back = grad_stream_one.astype(bf16)
    cross_outer = outer_of(
        (crossed_pair, [with_other(cross_back)]),
        (two_pair, [with_other(grad_cq_flat)]),
        (attended_pair, [with_other(self_back)]),
    )
    memory_outer = outer_of((text_pair, [with_other(grad_memory_proj)]))
    if square:
        cross_sum = sum_far(cross_outer)
        memory_sum = sum_far(memory_outer)
    grad_attended = dot(
        self_t, after(self_back, cross_outer[0], memory_outer[0]), TN
    ).astype(bf16)
    grad_q, grad_k, grad_v = attend_back(
        query, grad_attended, attended, self_inverse, keys, values
    )
    if square:
        cross_sum = sum_near(cross_sum, grad_q)
        memory_sum = sum_near(memory_sum, grad_q)
        out_sum = lax.psum_scatter(
            after(out_part, grad_level_three), all_plane, scatter_dimension=0, tiled=True
        )[0]
        blended = (stream_two + after(out_sum, grad_q).astype(f32)).astype(bf16)
        grad_q = after(grad_q, blended, *early, *cross_sum[3], *memory_sum[3])
    grad_key = grad_k[0] + swap(grad_k[1], "c").astype(f32)
    grad_value_proj = (grad_v[0] + swap(grad_v[1], "c").astype(f32)).astype(bf16)
    _, pull_query = jax.vjp(prepare, query_flat)
    _, pull_key = jax.vjp(prepare, key_flat)
    grad_pair_proj = jnp.concatenate([pull_query(grad_q)[0], pull_key(grad_key)[0]], axis=0).astype(
        bf16
    )
    first_outer = outer_of(
        (one_pair, [with_other(grad_value_proj), with_other(grad_pair_proj)]),
    )
    if square:
        first_sum = sum_far(first_outer)
        cross_sum, stacked = sum_z_offloaded(cross_sum, first_outer[0])
        memory_sum = sum_z(memory_sum, first_outer[0])
    else:
        stacked = first_outer[0]
        blended = (stream_two + dot(down_t, activated)).astype(bf16)
    blended_out = from_latent(blended.T, first_outer[0])
    grad_text_rows = dot(grad_memory_proj, memory_t, TN).astype(bf16)
    grad_text = from_latent(grad_text_rows, first_outer[0]).astype(f32)
    grad_pair_next = after(grad_pair_proj, first_outer[0], stacked, blended_out, grad_text)
    grad_level_one = dot(pair_t, grad_pair_next, TN) + dot(value_t, grad_value_proj, TN)
    _, pull_one = jax.vjp(shifted_norm, stream_zero, gain_one, shift)
    grad_from_one, grad_gain_one, grad_shift_part = pull_one(grad_level_one)
    skip_back = (grad_stream_one + grad_from_one).astype(bf16)
    skip_outer = outer_of((zero_pair, [with_other(skip_back)]))
    late = skip_outer[0]
    if square:
        skip_sum = sum_far(skip_outer)
        first_sum = sum_near(first_sum, skip_outer[0])
        late = first_sum[3][0]
    skip_rows = from_latent(skip_back.T, late)
    skip_back_rows = skip_rows.reshape(tokens, width)
    grad_level_zero = dot(skip_back_rows, skip_t, NN)
    if square:
        skip_sum = sum_near(skip_sum, grad_level_zero)
        first_sum = sum_z(first_sum, *skip_sum[3])
        stacked = first_sum[0]
        grad_level_zero = after(grad_level_zero, stacked)
        (grad_up,) = sum_end(up_sum, up_set, stacked)
        down_total = sum(after(part, stacked).astype(f32) for part in down_sum)
        grad_down = (
            down_total.reshape(cores, -1, slice_rows)
            .transpose(0, 2, 1)
            .reshape(cores * slice_rows, -1)
        )
        skip_sum = sum_z(skip_sum, grad_level_zero)
        late = skip_sum[0]
        grad_cout, grad_cq, grad_self = sum_end(
            cross_sum, [cross_output, cross_query, self_output], late
        )
        (grad_memory,) = sum_end(memory_sum, memory_set, late)
        (grad_skip_w,) = sum_end(skip_sum, skip_set, grad_memory)
        grad_value, grad_pair = sum_end(
            first_sum, [value_weight, query_key_weight], grad_skip_w
        )
    else:
        (grad_down,) = sum_end(sum_plain(down_outer), down_set)
        (grad_up,) = sum_end(sum_plain(up_outer), up_set)
        grad_cout, grad_cq, grad_self = sum_end(
            sum_plain(cross_outer), [cross_output, cross_query, self_output]
        )
        (grad_memory,) = sum_end(sum_plain(memory_outer), memory_set)
        grad_value, grad_pair = sum_end(sum_plain(first_outer), [value_weight, query_key_weight])
        (grad_skip_w,) = sum_end(sum_plain(skip_outer), skip_set)

    cond_act = jax.nn.silu(gather_rows(condition, ("c", "b", "a")).astype(f32)).astype(bf16)
    block_in, block_out = shift_weight.shape
    cond_block = lax.dynamic_slice_in_dim(cond_act, at_z * block_in, block_in, 1).astype(f32)
    small = jnp.stack([grad_shift_part, grad_gain_one, grad_gain_two, grad_gain_three])
    small = after(small, late)
    if square:
        small = small + swap(small, "c")
        columns = z_order(z_send(small))
        shift_grads = jnp.concatenate([column[:1] for column in columns], axis=0)
        gain_part = sum(column[1:] for column in columns)
        for axis in ("b", "a"):
            carried = jnp.concatenate([gain_part, shift_grads], axis=0)
            other = swap(carried, axis)
            gain_part = gain_part + other[:3]
            lower = here[axis] == 0
            shift_grads = jnp.concatenate(
                [
                    jnp.where(lower, shift_grads, other[3:]),
                    jnp.where(lower, other[3:], shift_grads),
                ],
                axis=0,
            )
    else:
        gain_part = lax.psum(small[1:], ("a", "b", "c", "z"))
        shift_grads = lax.all_gather(lax.psum(small[:1], "c"), ("a", "b", "z"), axis=0, tiled=True)
    own_columns = ((at_a * inner + at_b) * cores + at_c) * block_out
    grad_shift = jnp.dot(
        cond_block.T,
        lax.dynamic_slice_in_dim(shift_grads, own_columns, block_out, 1),
        precision=lax.Precision.HIGHEST,
    )

    joined_rows = jnp.concatenate([inputs, skipped], axis=-1).astype(f32).reshape(tokens, -1)
    _, pull_zero = jax.vjp(norm_gain_rows, joined_rows, gain_skip)
    grad_joined, grad_gain_skip = pull_zero(grad_level_zero)
    grad_input = grad_joined[:, :width].reshape(inputs.shape)
    grad_skipped = grad_joined[:, width:].reshape(inputs.shape)
    grad_gains = jnp.concatenate([total_of(grad_gain_skip), gain_part.reshape(-1)])
    return (
        blended_out,
        grad_input,
        grad_skipped,
        grad_text,
        grad_gains,
        grad_skip_w,
        grad_shift,
        grad_pair,
        grad_value,
        grad_self,
        grad_cq,
        grad_memory,
        grad_cout,
        grad_up,
        grad_down,
    )


def solution(mesh):
    dp, seq = mesh.shape["dp"], mesh.shape["seq"]
    inner, cores = 2, 2
    sizes = (dp // (inner * cores), inner, cores, seq)
    split = Mesh(mesh.devices.reshape(sizes), ("a", "b", "c", "z"))
    rows = P(("a", "b", "c"), "z", None)
    blocks = P("z", ("a", "b", "c"))
    return jax.shard_map(
        functools.partial(on_device, sizes),
        mesh=split,
        in_specs=(rows, rows, rows, P(("a", "b", "c"), None), rows, P()) + (blocks,) * 10,
        out_specs=(rows, rows, rows, rows, P()) + (blocks,) * 10,
        check_vma=False,
    )
```

```python
import functools
import math

import jax
import jax.numpy as jnp
from jax import lax
from jax.experimental import pallas as pl
from jax.experimental.pallas import tpu as pltpu
from jax.sharding import Mesh
from jax.sharding import PartitionSpec as P

H = 16
HD = 88
GRID = 32
PAIR = 2 * HD

epsilon = 1e-06
SCALE = HD ** (-0.5)
SCALE_LOG2 = SCALE * math.log2(math.e)

f32 = jnp.float32
bf16 = jnp.bfloat16


def normalize(values, axis):
    center = values - jnp.mean(values, axis=axis, keepdims=True)
    spread = jnp.mean(center * center, axis=axis, keepdims=True)
    return center * lax.rsqrt(spread + epsilon)


def norm_gain(values, gain_vec):
    return normalize(values, 0) * gain_vec[:, None]


def shifted_norm(values, gain_vec, offset):
    return normalize(values, 0) * gain_vec[:, None] + offset[:, None]


def norm_gain_rows(values, gain_vec):
    return normalize(values, -1) * gain_vec


def gelu_tanh(values):
    return jax.nn.gelu(values, approximate=True)


def head_norm(flat):
    return normalize(flat.reshape(H, HD, flat.shape[-1]), 1).reshape(flat.shape)


def rotate(per_head, tables):
    row_cos, row_sin, col_cos, col_sin = tables
    quarter = per_head.shape[1] // 4
    part_one = per_head[:, :quarter]
    part_two = per_head[:, quarter : 2 * quarter]
    part_three = per_head[:, 2 * quarter : 3 * quarter]
    part_four = per_head[:, 3 * quarter :]
    return jnp.concatenate(
        [
            part_one * row_cos - part_two * row_sin,
            part_two * row_cos + part_one * row_sin,
            part_three * col_cos - part_four * col_sin,
            part_four * col_cos + part_three * col_sin,
        ],
        axis=1,
    )


def dot(a, b, dims=((1,), (0,))):
    return lax.dot_general(a, b, (dims, ((), ())), preferred_element_type=f32)


NN = ((1,), (0,))
TN = ((0,), (0,))
NT = ((1,), (1,))


def heads_of(ref):
    pair = ref[...].astype(f32)
    return pair[:HD].astype(bf16), pair[HD:].astype(bf16)


def attend_kernel(blocks, *refs):
    q_ref = refs[0]
    k_refs = refs[1 : 1 + blocks]
    v_refs = refs[1 + blocks : 1 + 2 * blocks]
    o_ref, inv_ref = refs[1 + 2 * blocks :]
    q_heads = heads_of(q_ref)
    k_heads = [heads_of(r) for r in k_refs]
    v_heads = [heads_of(r) for r in v_refs]
    outs = []
    for i in range(2):
        total = None
        summed = None
        for k_pair, v_pair in zip(k_heads, v_heads):
            scores = dot(k_pair[i], q_heads[i], TN)
            probs = jnp.exp2(scores * SCALE_LOG2)
            part_sum = jnp.sum(probs, axis=0, keepdims=True)
            part = dot(v_pair[i], probs.astype(bf16), NN)
            total = part if total is None else total + part
            summed = part_sum if summed is None else summed + part_sum
        inverse = 1.0 / summed
        outs.append(total * inverse)
        inv_ref[0, i : i + 1, :] = inverse
    o_ref[...] = jnp.concatenate(outs, axis=0).astype(bf16)


def attend(query, keys, values):
    blocks = len(keys)
    tokens = query.shape[1]
    per_key = keys[0].shape[1]
    spec_q = pl.BlockSpec((PAIR, tokens), lambda h: (h, 0))
    spec_k = pl.BlockSpec((PAIR, per_key), lambda h: (h, 0))
    return pl.pallas_call(
        functools.partial(attend_kernel, blocks),
        grid=(H // 2,),
        in_specs=[spec_q] + [spec_k] * (2 * blocks),
        out_specs=[spec_q, pl.BlockSpec((1, 2, tokens), lambda h: (h, 0, 0))],
        out_shape=[
            jax.ShapeDtypeStruct((H * HD, tokens), bf16),
            jax.ShapeDtypeStruct((H // 2, 2, tokens), f32),
        ],
        compiler_params=pltpu.CompilerParams(vmem_limit_bytes=48 * 2**20),
        cost_estimate=pl.CostEstimate(
            flops=2 * 2 * H * 128 * tokens * per_key * blocks,
            bytes_accessed=2 * H * HD * (3 * tokens + 2 * per_key * blocks),
            transcendentals=H * tokens * per_key * blocks,
        ),
        name="attend",
    )(query, *keys, *values)


def attend_back_kernel(blocks, *refs):
    q_ref, g_ref, o_ref, inv_ref = refs[:4]
    k_refs = refs[4 : 4 + blocks]
    v_refs = refs[4 + blocks : 4 + 2 * blocks]
    dq_ref = refs[4 + 2 * blocks]
    dk_refs = refs[5 + 2 * blocks : 5 + 3 * blocks]
    dv_refs = refs[5 + 3 * blocks : 5 + 4 * blocks]
    q_heads = heads_of(q_ref)
    g_heads = heads_of(g_ref)
    gated = g_ref[...].astype(f32) * o_ref[...].astype(f32)
    k_heads = [heads_of(r) for r in k_refs]
    v_heads = [heads_of(r) for r in v_refs]
    grad_queries = []
    grad_keys = [[] for _ in range(blocks)]
    grad_values = [[] for _ in range(blocks)]
    for i in range(2):
        row_dot = jnp.sum(gated[i * HD : (i + 1) * HD], axis=0, keepdims=True)
        inverse = inv_ref[0, i : i + 1, :]
        grad_q = None
        for b in range(blocks):
            k_one, v_one = k_heads[b][i], v_heads[b][i]
            scores = dot(k_one, q_heads[i], TN)
            exact = jnp.exp2(scores * SCALE_LOG2) * inverse
            grad_probs = dot(v_one, g_heads[i], TN)
            grad_scores = (exact * (grad_probs - row_dot)).astype(bf16)
            part = dot(k_one, grad_scores, NN)
            grad_q = part if grad_q is None else grad_q + part
            grad_keys[b].append(dot(q_heads[i], grad_scores, NT) * SCALE)
            grad_values[b].append(dot(g_heads[i], exact.astype(bf16), NT))
        grad_queries.append(grad_q * SCALE)
    dq_ref[...] = jnp.concatenate(grad_queries, axis=0)
    for b in range(blocks):
        dk_refs[b][...] = jnp.concatenate(grad_keys[b], axis=0).astype(dk_refs[b].dtype)
        dv_refs[b][...] = jnp.concatenate(grad_values[b], axis=0).astype(dv_refs[b].dtype)


def attend_back(query, grad, out, inverse, keys, values):
    blocks = len(keys)
    tokens = query.shape[1]
    per_key = keys[0].shape[1]
    spec_q = pl.BlockSpec((PAIR, tokens), lambda h: (h, 0))
    spec_k = pl.BlockSpec((PAIR, per_key), lambda h: (h, 0))
    shapes_k = [jax.ShapeDtypeStruct((H * HD, per_key), kind) for kind in (f32, bf16)]
    outs = pl.pallas_call(
        functools.partial(attend_back_kernel, blocks),
        grid=(H // 2,),
        in_specs=[spec_q] * 3
        + [pl.BlockSpec((1, 2, tokens), lambda h: (h, 0, 0))]
        + [spec_k] * (2 * blocks),
        out_specs=[spec_q] + [spec_k] * (2 * blocks),
        out_shape=[jax.ShapeDtypeStruct((H * HD, tokens), f32)] + shapes_k * 2,
        compiler_params=pltpu.CompilerParams(vmem_limit_bytes=56 * 2**20),
        cost_estimate=pl.CostEstimate(
            flops=5 * 2 * H * 128 * tokens * per_key * blocks,
            bytes_accessed=2 * H * HD * (6 * tokens + 6 * per_key * blocks),
            transcendentals=H * tokens * per_key * blocks,
        ),
        name="attend_back",
    )(query, grad, out, inverse, *keys, *values)
    return outs[0], outs[1 : 1 + blocks], outs[1 + blocks :]


def assemble_kernel(heights, layout, *refs):
    count = len(layout)
    place_ref = refs[0]
    pieces = refs[1 : 1 + count]
    wholes = refs[1 + count : 1 + count + len(heights)]
    held = refs[1 + count + len(heights) : -2]
    sem_in, sem_out = refs[-2:]
    loads = [
        pltpu.make_async_copy(piece, room, sem_in.at[i])
        for i, (piece, room) in enumerate(zip(pieces, held))
    ]
    for load in loads:
        load.start()
    stores = []
    for load, room, (rank, low, high) in zip(loads, held, layout):
        load.wait()
        top = 0
        for height, whole in zip(heights, wholes):
            begin, end = max(low, top), min(high, top + height)
            if begin < end:
                row = pl.multiple_of(place_ref[rank] * height, 16) + (begin - top)
                store = pltpu.make_async_copy(
                    room.at[pl.ds(begin - low, end - begin)],
                    whole.at[pl.ds(row, end - begin)],
                    sem_out.at[len(stores)],
                )
                store.start()
                stores.append(store)
            top += height
    for store in stores:
        store.wait()


def assemble(pieces, layout, heights, places):
    width = pieces[0].shape[1]
    total = sum(heights)
    return pl.pallas_call(
        functools.partial(assemble_kernel, heights, layout),
        in_specs=[pl.BlockSpec(memory_space=pltpu.SMEM)]
        + [pl.BlockSpec(memory_space=pl.ANY)] * len(pieces),
        out_specs=[pl.BlockSpec(memory_space=pl.ANY)] * len(heights),
        out_shape=[jax.ShapeDtypeStruct((8 * height, width), bf16) for height in heights],
        scratch_shapes=[pltpu.VMEM(piece.shape, bf16) for piece in pieces]
        + [
            pltpu.SemaphoreType.DMA((len(pieces),)),
            pltpu.SemaphoreType.DMA((len(pieces) * len(heights),)),
        ],
        compiler_params=pltpu.CompilerParams(vmem_limit_bytes=24 * 2**20),
        cost_estimate=pl.CostEstimate(
            flops=0, bytes_accessed=2 * 2 * 8 * total * width, transcendentals=0
        ),
        name="assemble",
    )(places, *pieces)


def outer_kernel(heights, sharing, half, place_ref, *refs):
    count = len(heights)
    outs = 5 if half else 1
    dy_refs = refs[: 2 * count]
    x_refs = refs[2 * count : -outs]
    if half:
        low_ref, high_ref, over_a_ref, over_b_ref, own_ref = refs[-outs:]

    def put(rank, top, block):
        if not half:
            refs[-1][rank, top : top + block.shape[0], :] = block
            return
        if rank < 3:
            (own_ref, over_b_ref, over_a_ref)[rank][top : top + block.shape[0], :] = block
            return
        end = top + block.shape[0]
        if top < half:
            low_ref[top : min(end, half), :] = block[: min(end, half) - top]
        if end > half:
            high_ref[max(top, half) - half : end - half, :] = block[max(top, half) - top :]

    top = 0
    for i, (height, x_index) in enumerate(zip(heights, sharing)):
        step = 4 if height <= 176 else 2 if height <= 352 else 1
        for start in range(0, 4, step):
            total = None
            for core in range(2):
                chosen = [
                    dy_refs[2 * i + core][
                        pl.ds(pl.multiple_of(place_ref[rank] * height, 16), height), :
                    ]
                    for rank in range(start, start + step)
                ]
                lhs = chosen[0] if step == 1 else jnp.concatenate(chosen, axis=0)
                part = dot(lhs, x_refs[2 * x_index + core][...], NT)
                total = part if total is None else total + part
            total = total.astype(bf16)
            for n in range(step):
                put(start + n, top, total[n * height : (n + 1) * height])
        top += height


def outer_blocks(places, groups, blocks, split):
    x_pairs = [x_pair for x_pair, _ in groups]
    dy_pairs = [dy for _, group in groups for dy in group]
    sharing = [i for i, (_, group) in enumerate(groups) for _ in group]
    heights = [dy[0].shape[0] // blocks for dy in dy_pairs]
    rows = sum(heights)
    half = rows // 32 * 16 if split else 0
    tokens = dy_pairs[0][0].shape[1]
    width = x_pairs[0][0].shape[0]
    cut = next(c for c in (1408, 1536, 512, 128) if width % c == 0)
    once = pl.Buffered(1)
    dy_specs = [
        pl.BlockSpec(dy.shape, lambda i, place: (0, 0), pipeline_mode=once)
        for pair in dy_pairs
        for dy in pair
    ]
    x_buffers = {"pipeline_mode": once} if cut == width else {}
    x_specs = [
        pl.BlockSpec((cut, x.shape[1]), lambda i, place: (i, 0), **x_buffers)
        for pair in x_pairs
        for x in pair
    ]
    sizes = (half, rows - half, rows, rows, rows)
    if split:
        out_specs = [pl.BlockSpec((size, cut), lambda i, place: (0, i)) for size in sizes]
        out_shape = [jax.ShapeDtypeStruct((size, width), bf16) for size in sizes]
    else:
        out_specs = [pl.BlockSpec((4, rows, cut), lambda i, place: (0, 0, i))]
        out_shape = [jax.ShapeDtypeStruct((4, rows, width), bf16)]
    return pl.pallas_call(
        functools.partial(outer_kernel, heights, sharing, half),
        grid_spec=pltpu.PrefetchScalarGridSpec(
            num_scalar_prefetch=1,
            grid=(width // cut,),
            in_specs=dy_specs + x_specs,
            out_specs=out_specs,
        ),
        out_shape=out_shape,
        compiler_params=pltpu.CompilerParams(vmem_limit_bytes=56 * 2**20),
        cost_estimate=pl.CostEstimate(
            flops=2 * 2 * 4 * rows * width * tokens,
            bytes_accessed=2 * (2 * tokens * (8 * rows + width) + 4 * rows * width),
            transcendentals=0,
        ),
        name="outer_blocks",
    )(places, *[dy for pair in dy_pairs for dy in pair], *[x for pair in x_pairs for x in pair])


def cut_kernel(seq, z_ref, *refs):
    term_refs, out_refs, held = refs[: -seq - 1], refs[-seq - 1 : -1], refs[-1]
    at_z = z_ref[0]
    rows, width = term_refs[0].shape
    part = width // seq

    def chunk(i, _):
        at = pl.ds(pl.multiple_of(i * 16, 16), 16)
        total = term_refs[0][at, :]
        if len(term_refs) > 1:
            total = sum(ref[at, :].astype(f32) for ref in term_refs).astype(bf16)
        for j in range(seq):
            held[j, at, :] = total[:, j * part : (j + 1) * part]
        return 0

    lax.fori_loop(0, rows // 16, chunk, 0)
    for step in range(seq):
        out_refs[step][...] = held[lax.rem(at_z + step, seq)]


def cut_sum(at_z, seq, *terms):
    rows, width = terms[0].shape
    return pl.pallas_call(
        functools.partial(cut_kernel, seq),
        in_specs=[pl.BlockSpec(memory_space=pltpu.SMEM)]
        + [pl.BlockSpec(memory_space=pltpu.VMEM)] * len(terms),
        out_specs=[pl.BlockSpec(memory_space=pltpu.VMEM)] * seq,
        out_shape=[jax.ShapeDtypeStruct((rows, width // seq), bf16)] * seq,
        scratch_shapes=[pltpu.VMEM((seq, rows, width // seq), bf16)],
        compiler_params=pltpu.CompilerParams(vmem_limit_bytes=32 * 2**20),
        cost_estimate=pl.CostEstimate(
            flops=2 * rows * width, bytes_accessed=8 * rows * width, transcendentals=0
        ),
        name="cut_sum",
    )(at_z.reshape(1), *terms)


def join_kernel(seq, z_ref, *refs):
    part_refs, out_ref, held = refs[:seq], refs[seq], refs[seq + 1]
    at_z = z_ref[0]
    rows, width = out_ref.shape
    for step in range(seq):
        held[lax.rem(at_z + seq - step, seq)] = part_refs[step][...]

    def chunk(i, _):
        at = pl.ds(pl.multiple_of(i * 16, 16), 16)
        out_ref[at, :] = jnp.concatenate([held[j, at, :] for j in range(seq)], axis=1)
        return 0

    lax.fori_loop(0, rows // 16, chunk, 0)


def join_parts(at_z, parts):
    seq = len(parts)
    rows, part = parts[0].shape
    return pl.pallas_call(
        functools.partial(join_kernel, seq),
        in_specs=[pl.BlockSpec(memory_space=pltpu.SMEM)]
        + [pl.BlockSpec(memory_space=pltpu.VMEM)] * seq,
        out_specs=pl.BlockSpec(memory_space=pltpu.VMEM),
        out_shape=jax.ShapeDtypeStruct((rows, seq * part), bf16),
        scratch_shapes=[pltpu.VMEM((seq, rows, part), bf16)],
        compiler_params=pltpu.CompilerParams(vmem_limit_bytes=32 * 2**20),
        cost_estimate=pl.CostEstimate(
            flops=0, bytes_accessed=4 * seq * rows * part, transcendentals=0
        ),
        name="join_parts",
    )(at_z.reshape(1), *parts)


def join_gathered_kernel(gathered_ref, out_ref):
    seq = gathered_ref.shape[0]

    def chunk(i, _):
        at = pl.ds(pl.multiple_of(i * 16, 16), 16)
        out_ref[at, :] = jnp.concatenate([gathered_ref[j, at, :] for j in range(seq)], axis=1)
        return 0

    lax.fori_loop(0, out_ref.shape[0] // 16, chunk, 0)


def join_gathered(gathered):
    seq, rows, part = gathered.shape
    return pl.pallas_call(
        join_gathered_kernel,
        in_specs=[pl.BlockSpec(memory_space=pltpu.VMEM)],
        out_specs=pl.BlockSpec(memory_space=pltpu.VMEM),
        out_shape=jax.ShapeDtypeStruct((rows, seq * part), bf16),
        compiler_params=pltpu.CompilerParams(vmem_limit_bytes=32 * 2**20),
        cost_estimate=pl.CostEstimate(
            flops=0, bytes_accessed=4 * seq * rows * part, transcendentals=0
        ),
        name="join_gathered",
    )(gathered)


def stack_kernel(*refs):
    term_refs, out_ref = refs[:-1], refs[-1]
    seq, _, part = out_ref.shape

    def chunk(i, _):
        at = pl.ds(pl.multiple_of(i * 16, 16), 16)
        total = sum(ref[at, :].astype(f32) for ref in term_refs).astype(bf16)
        for j in range(seq):
            out_ref[j, at, :] = total[:, j * part : (j + 1) * part]
        return 0

    lax.fori_loop(0, out_ref.shape[1] // 16, chunk, 0)


def stack_sum(seq, *terms):
    rows, width = terms[0].shape
    return pl.pallas_call(
        stack_kernel,
        in_specs=[pl.BlockSpec(memory_space=pltpu.VMEM)] * len(terms),
        out_specs=pl.BlockSpec(memory_space=pltpu.VMEM),
        out_shape=jax.ShapeDtypeStruct((seq, rows, width // seq), bf16),
        compiler_params=pltpu.CompilerParams(vmem_limit_bytes=32 * 2**20),
        cost_estimate=pl.CostEstimate(
            flops=2 * rows * width, bytes_accessed=8 * rows * width, transcendentals=0
        ),
        name="stack_sum",
    )(*terms)


def gelu_slope(x):
    scale = math.sqrt(2.0 / math.pi)
    bend = 0.044715
    curve = jnp.tanh(scale * (x + bend * x * x * x))
    return 0.5 * (1.0 + curve) + 0.5 * x * (1.0 - curve * curve) * scale * (1.0 + 3.0 * bend * x * x)


def mlp_up_kernel(up_ref, u_ref, hidden_ref, act_ref):
    hidden = dot(up_ref[...], u_ref[0], NN)
    hidden_ref[0] = hidden
    act_ref[0] = gelu_tanh(hidden).astype(bf16)


def mlp_down_kernel(down_ref, act_ref, out_ref):
    out_ref[0] = dot(down_ref[...], act_ref[0], NN).astype(bf16)


def mlp_back_kernel(down_flip_ref, up_flip_ref, grad_ref, hidden_ref, dh_ref, du_ref):
    grad_act = dot(down_flip_ref[...], grad_ref[0], NN)
    grad_hidden = (grad_act * gelu_slope(hidden_ref[0])).astype(bf16)
    dh_ref[0] = grad_hidden
    du_ref[0] = dot(up_flip_ref[...], grad_hidden, NN).astype(bf16)


def mlp_outer_kernel(a_ref, b_ref, out_ref, total_ref):
    step = pl.program_id(0)

    @pl.when(step == 0)
    def _():
        total_ref[...] = jnp.zeros_like(total_ref)

    total_ref[...] += dot(a_ref[0], b_ref[0], NT)

    @pl.when(step == pl.num_programs(0) - 1)
    def _():
        out_ref[...] = total_ref[...].astype(bf16)


def by_device(shape):
    return pl.BlockSpec((1,) + shape, lambda i: (i, 0, 0))


def kept(shape):
    return pl.BlockSpec(shape, lambda i: (0, 0))


def mlp_call(kernel, name, held, streams, outs, whole=None):
    count, _, tokens = streams[0].shape
    params = pltpu.CompilerParams(vmem_limit_bytes=48 * 2**20)
    flops = 2 * count * tokens * sum(x.shape[0] * x.shape[1] for x in held)
    moved = sum(x.size * 2 for x in streams) + sum(count * r * tokens * 3 for r, _ in outs)
    if whole:
        flops = 2 * count * tokens * whole[0] * whole[1]
        out_specs, out_shape = kept(whole), jax.ShapeDtypeStruct(whole, bf16)
        scratch = [pltpu.VMEM(whole, f32)]
    else:
        out_specs = [by_device((rows, tokens)) for rows, _ in outs]
        out_shape = [jax.ShapeDtypeStruct((count, rows, tokens), kind) for rows, kind in outs]
        scratch = []
    return pl.pallas_call(
        kernel,
        grid=(count,),
        in_specs=[kept(x.shape) for x in held] + [by_device(x.shape[1:]) for x in streams],
        out_specs=out_specs,
        out_shape=out_shape,
        scratch_shapes=scratch,
        compiler_params=params,
        cost_estimate=pl.CostEstimate(flops=flops, bytes_accessed=moved, transcendentals=0),
        name=name,
    )(*held, *streams)


def join_two_kernel(gathered_ref, first_ref, second_ref):
    seq = gathered_ref.shape[0]
    top = 0
    for out_ref in (first_ref, second_ref):
        rows, part = out_ref.shape[0], out_ref.shape[1] // seq

        def chunk(i, _, top=top, part=part, out_ref=out_ref):
            at = pl.ds(pl.multiple_of(i * 16, 16), 16)
            source = pl.ds(pl.multiple_of(top + i * 16, 16), 16)
            out_ref[at, :] = jnp.concatenate(
                [gathered_ref[j, source, :part] for j in range(seq)], axis=1
            )
            return 0

        lax.fori_loop(0, rows // 16, chunk, 0)
        top += rows


def join_two(gathered, first, second):
    seq = gathered.shape[0]
    shapes = [(rows, seq * part) for rows, part in (first, second)]
    return pl.pallas_call(
        join_two_kernel,
        in_specs=[pl.BlockSpec(memory_space=pltpu.VMEM)],
        out_specs=[pl.BlockSpec(memory_space=pltpu.VMEM)] * 2,
        out_shape=[jax.ShapeDtypeStruct(shape, bf16) for shape in shapes],
        compiler_params=pltpu.CompilerParams(vmem_limit_bytes=32 * 2**20),
        cost_estimate=pl.CostEstimate(
            flops=0, bytes_accessed=4 * gathered.size, transcendentals=0
        ),
        name="join_two",
    )(gathered)


def unpack_kernel(wide, tall, packed_ref, up_ref, down_ref):
    seq = packed_ref.shape[0]
    up_rows, down_rows = tall
    slabs = (packed_ref.shape[1] - up_rows) // down_rows

    def chunk(i, _):
        at = pl.ds(pl.multiple_of(i * 16, 16), 16)
        up_ref[at, :] = jnp.concatenate([packed_ref[z, at, :wide] for z in range(seq)], axis=1)
        return 0

    lax.fori_loop(0, up_rows // 16, chunk, 0)
    lanes = packed_ref.shape[2]
    for z in range(seq):
        for slab in range(slabs):
            left = (z * slabs + slab) * lanes
            top = up_rows + slab * down_rows
            down_ref[:, left : left + lanes] = packed_ref[z, top : top + down_rows, :]


def unpack(packed, seq, wide, tall):
    devices, rows, lanes = packed.shape
    blocks = devices // seq
    up_rows, down_rows = tall
    down_width = seq * lanes * ((rows - up_rows) // down_rows)
    return pl.pallas_call(
        functools.partial(unpack_kernel, wide, tall),
        grid=(blocks,),
        in_specs=[pl.BlockSpec((seq, rows, lanes), lambda p: (p, 0, 0))],
        out_specs=[
            pl.BlockSpec((up_rows, seq * wide), lambda p: (p, 0)),
            pl.BlockSpec((down_rows, down_width), lambda p: (p, 0)),
        ],
        out_shape=[
            jax.ShapeDtypeStruct((blocks * up_rows, seq * wide), bf16),
            jax.ShapeDtypeStruct((blocks * down_rows, down_width), bf16),
        ],
        compiler_params=pltpu.CompilerParams(vmem_limit_bytes=40 * 2**20),
        cost_estimate=pl.CostEstimate(
            flops=0, bytes_accessed=4 * devices * rows * lanes, transcendentals=0
        ),
        name="unpack",
    )(packed)


def pack_kernel(up_ref, down_ref, out_ref):
    seq, _, lanes = out_ref.shape
    up_rows, up_width = up_ref.shape
    part = up_width // seq
    down_rows, down_width = down_ref.shape
    block = down_rows // seq

    def chunk(i, _):
        at = pl.ds(pl.multiple_of(i * 16, 16), 16)
        rows = up_ref[at, :]
        fill = jnp.zeros((16, lanes - part), rows.dtype)
        for z in range(seq):
            out_ref[z, at, :] = jnp.concatenate(
                [rows[:, z * part : (z + 1) * part], fill], axis=1
            )
        return 0

    lax.fori_loop(0, up_rows // 16, chunk, 0)
    for z in range(seq):
        for slab in range(down_width // lanes):
            top = up_rows + slab * block
            out_ref[z, top : top + block, :] = down_ref[
                z * block : (z + 1) * block, slab * lanes : (slab + 1) * lanes
            ]


def pack(up_grad, down_grad, seq, lanes):
    rows = up_grad.shape[0] + down_grad.shape[0] // seq * (down_grad.shape[1] // lanes)
    return pl.pallas_call(
        pack_kernel,
        in_specs=[pl.BlockSpec(memory_space=pltpu.VMEM)] * 2,
        out_specs=pl.BlockSpec(memory_space=pltpu.VMEM),
        out_shape=jax.ShapeDtypeStruct((seq, rows, lanes), bf16),
        compiler_params=pltpu.CompilerParams(vmem_limit_bytes=32 * 2**20),
        cost_estimate=pl.CostEstimate(
            flops=0, bytes_accessed=4 * seq * rows * lanes, transcendentals=0
        ),
        name="pack",
    )(up_grad, down_grad)


def after(value, *others):
    return lax.optimization_barrier((value,) + others)[0]


SWAP = ((0, 1), (1, 0))


def swap(values, axis):
    return lax.ppermute(values, axis, SWAP)


def on_device(
    sizes,
    inputs,
    skipped,
    text_rows,
    condition,
    cotangent,
    norm_gains,
    skip_weight,
    shift_weight,
    query_key_weight,
    value_weight,
    self_output,
    cross_query,
    cross_memory,
    cross_output,
    up_weight,
    down_weight,
):
    outer, inner, cores, seq = sizes
    plane = outer * inner
    square = outer == 2 and inner == 2
    lat_count, local_rows, width = inputs.shape
    text_local = text_rows.shape[1]
    at_a = lax.axis_index("a")
    at_b = lax.axis_index("b")
    at_c = lax.axis_index("c")
    at_z = lax.axis_index("z")
    tokens = lat_count * local_rows

    def route(step):
        return [
            (
                core * seq + z,
                (z // lat_count) * seq + core * lat_count + (z % lat_count + step) % lat_count,
            )
            for core in range(cores)
            for z in range(seq)
        ]

    slot = at_z % lat_count

    def to_latent(values):
        parts = []
        for step in range(lat_count):
            chosen = lax.dynamic_index_in_dim(
                values, (slot + step) % lat_count, 0, keepdims=False
            )
            parts.append(lax.ppermute(chosen, ("c", "z"), route(step)))
        return jnp.concatenate(parts, axis=0)

    def from_latent(rows, *others):
        height = rows.shape[0] // lat_count
        parts = []
        for step in range(lat_count):
            back = [(target, source) for source, target in route(step)]
            parts.append(
                lax.ppermute(rows[step * height : (step + 1) * height], ("c", "z"), back)
            )
        parts = [after(part, *others) for part in parts]
        stacked = jnp.stack(parts + parts)
        return lax.dynamic_slice_in_dim(stacked, (lat_count - slot) % lat_count, lat_count, 0)

    places = jnp.stack(
        [
            ((at_a + da) % outer * inner + (at_b + db) % inner) * cores + (at_c + dc) % cores
            for dc in range(2)
            for da in range(2)
            for db in range(2)
        ]
    ).astype(jnp.int32)
    here = {"a": at_a, "b": at_b, "c": at_c}

    def z_shift(values, step):
        return lax.ppermute(values, "z", [(z, (z + step) % seq) for z in range(seq)])

    def z_send(values):
        return [values] + [z_shift(values, step) for step in range(1, seq)]

    def z_order(arrived):
        blocks = []
        for z in range(seq):
            block = arrived[0]
            for step in range(1, seq):
                block = jnp.where(at_z == (z + step) % seq, arrived[step], block)
            blocks.append(block)
        return blocks

    def z_piece(arrived, *others):
        arrived = [after(part, *others) for part in arrived]
        if square:
            return join_parts(at_z, arrived)
        return jnp.concatenate(z_order(arrived), axis=1)

    def flip(shards):
        return jnp.concatenate([shard.T for shard in shards], axis=0)

    def gather_rows(values, axes):
        if not square:
            return lax.all_gather(values, axes[::-1], axis=0, tiled=True)
        for axis in axes:
            other = swap(values, axis)
            lower = here[axis] == 0
            values = jnp.concatenate(
                [jnp.where(lower, values, other), jnp.where(lower, other, values)], axis=0
            )
        return values

    def to_rank(values, rank):
        axes = tuple(axis for axis, bit in (("c", 4), ("a", 2), ("b", 1)) if rank & bit)
        axes = tuple(axis for axis in ("a", "b", "c") if axis in axes)
        last = 2 ** len(axes) - 1
        return lax.ppermute(values, axes, [(i, last - i) for i in range(last + 1)])

    def exchange(blocks):
        return [blocks[0]] + [to_rank(blocks[rank], rank) for rank in range(1, 8)]

    def stack_by_device(blocks):
        rows = blocks[0].shape[0]
        layout = tuple((rank, 0, rows) for rank in range(8))
        return assemble(tuple(blocks), layout, [rows], places)[0]

    def hop_one(piece):
        return swap(piece, "b"), swap(piece, "a")

    def halves(over_b, over_a):
        half = over_b.shape[0] // 32 * 16
        return over_b[:half], over_a[half:]

    def hop_two(low, high):
        return swap(low, "a"), swap(high, "b")

    def after_all(parts, *others):
        return tuple(lax.optimization_barrier(tuple(parts) + others)[: len(parts)])

    def to_core(parts):
        return tuple(swap(part, "c") for part in parts)

    def whole_of(mine, others, shards):
        rows = mine[0].shape[0]
        half = mine[3].shape[0]
        spans = ((0, 0, rows), (1, 0, rows), (2, 0, rows), (3, 0, half), (3, half, rows))
        layout = spans + tuple((rank + 4, begin, end) for rank, begin, end in spans)
        return assemble(mine + others, layout, [shard.shape[1] for shard in shards], places)

    def gather_plain(piece, shards):
        heights = [shard.shape[1] for shard in shards]
        starts = [sum(heights[:i]) for i in range(len(heights))]
        return [
            lax.all_gather(piece[s : s + h], ("a", "b", "c"), axis=0, tiled=True)
            for s, h in zip(starts, heights)
        ]

    in_order = jnp.arange(4, dtype=jnp.int32) * cores + at_c

    def outer_of(*groups, split=True):
        if square:
            return outer_blocks(
                places[:4] if split else in_order, groups, plane * cores, split
            )
        outs = []
        for x_pair, dy_pairs in groups:
            for dy_pair in dy_pairs:
                total = 0.0
                for dy, x in zip(dy_pair, x_pair):
                    cube = dy.reshape(plane, cores, -1, dy.shape[1])
                    mine = lax.dynamic_index_in_dim(cube, at_c, 1, keepdims=False)
                    total = total + dot(mine.reshape(-1, dy.shape[1]), x, NT)
                cube = total.astype(bf16).reshape(plane, -1, x_pair[0].shape[0])
                outs.append(
                    lax.psum_scatter(cube, ("a", "b"), scatter_dimension=0, tiled=True)[0]
                )
        return (jnp.concatenate(outs, axis=0),)

    def sum_far(state):
        low, high, over_a, over_b, own = state
        return swap(low, "b"), swap(high, "a"), over_a, over_b, own

    def sum_near(state, *others):
        low, high, over_a, over_b, own = state
        half = low.shape[0]
        low = after(low, *others)
        over_a = lax.dynamic_update_slice(over_a, over_a[:half] + low, (0, 0))
        over_b = lax.dynamic_update_slice(over_b, over_b[half:] + high, (half, 0))
        return own, swap(over_a, "a"), swap(over_b, "b"), (over_a, over_b)

    def sum_z(state, *others):
        own, got_a, got_b, _ = state
        parts = cut_sum(at_z, seq, own, after(got_a, *others), got_b)
        return [parts[0]] + [z_shift(parts[step], step) for step in range(1, seq)]

    def sum_z_offloaded(state, *others):
        own, got_a, got_b, _ = state
        stacked = stack_sum(seq, own, after(got_a, *others), got_b)
        return [lax.psum_scatter(stacked, "z", scatter_dimension=0, tiled=True)[0]], stacked

    def sum_plain(state):
        (total,) = state
        cut = total.reshape(total.shape[0], seq, -1).transpose(1, 0, 2)
        return [
            z_shift(lax.dynamic_index_in_dim(cut, (at_z + step) % seq, 0, keepdims=False), step)
            for step in range(seq)
        ]

    def sum_end(parts, shards, *others):
        owned = sum(after(part, *others).astype(f32) for part in parts)
        results = []
        start = 0
        for shard in shards:
            results.append(owned[start : start + shard.shape[1]].T)
            start += shard.shape[1]
        return results

    gain_skip = norm_gains[: 2 * width]
    gain_one = norm_gains[2 * width : 3 * width]
    gain_two = norm_gains[3 * width : 4 * width]
    gain_three = norm_gains[4 * width :]

    skip_set = [skip_weight]
    pair_set = [query_key_weight, value_weight, shift_weight]
    self_set = [self_output, cross_query, cross_output]
    memory_set = [cross_memory]
    up_set = [up_weight]
    down_set = [down_weight]
    skip_flip, pair_flip, self_flip, memory_flip, up_flip, down_flip = (
        flip(one) for one in (skip_set, pair_set, self_set, memory_set, up_set, down_set)
    )
    if square:
        skip_sent = z_send(skip_flip)
        lanes = down_weight.shape[0] // seq
        cross_flip = jnp.concatenate(
            [
                jnp.pad(one, ((0, 0), (0, lanes - one.shape[1])))
                for one in (self_flip, memory_flip)
            ],
            axis=0,
        )
        cross_flip = after(cross_flip, pair_flip)
        up_padded = jnp.pad(up_flip, ((0, 0), (0, lanes - up_flip.shape[1])))
        slabs = [down_flip[:, i * lanes : (i + 1) * lanes] for i in range(seq)]
        mlp_flip = jnp.concatenate([up_padded] + slabs, axis=0)
        pair_sent = lax.all_gather(pair_flip, "z", axis=0, tiled=False)
        cross_sent = lax.all_gather(cross_flip, "z", axis=0, tiled=False)
        skip_piece = z_piece(skip_sent)
        skip_near = hop_one(skip_piece)
        skip_half = halves(*skip_near)
        skip_far = hop_two(*skip_half)
        pair_piece = join_gathered(after(pair_sent, *skip_half))
        pair_near = hop_one(pair_piece)
        skip_far = after_all(skip_far, pair_piece)
        skip_mine = (skip_piece,) + skip_near + skip_far
        skip_other = to_core(skip_mine)
        (skip_t,) = whole_of(skip_mine, skip_other, skip_set)
        joined = jnp.concatenate(
            [
                inputs.reshape(tokens, width).T,
                skipped.reshape(tokens, width).T,
            ],
            axis=0,
        ).astype(f32)
        level_zero = norm_gain(joined, gain_skip).astype(bf16)
        start_zero = dot(skip_t, level_zero).astype(bf16)
        zero_sent = to_latent(start_zero.T.reshape(inputs.shape))
        pair_near = after_all(pair_near, start_zero)
        pair_half = halves(*pair_near)
        pair_far = hop_two(*pair_half)
        self_piece, memory_piece = join_two(
            after(cross_sent, *pair_half), self_flip.shape, memory_flip.shape
        )
        pair_far = after_all(pair_far, self_piece)
        pair_mine = (pair_piece,) + pair_near + pair_far
        pair_other = to_core(pair_mine)
        self_near = hop_one(self_piece)
        memory_near = hop_one(memory_piece)
        stream_zero = after(zero_sent, *pair_far).T.astype(f32)
        mlp_sent = lax.all_gather(after(mlp_flip, zero_sent), "z", axis=0, tiled=False)
        pair_t, value_t, shift_t = whole_of(pair_mine, pair_other, pair_set)
    else:
        chip_both = to_latent(jnp.concatenate([inputs, skipped], axis=-1))
        joined = chip_both.T.astype(f32)
        level_zero = norm_gain(joined, gain_skip).astype(bf16)
        chip_text = to_latent(text_rows).T
        chip_grad = to_latent(cotangent).T
        (skip_t,) = gather_plain(z_piece(z_send(skip_flip)), skip_set)
        pair_t, value_t, shift_t = gather_plain(z_piece(z_send(pair_flip)), pair_set)
        self_t, cq_t, cout_t = gather_plain(z_piece(z_send(self_flip)), self_set)
        (memory_t,) = gather_plain(z_piece(z_send(memory_flip)), memory_set)
        (up_t,) = gather_plain(z_piece(z_send(up_flip)), up_set)
        (down_t,) = gather_plain(z_piece(z_send(down_flip)), down_set)
        stream_zero = dot(skip_t, level_zero)

    quarter = HD // 4
    frequency = jnp.power(10000.0, -jnp.arange(quarter, dtype=f32) / quarter)
    position = jnp.concatenate(
        [
            (at_c * lat_count + (slot - step) % lat_count) * local_rows
            + jnp.arange(local_rows, dtype=jnp.int32)
            for step in range(lat_count)
        ]
    )
    row_angle = (position // GRID).astype(f32)[None, :] * frequency[:, None]
    col_angle = (position % GRID).astype(f32)[None, :] * frequency[:, None]
    tables = (jnp.cos(row_angle), jnp.sin(row_angle), jnp.cos(col_angle), jnp.sin(col_angle))

    def prepare(flat):
        cube = flat.reshape(H, HD, flat.shape[-1])
        return rotate(normalize(cube, 1), tables).reshape(flat.shape)

    cond_pair = (condition, swap(condition, "c"))
    same_core = at_z // lat_count == at_c
    cond_two = jnp.where(same_core, cond_pair[0], cond_pair[1])
    chip_cond = lax.dynamic_index_in_dim(cond_two, slot, 0, keepdims=False)
    shift = dot(shift_t, jax.nn.silu(chip_cond.astype(f32)).astype(bf16)[:, None], NN)[:, 0]

    level_one = shifted_norm(stream_zero, gain_one, shift).astype(bf16)
    pair_proj = dot(pair_t, level_one)
    value_proj = dot(value_t, level_one).astype(bf16)
    query_flat = pair_proj[:width]
    key_flat = pair_proj[width:]
    query = prepare(query_flat).astype(bf16)
    key = prepare(key_flat).astype(bf16)
    keys = [key, swap(key, "c")]
    values = [value_proj, swap(value_proj, "c")]
    query_next = query
    if square:
        self_near = after_all(self_near, query)
        self_half = halves(*self_near)
        self_far = hop_two(*self_half)
        query_next = after(query, *self_half)
    attended, self_inverse = attend(query_next, keys, values)
    attended_next = attended
    if square:
        all_plane = ("a", "b", "c")
        up_piece, down_piece = unpack(
            after(mlp_sent, attended),
            seq,
            up_flip.shape[1],
            (up_flip.shape[0], down_flip.shape[0]),
        )
        slice_rows = up_weight.shape[1]
        down_blocks = [
            lax.dynamic_slice_in_dim(down_piece, places[rank] * slice_rows, slice_rows, 1)
            for rank in range(8)
        ]
        text_padded = jnp.pad(text_rows, ((0, 0), (0, 0), (0, width - text_rows.shape[2])))
        mixed = to_latent(after(jnp.concatenate([cotangent, text_padded], axis=1), query))
        mixed = mixed.reshape(lat_count, -1, width)
        attended_next = after(attended, up_piece)
        down_sent = exchange(down_blocks)
        memory_near = after_all(memory_near, attended)
        memory_half = halves(*memory_near)
        memory_far = hop_two(*memory_half)
        self_far = after_all(self_far, *memory_half)
        self_mine = (self_piece,) + self_near + self_far
        self_other = to_core(self_mine)
        memory_far = after_all(memory_far, *self_far)
        memory_mine = (memory_piece,) + memory_near + memory_far
        memory_other = to_core(memory_mine)
        self_t, cq_t, cout_t = whole_of(self_mine, self_other, self_set)
        (memory_t,) = whole_of(memory_mine, memory_other, memory_set)
        mixed = after(mixed, *memory_far)
        chip_text = mixed[:, local_rows:, : text_rows.shape[2]].reshape(-1, text_rows.shape[2]).T
    stream_one = stream_zero + dot(self_t, attended_next)
    level_two = norm_gain(stream_one, gain_two).astype(bf16)
    cross_proj = dot(cq_t, level_two)
    cross = head_norm(cross_proj).astype(bf16)
    memory_proj = dot(memory_t, chip_text)
    memory_key_flat = memory_proj[:width]
    memory_key = head_norm(memory_key_flat).astype(bf16)
    memory_value = memory_proj[width:].astype(bf16)
    text_keys = [memory_key, swap(memory_key, "c")]
    text_values = [memory_value, swap(memory_value, "c")]
    cross_next = cross
    if square:
        chip_grad = mixed[:, :local_rows].reshape(-1, width).T
        grad_all = lax.all_gather(chip_grad, all_plane, axis=0, tiled=False)
        cross_next = after(cross, chip_grad)
    crossed, cross_inverse = attend(cross_next, text_keys, text_values)
    stream_two = stream_one + dot(cout_t, crossed)
    level_three = norm_gain(stream_two, gain_three).astype(bf16)
    def with_other(values):
        return values, swap(values, "c")

    one_pair = with_other(level_one)
    attended_pair = with_other(attended)
    two_pair = with_other(level_two)
    text_pair = with_other(chip_text)
    crossed_pair = with_other(crossed)
    if square:
        zero_pair = with_other(level_zero)
        swapped = [
            pair[1]
            for pair in (one_pair, attended_pair, two_pair, text_pair, crossed_pair, zero_pair)
        ]
        up_slice = after(up_piece, *swapped)
        three_all = lax.all_gather(
            after(level_three, grad_all), all_plane, axis=0, tiled=False
        )
        down_slice = stack_by_device([after(part, level_three) for part in down_sent])
        hidden, activated = mlp_call(
            mlp_up_kernel,
            "mlp_up",
            [up_slice],
            [three_all],
            [(slice_rows, f32), (slice_rows, bf16)],
        )
    else:
        hidden = dot(up_t, level_three)
        activated = gelu_tanh(hidden).astype(bf16)

    if square:
        grad_hidden, part = mlp_call(
            mlp_back_kernel,
            "mlp_back",
            [down_slice.T, up_slice.T],
            [grad_all, hidden],
            [(slice_rows, bf16), (width, bf16)],
        )
        grad_level_three = lax.psum_scatter(part, all_plane, scatter_dimension=0, tiled=True)[0]
        down_grad = mlp_call(
            mlp_outer_kernel,
            "mlp_outer",
            [],
            [after(grad_all, part), activated],
            [],
            (width, slice_rows),
        )
        down_parts = exchange(
            [
                lax.dynamic_slice_in_dim(
                    down_grad, places[rank] * (width // 8), width // 8, 0
                )
                for rank in range(8)
            ]
        )
        up_grad = mlp_call(
            mlp_outer_kernel,
            "mlp_outer",
            [],
            [after(grad_hidden, down_grad), three_all],
            [],
            (slice_rows, width),
        )
        (out_part,) = mlp_call(
            mlp_down_kernel,
            "mlp_down",
            [down_slice],
            [after(activated, up_grad)],
            [(width, bf16)],
        )
        down_whole = stack_by_device([after(part, out_part) for part in down_parts])
        mlp_cut = pack(up_grad, down_whole, seq, lanes)
        grad_level_three = after(grad_level_three, mlp_cut).astype(f32)
    else:
        grad_act = dot(down_t, chip_grad, TN)
        _, gelu_pull = jax.vjp(gelu_tanh, hidden)
        grad_hidden = gelu_pull(grad_act)[0].astype(bf16)
        down_outer = outer_of((with_other(activated), [with_other(chip_grad)]))
        up_outer = outer_of((with_other(level_three), [with_other(grad_hidden)]))
        grad_level_three = dot(up_t, grad_hidden, TN)
        zero_pair = with_other(level_zero)
    _, pull_three = jax.vjp(norm_gain, stream_two, gain_three)
    grad_from_three, grad_gain_three = pull_three(grad_level_three)
    grad_stream_two = chip_grad.astype(f32) + grad_from_three
    cross_back = grad_stream_two.astype(bf16)
    grad_crossed = dot(cout_t, cross_back, TN).astype(bf16)
    grad_cross, grad_tk, grad_tv = attend_back(
        cross, grad_crossed, crossed, cross_inverse, text_keys, text_values
    )
    grad_memory_key = grad_tk[0] + swap(grad_tk[1], "c").astype(f32)
    grad_memory_value = grad_tv[0] + swap(grad_tv[1], "c").astype(f32)
    _, pull_memory = jax.vjp(head_norm, memory_key_flat)
    grad_memory_proj = jnp.concatenate(
        [pull_memory(grad_memory_key)[0], grad_memory_value], axis=0
    ).astype(bf16)
    _, pull_cq = jax.vjp(head_norm, cross_proj)
    grad_cq_flat = pull_cq(grad_cross)[0].astype(bf16)
    if square:
        def spread(values):
            cube = values.reshape(seq, -1, values.shape[1])
            cube = jnp.pad(cube, ((0, 0), (0, width // seq - cube.shape[1]), (0, 0)))
            return cube.reshape(width, -1)

        cross_outer = outer_of(
            (crossed_pair, [with_other(cross_back)]),
            (two_pair, [with_other(grad_cq_flat)]),
            (tuple(spread(text) for text in text_pair), [with_other(grad_memory_proj)]),
        )
        cross_sum = sum_far(cross_outer)
    else:
        cross_outer = outer_of(
            (crossed_pair, [with_other(cross_back)]), (two_pair, [with_other(grad_cq_flat)])
        )
        memory_outer = outer_of((text_pair, [with_other(grad_memory_proj)]))
    grad_level_two = dot(cq_t, grad_cq_flat, TN)
    _, pull_two = jax.vjp(norm_gain, stream_one, gain_two)
    grad_from_two, grad_gain_two = pull_two(grad_level_two)
    grad_stream_one = grad_stream_two + grad_from_two
    self_back = grad_stream_one.astype(bf16)
    grad_attended = dot(
        self_t, after(self_back, cross_outer[0]), TN
    ).astype(bf16)
    grad_q, grad_k, grad_v = attend_back(
        query, grad_attended, attended, self_inverse, keys, values
    )
    if square:
        cross_sum = sum_near(cross_sum, grad_q)
        out_sum = lax.psum_scatter(
            after(out_part, grad_level_three), all_plane, scatter_dimension=0, tiled=True
        )[0]
        blended = (stream_two + after(out_sum, grad_q).astype(f32)).astype(bf16)
        mlp_sum = lax.psum_scatter(
            after(mlp_cut, grad_level_three), "z", scatter_dimension=0, tiled=True
        )[0]
        grad_q = after(grad_q, blended, *cross_sum[3])
    grad_key = grad_k[0] + swap(grad_k[1], "c").astype(f32)
    grad_value_proj = (grad_v[0] + swap(grad_v[1], "c").astype(f32)).astype(bf16)
    _, pull_query = jax.vjp(prepare, query_flat)
    _, pull_key = jax.vjp(prepare, key_flat)
    grad_pair_proj = jnp.concatenate([pull_query(grad_q)[0], pull_key(grad_key)[0]], axis=0).astype(
        bf16
    )
    first_outer = outer_of(
        (attended_pair, [with_other(self_back)]),
        (one_pair, [with_other(grad_value_proj), with_other(grad_pair_proj)]),
    )
    if square:
        first_sum = sum_far(first_outer)
        cross_sum, stacked = sum_z_offloaded(cross_sum, first_outer[0])
        early = [stacked, mlp_sum]
    else:
        early = []
        blended = (stream_two + dot(down_t, activated)).astype(bf16)
    grad_text_rows = dot(grad_memory_proj, memory_t, TN).astype(bf16)
    text_width = text_rows.shape[2]
    back = jnp.concatenate(
        [
            blended.T.reshape(lat_count, -1, width),
            jnp.pad(grad_text_rows, ((0, 0), (0, width - text_width))).reshape(
                lat_count, -1, width
            ),
        ],
        axis=1,
    )
    back = from_latent(back.reshape(-1, width), first_outer[0])
    blended_out = back[:, :local_rows]
    grad_text = back[:, local_rows:, :text_width].astype(f32)
    grad_pair_next = after(grad_pair_proj, first_outer[0], back, *early)
    grad_level_one = dot(pair_t, grad_pair_next, TN) + dot(value_t, grad_value_proj, TN)
    _, pull_one = jax.vjp(shifted_norm, stream_zero, gain_one, shift)
    grad_from_one, grad_gain_one, grad_shift_part = pull_one(grad_level_one)
    skip_back = (grad_stream_one + grad_from_one).astype(bf16)
    if square:
        first_sum = sum_near(first_sum, skip_back)
        skip_back_rows = from_latent(skip_back.T, *first_sum[3]).reshape(tokens, width)
        skip_outer = outer_of((zero_pair, [with_other(skip_back_rows.T)]))
        skip_sum = sum_far(skip_outer)
        skip_back_rows = after(skip_back_rows, skip_outer[0])
    else:
        skip_outer = outer_of((zero_pair, [with_other(skip_back)]))
        skip_back_rows = from_latent(skip_back.T).reshape(tokens, width)
    grad_level_zero = dot(skip_back_rows, skip_t, NN)
    if square:
        skip_sum = sum_near(skip_sum, grad_level_zero)
        first_sum, stacked = sum_z_offloaded(first_sum, *skip_sum[3])
        late = stacked
        up_rows, up_part = up_weight.shape[1], up_weight.shape[0]
        mlp_sum = after(mlp_sum, late).astype(f32)
        grad_up = mlp_sum[:up_rows, :up_part].T
        grad_down = (
            mlp_sum[up_rows:]
            .reshape(slice_rows // lanes, cores, -1, lanes)
            .transpose(1, 0, 3, 2)
            .reshape(cores * slice_rows, -1)
        )
        skip_sum = sum_z(skip_sum, stacked)
        late = skip_sum[0]
        grad_cout, grad_cq, grad_memory = sum_end(
            cross_sum, [cross_output, cross_query, cross_memory], late
        )
        grad_memory = grad_memory[: cross_memory.shape[0]]
        grad_self, grad_value, grad_pair = sum_end(
            first_sum, [self_output, value_weight, query_key_weight], late
        )
        (grad_skip_w,) = sum_end(skip_sum, skip_set, grad_pair)
    else:
        (grad_down,) = sum_end(sum_plain(down_outer), down_set)
        (grad_up,) = sum_end(sum_plain(up_outer), up_set)
        grad_cout, grad_cq = sum_end(sum_plain(cross_outer), [cross_output, cross_query])
        (grad_memory,) = sum_end(sum_plain(memory_outer), memory_set)
        grad_self, grad_value, grad_pair = sum_end(
            sum_plain(first_outer), [self_output, value_weight, query_key_weight]
        )
        (grad_skip_w,) = sum_end(sum_plain(skip_outer), skip_set)

    joined_rows = jnp.concatenate([inputs, skipped], axis=-1).astype(f32).reshape(tokens, -1)
    _, pull_zero = jax.vjp(norm_gain_rows, joined_rows, gain_skip)
    grad_joined, grad_gain_skip = pull_zero(grad_level_zero)
    grad_input = grad_joined[:, :width].reshape(inputs.shape)
    grad_skipped = grad_joined[:, width:].reshape(inputs.shape)
    small = jnp.concatenate(
        [grad_shift_part, grad_gain_skip, grad_gain_one, grad_gain_two, grad_gain_three]
    ).reshape(-1, width)
    if square:
        small = jnp.concatenate([after(small, stacked), condition.astype(f32)], axis=0)
        held = jnp.zeros((8,) + small.shape, f32)
        for rank in range(8):
            arrived = to_rank(small, rank) if rank else small
            held = lax.dynamic_update_slice(held, arrived[None], (places[rank], 0, 0))
        shift_plane = held[:, 0].reshape(plane, cores, width).sum(axis=1)
        gain_plane = sum(held[i, 1:-lat_count] for i in range(8))
        cond_rows = held[:, -lat_count:].reshape(-1, width)
        columns = z_order(z_send(jnp.concatenate([gain_plane, shift_plane], axis=0)))
        gain_rows = len(gain_plane)
        grad_gains = sum(column[:gain_rows] for column in columns).reshape(-1)
        shift_grads = jnp.stack([column[gain_rows:] for column in columns], axis=1)
        shift_grads = shift_grads.reshape(-1, width)
    else:
        cond_rows = gather_rows(condition, ("c", "b", "a")).astype(f32)
        grad_gains = lax.psum(small[1:], ("a", "b", "c", "z")).reshape(-1)
        shift_grads = lax.all_gather(lax.psum(small[:1], "c"), ("a", "b", "z"), axis=0, tiled=True)
    cond_act = jax.nn.silu(cond_rows).astype(bf16)
    block_in, block_out = shift_weight.shape
    cond_block = lax.dynamic_slice_in_dim(cond_act, at_z * block_in, block_in, 1).astype(f32)
    own_columns = ((at_a * inner + at_b) * cores + at_c) * block_out
    grad_shift = jnp.dot(
        cond_block.T,
        lax.dynamic_slice_in_dim(shift_grads, own_columns, block_out, 1),
        precision=lax.Precision.HIGHEST,
    )

    return (
        blended_out,
        grad_input,
        grad_skipped,
        grad_text,
        grad_gains,
        grad_skip_w,
        grad_shift,
        grad_pair,
        grad_value,
        grad_self,
        grad_cq,
        grad_memory,
        grad_cout,
        grad_up,
        grad_down,
    )


def solution(mesh):
    dp, seq = mesh.shape["dp"], mesh.shape["seq"]
    inner, cores = 2, 2
    sizes = (dp // (inner * cores), inner, cores, seq)
    split = Mesh(mesh.devices.reshape(sizes), ("a", "b", "c", "z"))
    rows = P(("a", "b", "c"), "z", None)
    blocks = P("z", ("a", "b", "c"))
    return jax.shard_map(
        functools.partial(on_device, sizes),
        mesh=split,
        in_specs=(rows, rows, rows, P(("a", "b", "c"), None), rows, P()) + (blocks,) * 10,
        out_specs=(rows, rows, rows, rows, P()) + (blocks,) * 10,
        check_vma=False,
    )
```

```python
import functools
import math

import jax
import jax.numpy as jnp
from jax import lax
from jax.experimental import pallas as pl
from jax.experimental.pallas import tpu as pltpu
from jax.sharding import Mesh
from jax.sharding import PartitionSpec as P

H = 16
HD = 88
GRID = 32
PAIR = 2 * HD

epsilon = 1e-06
SCALE = HD ** (-0.5)
SCALE_LOG2 = SCALE * math.log2(math.e)

f32 = jnp.float32
bf16 = jnp.bfloat16


def normalize(values, axis):
    center = values - jnp.mean(values, axis=axis, keepdims=True)
    spread = jnp.mean(center * center, axis=axis, keepdims=True)
    return center * lax.rsqrt(spread + epsilon)


def norm_gain(values, gain_vec):
    return normalize(values, 0) * gain_vec[:, None]


def shifted_norm(values, gain_vec, offset):
    return normalize(values, 0) * gain_vec[:, None] + offset[:, None]


def norm_gain_rows(values, gain_vec):
    return normalize(values, -1) * gain_vec


def gelu_tanh(values):
    return jax.nn.gelu(values, approximate=True)


def head_norm(flat):
    return normalize(flat.reshape(H, HD, flat.shape[-1]), 1).reshape(flat.shape)


def rotate(per_head, tables):
    row_cos, row_sin, col_cos, col_sin = tables
    quarter = per_head.shape[1] // 4
    part_one = per_head[:, :quarter]
    part_two = per_head[:, quarter : 2 * quarter]
    part_three = per_head[:, 2 * quarter : 3 * quarter]
    part_four = per_head[:, 3 * quarter :]
    return jnp.concatenate(
        [
            part_one * row_cos - part_two * row_sin,
            part_two * row_cos + part_one * row_sin,
            part_three * col_cos - part_four * col_sin,
            part_four * col_cos + part_three * col_sin,
        ],
        axis=1,
    )


def dot(a, b, dims=((1,), (0,))):
    return lax.dot_general(a, b, (dims, ((), ())), preferred_element_type=f32)


NN = ((1,), (0,))
TN = ((0,), (0,))
NT = ((1,), (1,))


def heads_of(ref):
    pair = ref[...].astype(f32)
    return pair[:HD].astype(bf16), pair[HD:].astype(bf16)


def attend_kernel(blocks, *refs):
    q_ref = refs[0]
    k_refs = refs[1 : 1 + blocks]
    v_refs = refs[1 + blocks : 1 + 2 * blocks]
    o_ref, inv_ref = refs[1 + 2 * blocks :]
    q_heads = heads_of(q_ref)
    k_heads = [heads_of(r) for r in k_refs]
    v_heads = [heads_of(r) for r in v_refs]
    outs = []
    for i in range(2):
        total = None
        summed = None
        for k_pair, v_pair in zip(k_heads, v_heads):
            scores = dot(k_pair[i], q_heads[i], TN)
            probs = jnp.exp2(scores * SCALE_LOG2)
            part_sum = jnp.sum(probs, axis=0, keepdims=True)
            part = dot(v_pair[i], probs.astype(bf16), NN)
            total = part if total is None else total + part
            summed = part_sum if summed is None else summed + part_sum
        inverse = 1.0 / summed
        outs.append(total * inverse)
        inv_ref[0, i : i + 1, :] = inverse
    o_ref[...] = jnp.concatenate(outs, axis=0).astype(bf16)


def attend(query, keys, values):
    blocks = len(keys)
    tokens = query.shape[1]
    per_key = keys[0].shape[1]
    spec_q = pl.BlockSpec((PAIR, tokens), lambda h: (h, 0))
    spec_k = pl.BlockSpec((PAIR, per_key), lambda h: (h, 0))
    return pl.pallas_call(
        functools.partial(attend_kernel, blocks),
        grid=(H // 2,),
        in_specs=[spec_q] + [spec_k] * (2 * blocks),
        out_specs=[spec_q, pl.BlockSpec((1, 2, tokens), lambda h: (h, 0, 0))],
        out_shape=[
            jax.ShapeDtypeStruct((H * HD, tokens), bf16),
            jax.ShapeDtypeStruct((H // 2, 2, tokens), f32),
        ],
        compiler_params=pltpu.CompilerParams(vmem_limit_bytes=48 * 2**20),
        cost_estimate=pl.CostEstimate(
            flops=2 * 2 * H * 128 * tokens * per_key * blocks,
            bytes_accessed=2 * H * HD * (3 * tokens + 2 * per_key * blocks),
            transcendentals=H * tokens * per_key * blocks,
        ),
        name="attend",
    )(query, *keys, *values)


def attend_back_kernel(blocks, *refs):
    q_ref, g_ref, o_ref, inv_ref = refs[:4]
    k_refs = refs[4 : 4 + blocks]
    v_refs = refs[4 + blocks : 4 + 2 * blocks]
    dq_ref = refs[4 + 2 * blocks]
    dk_refs = refs[5 + 2 * blocks : 5 + 3 * blocks]
    dv_refs = refs[5 + 3 * blocks : 5 + 4 * blocks]
    q_heads = heads_of(q_ref)
    g_heads = heads_of(g_ref)
    gated = g_ref[...].astype(f32) * o_ref[...].astype(f32)
    k_heads = [heads_of(r) for r in k_refs]
    v_heads = [heads_of(r) for r in v_refs]
    grad_queries = []
    grad_keys = [[] for _ in range(blocks)]
    grad_values = [[] for _ in range(blocks)]
    for i in range(2):
        row_dot = jnp.sum(gated[i * HD : (i + 1) * HD], axis=0, keepdims=True)
        inverse = inv_ref[0, i : i + 1, :]
        grad_q = None
        for b in range(blocks):
            k_one, v_one = k_heads[b][i], v_heads[b][i]
            scores = dot(k_one, q_heads[i], TN)
            exact = jnp.exp2(scores * SCALE_LOG2) * inverse
            grad_probs = dot(v_one, g_heads[i], TN)
            grad_scores = (exact * (grad_probs - row_dot)).astype(bf16)
            part = dot(k_one, grad_scores, NN)
            grad_q = part if grad_q is None else grad_q + part
            grad_keys[b].append(dot(q_heads[i], grad_scores, NT) * SCALE)
            grad_values[b].append(dot(g_heads[i], exact.astype(bf16), NT))
        grad_queries.append(grad_q * SCALE)
    dq_ref[...] = jnp.concatenate(grad_queries, axis=0)
    for b in range(blocks):
        dk_refs[b][...] = jnp.concatenate(grad_keys[b], axis=0).astype(dk_refs[b].dtype)
        dv_refs[b][...] = jnp.concatenate(grad_values[b], axis=0).astype(dv_refs[b].dtype)


def attend_back(query, grad, out, inverse, keys, values):
    blocks = len(keys)
    tokens = query.shape[1]
    per_key = keys[0].shape[1]
    spec_q = pl.BlockSpec((PAIR, tokens), lambda h: (h, 0))
    spec_k = pl.BlockSpec((PAIR, per_key), lambda h: (h, 0))
    shapes_k = [jax.ShapeDtypeStruct((H * HD, per_key), kind) for kind in (f32, bf16)]
    outs = pl.pallas_call(
        functools.partial(attend_back_kernel, blocks),
        grid=(H // 2,),
        in_specs=[spec_q] * 3
        + [pl.BlockSpec((1, 2, tokens), lambda h: (h, 0, 0))]
        + [spec_k] * (2 * blocks),
        out_specs=[spec_q] + [spec_k] * (2 * blocks),
        out_shape=[jax.ShapeDtypeStruct((H * HD, tokens), f32)] + shapes_k * 2,
        compiler_params=pltpu.CompilerParams(vmem_limit_bytes=56 * 2**20),
        cost_estimate=pl.CostEstimate(
            flops=5 * 2 * H * 128 * tokens * per_key * blocks,
            bytes_accessed=2 * H * HD * (6 * tokens + 6 * per_key * blocks),
            transcendentals=H * tokens * per_key * blocks,
        ),
        name="attend_back",
    )(query, grad, out, inverse, *keys, *values)
    return outs[0], outs[1 : 1 + blocks], outs[1 + blocks :]


def assemble_kernel(heights, layout, *refs):
    count = len(layout)
    place_ref = refs[0]
    pieces = refs[1 : 1 + count]
    wholes = refs[1 + count : 1 + count + len(heights)]
    held = refs[1 + count + len(heights) : -2]
    sem_in, sem_out = refs[-2:]
    loads = [
        pltpu.make_async_copy(piece, room, sem_in.at[i])
        for i, (piece, room) in enumerate(zip(pieces, held))
    ]
    for load in loads:
        load.start()
    stores = []
    for load, room, (rank, low, high) in zip(loads, held, layout):
        load.wait()
        top = 0
        for height, whole in zip(heights, wholes):
            begin, end = max(low, top), min(high, top + height)
            if begin < end:
                row = pl.multiple_of(place_ref[rank] * height, 16) + (begin - top)
                store = pltpu.make_async_copy(
                    room.at[pl.ds(begin - low, end - begin)],
                    whole.at[pl.ds(row, end - begin)],
                    sem_out.at[len(stores)],
                )
                store.start()
                stores.append(store)
            top += height
    for store in stores:
        store.wait()


def assemble(pieces, layout, heights, places):
    width = pieces[0].shape[1]
    total = sum(heights)
    return pl.pallas_call(
        functools.partial(assemble_kernel, heights, layout),
        in_specs=[pl.BlockSpec(memory_space=pltpu.SMEM)]
        + [pl.BlockSpec(memory_space=pl.ANY)] * len(pieces),
        out_specs=[pl.BlockSpec(memory_space=pl.ANY)] * len(heights),
        out_shape=[jax.ShapeDtypeStruct((8 * height, width), bf16) for height in heights],
        scratch_shapes=[pltpu.VMEM(piece.shape, bf16) for piece in pieces]
        + [
            pltpu.SemaphoreType.DMA((len(pieces),)),
            pltpu.SemaphoreType.DMA((len(pieces) * len(heights),)),
        ],
        compiler_params=pltpu.CompilerParams(vmem_limit_bytes=24 * 2**20),
        cost_estimate=pl.CostEstimate(
            flops=0, bytes_accessed=2 * 2 * 8 * total * width, transcendentals=0
        ),
        name="assemble",
    )(places, *pieces)


def outer_kernel(heights, sharing, half, place_ref, *refs):
    count = len(heights)
    outs = 5 if half else 1
    dy_refs = refs[: 2 * count]
    x_refs = refs[2 * count : -outs]
    if half:
        low_ref, high_ref, over_a_ref, over_b_ref, own_ref = refs[-outs:]

    def put(rank, top, block):
        if not half:
            refs[-1][rank, top : top + block.shape[0], :] = block
            return
        if rank < 3:
            (own_ref, over_b_ref, over_a_ref)[rank][top : top + block.shape[0], :] = block
            return
        end = top + block.shape[0]
        if top < half:
            low_ref[top : min(end, half), :] = block[: min(end, half) - top]
        if end > half:
            high_ref[max(top, half) - half : end - half, :] = block[max(top, half) - top :]

    top = 0
    for i, (height, x_index) in enumerate(zip(heights, sharing)):
        step = 4 if height <= 176 else 2 if height <= 352 else 1
        for start in range(0, 4, step):
            total = None
            for core in range(2):
                chosen = [
                    dy_refs[2 * i + core][
                        pl.ds(pl.multiple_of(place_ref[rank] * height, 16), height), :
                    ]
                    for rank in range(start, start + step)
                ]
                lhs = chosen[0] if step == 1 else jnp.concatenate(chosen, axis=0)
                part = dot(lhs, x_refs[2 * x_index + core][...], NT)
                total = part if total is None else total + part
            total = total.astype(bf16)
            for n in range(step):
                put(start + n, top, total[n * height : (n + 1) * height])
        top += height


def outer_blocks(places, groups, blocks, split):
    x_pairs = [x_pair for x_pair, _ in groups]
    dy_pairs = [dy for _, group in groups for dy in group]
    sharing = [i for i, (_, group) in enumerate(groups) for _ in group]
    heights = [dy[0].shape[0] // blocks for dy in dy_pairs]
    rows = sum(heights)
    half = rows // 32 * 16 if split else 0
    tokens = dy_pairs[0][0].shape[1]
    width = x_pairs[0][0].shape[0]
    cut = next(c for c in (1408, 1536, 512, 128) if width % c == 0)
    once = pl.Buffered(1)
    dy_specs = [
        pl.BlockSpec(dy.shape, lambda i, place: (0, 0), pipeline_mode=once)
        for pair in dy_pairs
        for dy in pair
    ]
    x_buffers = {"pipeline_mode": once} if cut == width else {}
    x_specs = [
        pl.BlockSpec((cut, x.shape[1]), lambda i, place: (i, 0), **x_buffers)
        for pair in x_pairs
        for x in pair
    ]
    sizes = (half, rows - half, rows, rows, rows)
    if split:
        out_specs = [pl.BlockSpec((size, cut), lambda i, place: (0, i)) for size in sizes]
        out_shape = [jax.ShapeDtypeStruct((size, width), bf16) for size in sizes]
    else:
        out_specs = [pl.BlockSpec((4, rows, cut), lambda i, place: (0, 0, i))]
        out_shape = [jax.ShapeDtypeStruct((4, rows, width), bf16)]
    return pl.pallas_call(
        functools.partial(outer_kernel, heights, sharing, half),
        grid_spec=pltpu.PrefetchScalarGridSpec(
            num_scalar_prefetch=1,
            grid=(width // cut,),
            in_specs=dy_specs + x_specs,
            out_specs=out_specs,
        ),
        out_shape=out_shape,
        compiler_params=pltpu.CompilerParams(vmem_limit_bytes=56 * 2**20),
        cost_estimate=pl.CostEstimate(
            flops=2 * 2 * 4 * rows * width * tokens,
            bytes_accessed=2 * (2 * tokens * (8 * rows + width) + 4 * rows * width),
            transcendentals=0,
        ),
        name="outer_blocks",
    )(places, *[dy for pair in dy_pairs for dy in pair], *[x for pair in x_pairs for x in pair])


def cut_kernel(seq, z_ref, *refs):
    term_refs, out_refs, held = refs[: -seq - 1], refs[-seq - 1 : -1], refs[-1]
    at_z = z_ref[0]
    rows, width = term_refs[0].shape
    part = width // seq

    def chunk(i, _):
        at = pl.ds(pl.multiple_of(i * 16, 16), 16)
        total = term_refs[0][at, :]
        if len(term_refs) > 1:
            total = sum(ref[at, :].astype(f32) for ref in term_refs).astype(bf16)
        for j in range(seq):
            held[j, at, :] = total[:, j * part : (j + 1) * part]
        return 0

    lax.fori_loop(0, rows // 16, chunk, 0)
    for step in range(seq):
        out_refs[step][...] = held[lax.rem(at_z + step, seq)]


def cut_sum(at_z, seq, *terms):
    rows, width = terms[0].shape
    return pl.pallas_call(
        functools.partial(cut_kernel, seq),
        in_specs=[pl.BlockSpec(memory_space=pltpu.SMEM)]
        + [pl.BlockSpec(memory_space=pltpu.VMEM)] * len(terms),
        out_specs=[pl.BlockSpec(memory_space=pltpu.VMEM)] * seq,
        out_shape=[jax.ShapeDtypeStruct((rows, width // seq), bf16)] * seq,
        scratch_shapes=[pltpu.VMEM((seq, rows, width // seq), bf16)],
        compiler_params=pltpu.CompilerParams(vmem_limit_bytes=32 * 2**20),
        cost_estimate=pl.CostEstimate(
            flops=2 * rows * width, bytes_accessed=8 * rows * width, transcendentals=0
        ),
        name="cut_sum",
    )(at_z.reshape(1), *terms)


def join_kernel(seq, z_ref, *refs):
    part_refs, out_ref, held = refs[:seq], refs[seq], refs[seq + 1]
    at_z = z_ref[0]
    rows, width = out_ref.shape
    for step in range(seq):
        held[lax.rem(at_z + seq - step, seq)] = part_refs[step][...]

    def chunk(i, _):
        at = pl.ds(pl.multiple_of(i * 16, 16), 16)
        out_ref[at, :] = jnp.concatenate([held[j, at, :] for j in range(seq)], axis=1)
        return 0

    lax.fori_loop(0, rows // 16, chunk, 0)


def join_parts(at_z, parts):
    seq = len(parts)
    rows, part = parts[0].shape
    return pl.pallas_call(
        functools.partial(join_kernel, seq),
        in_specs=[pl.BlockSpec(memory_space=pltpu.SMEM)]
        + [pl.BlockSpec(memory_space=pltpu.VMEM)] * seq,
        out_specs=pl.BlockSpec(memory_space=pltpu.VMEM),
        out_shape=jax.ShapeDtypeStruct((rows, seq * part), bf16),
        scratch_shapes=[pltpu.VMEM((seq, rows, part), bf16)],
        compiler_params=pltpu.CompilerParams(vmem_limit_bytes=32 * 2**20),
        cost_estimate=pl.CostEstimate(
            flops=0, bytes_accessed=4 * seq * rows * part, transcendentals=0
        ),
        name="join_parts",
    )(at_z.reshape(1), *parts)


def join_gathered_kernel(gathered_ref, out_ref):
    seq = gathered_ref.shape[0]

    def chunk(i, _):
        at = pl.ds(pl.multiple_of(i * 16, 16), 16)
        out_ref[at, :] = jnp.concatenate([gathered_ref[j, at, :] for j in range(seq)], axis=1)
        return 0

    lax.fori_loop(0, out_ref.shape[0] // 16, chunk, 0)


def join_gathered(gathered):
    seq, rows, part = gathered.shape
    return pl.pallas_call(
        join_gathered_kernel,
        in_specs=[pl.BlockSpec(memory_space=pltpu.VMEM)],
        out_specs=pl.BlockSpec(memory_space=pltpu.VMEM),
        out_shape=jax.ShapeDtypeStruct((rows, seq * part), bf16),
        compiler_params=pltpu.CompilerParams(vmem_limit_bytes=32 * 2**20),
        cost_estimate=pl.CostEstimate(
            flops=0, bytes_accessed=4 * seq * rows * part, transcendentals=0
        ),
        name="join_gathered",
    )(gathered)


def stack_kernel(counts, *refs):
    term_refs, out_ref = refs[:-1], refs[-1]
    seq, _, part = out_ref.shape
    top = 0
    first = 0
    for count in counts:
        group = term_refs[first : first + count]
        rows = group[0].shape[0]

        def chunk(i, _, group=group, top=top):
            at = pl.ds(pl.multiple_of(i * 16, 16), 16)
            total = group[0][at, :]
            if len(group) > 1:
                total = sum(ref[at, :].astype(f32) for ref in group).astype(bf16)
            to = pl.ds(pl.multiple_of(top + i * 16, 16), 16)
            for j in range(seq):
                out_ref[j, to, :] = total[:, j * part : (j + 1) * part]
            return 0

        lax.fori_loop(0, rows // 16, chunk, 0)
        top += rows
        first += count


def stack_sum(seq, *groups):
    terms = [term for group in groups for term in group]
    rows, width = sum(group[0].shape[0] for group in groups), terms[0].shape[1]
    return pl.pallas_call(
        functools.partial(stack_kernel, [len(group) for group in groups]),
        in_specs=[pl.BlockSpec(memory_space=pltpu.VMEM)] * len(terms),
        out_specs=pl.BlockSpec(memory_space=pltpu.VMEM),
        out_shape=jax.ShapeDtypeStruct((seq, rows, width // seq), bf16),
        compiler_params=pltpu.CompilerParams(vmem_limit_bytes=32 * 2**20),
        cost_estimate=pl.CostEstimate(
            flops=2 * rows * width, bytes_accessed=8 * rows * width, transcendentals=0
        ),
        name="stack_sum",
    )(*terms)


def gelu_slope(x):
    scale = math.sqrt(2.0 / math.pi)
    bend = 0.044715
    curve = jnp.tanh(scale * (x + bend * x * x * x))
    return 0.5 * (1.0 + curve) + 0.5 * x * (1.0 - curve * curve) * scale * (1.0 + 3.0 * bend * x * x)


def mlp_up_kernel(up_ref, u_ref, hidden_ref, act_ref):
    hidden = dot(up_ref[...], u_ref[0], NN)
    hidden_ref[0] = hidden
    act_ref[0] = gelu_tanh(hidden).astype(bf16)


def mlp_down_kernel(down_ref, act_ref, out_ref):
    out_ref[0] = dot(down_ref[...], act_ref[0], NN).astype(bf16)


def mlp_back_kernel(down_flip_ref, up_flip_ref, grad_ref, hidden_ref, dh_ref, du_ref):
    grad_act = dot(down_flip_ref[...], grad_ref[0], NN)
    grad_hidden = (grad_act * gelu_slope(hidden_ref[0])).astype(bf16)
    dh_ref[0] = grad_hidden
    du_ref[0] = dot(up_flip_ref[...], grad_hidden, NN).astype(bf16)


def mlp_outer_kernel(a_ref, b_ref, out_ref, total_ref):
    step = pl.program_id(0)

    @pl.when(step == 0)
    def _():
        total_ref[...] = jnp.zeros_like(total_ref)

    total_ref[...] += dot(a_ref[0], b_ref[0], NT)

    @pl.when(step == pl.num_programs(0) - 1)
    def _():
        out_ref[...] = total_ref[...].astype(bf16)


def by_device(shape):
    return pl.BlockSpec((1,) + shape, lambda i: (i, 0, 0))


def kept(shape):
    return pl.BlockSpec(shape, lambda i: (0, 0))


def mlp_call(kernel, name, held, streams, outs, whole=None):
    count, _, tokens = streams[0].shape
    params = pltpu.CompilerParams(vmem_limit_bytes=48 * 2**20)
    flops = 2 * count * tokens * sum(x.shape[0] * x.shape[1] for x in held)
    moved = sum(x.size * 2 for x in streams) + sum(count * r * tokens * 3 for r, _ in outs)
    if whole:
        flops = 2 * count * tokens * whole[0] * whole[1]
        out_specs, out_shape = kept(whole), jax.ShapeDtypeStruct(whole, bf16)
        scratch = [pltpu.VMEM(whole, f32)]
    else:
        out_specs = [by_device((rows, tokens)) for rows, _ in outs]
        out_shape = [jax.ShapeDtypeStruct((count, rows, tokens), kind) for rows, kind in outs]
        scratch = []
    return pl.pallas_call(
        kernel,
        grid=(count,),
        in_specs=[kept(x.shape) for x in held] + [by_device(x.shape[1:]) for x in streams],
        out_specs=out_specs,
        out_shape=out_shape,
        scratch_shapes=scratch,
        compiler_params=params,
        cost_estimate=pl.CostEstimate(flops=flops, bytes_accessed=moved, transcendentals=0),
        name=name,
    )(*held, *streams)


def join_two_kernel(gathered_ref, first_ref, second_ref):
    seq = gathered_ref.shape[0]
    top = 0
    for out_ref in (first_ref, second_ref):
        rows, part = out_ref.shape[0], out_ref.shape[1] // seq

        def chunk(i, _, top=top, part=part, out_ref=out_ref):
            at = pl.ds(pl.multiple_of(i * 16, 16), 16)
            source = pl.ds(pl.multiple_of(top + i * 16, 16), 16)
            out_ref[at, :] = jnp.concatenate(
                [gathered_ref[j, source, :part] for j in range(seq)], axis=1
            )
            return 0

        lax.fori_loop(0, rows // 16, chunk, 0)
        top += rows


def join_two(gathered, first, second):
    seq = gathered.shape[0]
    shapes = [(rows, seq * part) for rows, part in (first, second)]
    return pl.pallas_call(
        join_two_kernel,
        in_specs=[pl.BlockSpec(memory_space=pltpu.VMEM)],
        out_specs=[pl.BlockSpec(memory_space=pltpu.VMEM)] * 2,
        out_shape=[jax.ShapeDtypeStruct(shape, bf16) for shape in shapes],
        compiler_params=pltpu.CompilerParams(vmem_limit_bytes=32 * 2**20),
        cost_estimate=pl.CostEstimate(
            flops=0, bytes_accessed=4 * gathered.size, transcendentals=0
        ),
        name="join_two",
    )(gathered)


def unpack_kernel(wide, tall, packed_ref, up_ref, down_ref):
    seq = packed_ref.shape[0]
    up_rows, down_rows = tall
    slabs = (packed_ref.shape[1] - up_rows) // down_rows

    def chunk(i, _):
        at = pl.ds(pl.multiple_of(i * 16, 16), 16)
        up_ref[at, :] = jnp.concatenate([packed_ref[z, at, :wide] for z in range(seq)], axis=1)
        return 0

    lax.fori_loop(0, up_rows // 16, chunk, 0)
    lanes = packed_ref.shape[2]
    for z in range(seq):
        for slab in range(slabs):
            left = (z * slabs + slab) * lanes
            top = up_rows + slab * down_rows
            down_ref[:, left : left + lanes] = packed_ref[z, top : top + down_rows, :]


def unpack(packed, seq, wide, tall):
    devices, rows, lanes = packed.shape
    blocks = devices // seq
    up_rows, down_rows = tall
    down_width = seq * lanes * ((rows - up_rows) // down_rows)
    return pl.pallas_call(
        functools.partial(unpack_kernel, wide, tall),
        grid=(blocks,),
        in_specs=[pl.BlockSpec((seq, rows, lanes), lambda p: (p, 0, 0))],
        out_specs=[
            pl.BlockSpec((up_rows, seq * wide), lambda p: (p, 0)),
            pl.BlockSpec((down_rows, down_width), lambda p: (p, 0)),
        ],
        out_shape=[
            jax.ShapeDtypeStruct((blocks * up_rows, seq * wide), bf16),
            jax.ShapeDtypeStruct((blocks * down_rows, down_width), bf16),
        ],
        compiler_params=pltpu.CompilerParams(vmem_limit_bytes=40 * 2**20),
        cost_estimate=pl.CostEstimate(
            flops=0, bytes_accessed=4 * devices * rows * lanes, transcendentals=0
        ),
        name="unpack",
    )(packed)


def pack_kernel(up_ref, down_ref, out_ref):
    seq, _, lanes = out_ref.shape
    up_rows, up_width = up_ref.shape
    part = up_width // seq
    down_rows, down_width = down_ref.shape
    block = down_rows // seq

    def chunk(i, _):
        at = pl.ds(pl.multiple_of(i * 16, 16), 16)
        rows = up_ref[at, :]
        fill = jnp.zeros((16, lanes - part), rows.dtype)
        for z in range(seq):
            out_ref[z, at, :] = jnp.concatenate(
                [rows[:, z * part : (z + 1) * part], fill], axis=1
            )
        return 0

    lax.fori_loop(0, up_rows // 16, chunk, 0)
    for z in range(seq):
        for slab in range(down_width // lanes):
            top = up_rows + slab * block
            out_ref[z, top : top + block, :] = down_ref[
                z * block : (z + 1) * block, slab * lanes : (slab + 1) * lanes
            ]


def pack(up_grad, down_grad, seq, lanes):
    rows = up_grad.shape[0] + down_grad.shape[0] // seq * (down_grad.shape[1] // lanes)
    return pl.pallas_call(
        pack_kernel,
        in_specs=[pl.BlockSpec(memory_space=pltpu.VMEM)] * 2,
        out_specs=pl.BlockSpec(memory_space=pltpu.VMEM),
        out_shape=jax.ShapeDtypeStruct((seq, rows, lanes), bf16),
        compiler_params=pltpu.CompilerParams(vmem_limit_bytes=32 * 2**20),
        cost_estimate=pl.CostEstimate(
            flops=0, bytes_accessed=4 * seq * rows * lanes, transcendentals=0
        ),
        name="pack",
    )(up_grad, down_grad)


def after(value, *others):
    return lax.optimization_barrier((value,) + others)[0]


SWAP = ((0, 1), (1, 0))


def swap(values, axis):
    return lax.ppermute(values, axis, SWAP)


def on_device(
    sizes,
    inputs,
    skipped,
    text_rows,
    condition,
    cotangent,
    norm_gains,
    skip_weight,
    shift_weight,
    query_key_weight,
    value_weight,
    self_output,
    cross_query,
    cross_memory,
    cross_output,
    up_weight,
    down_weight,
):
    outer, inner, cores, seq = sizes
    plane = outer * inner
    square = outer == 2 and inner == 2
    lat_count, local_rows, width = inputs.shape
    text_local = text_rows.shape[1]
    at_a = lax.axis_index("a")
    at_b = lax.axis_index("b")
    at_c = lax.axis_index("c")
    at_z = lax.axis_index("z")
    tokens = lat_count * local_rows

    def route(step):
        return [
            (
                core * seq + z,
                (z // lat_count) * seq + core * lat_count + (z % lat_count + step) % lat_count,
            )
            for core in range(cores)
            for z in range(seq)
        ]

    slot = at_z % lat_count

    def to_latent(values):
        parts = []
        for step in range(lat_count):
            chosen = lax.dynamic_index_in_dim(
                values, (slot + step) % lat_count, 0, keepdims=False
            )
            parts.append(lax.ppermute(chosen, ("c", "z"), route(step)))
        return jnp.concatenate(parts, axis=0)

    def from_latent(rows, *others):
        height = rows.shape[0] // lat_count
        parts = []
        for step in range(lat_count):
            back = [(target, source) for source, target in route(step)]
            parts.append(
                lax.ppermute(rows[step * height : (step + 1) * height], ("c", "z"), back)
            )
        parts = [after(part, *others) for part in parts]
        stacked = jnp.stack(parts + parts)
        return lax.dynamic_slice_in_dim(stacked, (lat_count - slot) % lat_count, lat_count, 0)

    places = jnp.stack(
        [
            ((at_a + da) % outer * inner + (at_b + db) % inner) * cores + (at_c + dc) % cores
            for dc in range(2)
            for da in range(2)
            for db in range(2)
        ]
    ).astype(jnp.int32)
    here = {"a": at_a, "b": at_b, "c": at_c}

    def z_shift(values, step):
        return lax.ppermute(values, "z", [(z, (z + step) % seq) for z in range(seq)])

    def z_send(values):
        return [values] + [z_shift(values, step) for step in range(1, seq)]

    def z_order(arrived):
        blocks = []
        for z in range(seq):
            block = arrived[0]
            for step in range(1, seq):
                block = jnp.where(at_z == (z + step) % seq, arrived[step], block)
            blocks.append(block)
        return blocks

    def z_piece(arrived, *others):
        arrived = [after(part, *others) for part in arrived]
        if square:
            return join_parts(at_z, arrived)
        return jnp.concatenate(z_order(arrived), axis=1)

    def flip(shards):
        return jnp.concatenate([shard.T for shard in shards], axis=0)

    def gather_rows(values, axes):
        if not square:
            return lax.all_gather(values, axes[::-1], axis=0, tiled=True)
        for axis in axes:
            other = swap(values, axis)
            lower = here[axis] == 0
            values = jnp.concatenate(
                [jnp.where(lower, values, other), jnp.where(lower, other, values)], axis=0
            )
        return values

    def to_rank(values, rank):
        axes = tuple(axis for axis, bit in (("c", 4), ("a", 2), ("b", 1)) if rank & bit)
        axes = tuple(axis for axis in ("a", "b", "c") if axis in axes)
        last = 2 ** len(axes) - 1
        return lax.ppermute(values, axes, [(i, last - i) for i in range(last + 1)])

    def exchange(blocks):
        return [blocks[0]] + [to_rank(blocks[rank], rank) for rank in range(1, 8)]

    def stack_by_device(blocks):
        rows = blocks[0].shape[0]
        layout = tuple((rank, 0, rows) for rank in range(8))
        return assemble(tuple(blocks), layout, [rows], places)[0]

    def hop_one(piece):
        return swap(piece, "b"), swap(piece, "a")

    def halves(over_b, over_a):
        half = over_b.shape[0] // 32 * 16
        return over_b[:half], over_a[half:]

    def hop_two(low, high):
        return swap(low, "a"), swap(high, "b")

    def after_all(parts, *others):
        return tuple(lax.optimization_barrier(tuple(parts) + others)[: len(parts)])

    def to_core(parts):
        return tuple(swap(part, "c") for part in parts)

    def whole_of(mine, others, shards):
        rows = mine[0].shape[0]
        half = mine[3].shape[0]
        spans = ((0, 0, rows), (1, 0, rows), (2, 0, rows), (3, 0, half), (3, half, rows))
        layout = spans + tuple((rank + 4, begin, end) for rank, begin, end in spans)
        return assemble(mine + others, layout, [shard.shape[1] for shard in shards], places)

    def gather_plain(piece, shards):
        heights = [shard.shape[1] for shard in shards]
        starts = [sum(heights[:i]) for i in range(len(heights))]
        return [
            lax.all_gather(piece[s : s + h], ("a", "b", "c"), axis=0, tiled=True)
            for s, h in zip(starts, heights)
        ]

    in_order = jnp.arange(4, dtype=jnp.int32) * cores + at_c

    def outer_of(*groups, split=True):
        if square:
            return outer_blocks(
                places[:4] if split else in_order, groups, plane * cores, split
            )
        outs = []
        for x_pair, dy_pairs in groups:
            for dy_pair in dy_pairs:
                total = 0.0
                for dy, x in zip(dy_pair, x_pair):
                    cube = dy.reshape(plane, cores, -1, dy.shape[1])
                    mine = lax.dynamic_index_in_dim(cube, at_c, 1, keepdims=False)
                    total = total + dot(mine.reshape(-1, dy.shape[1]), x, NT)
                cube = total.astype(bf16).reshape(plane, -1, x_pair[0].shape[0])
                outs.append(
                    lax.psum_scatter(cube, ("a", "b"), scatter_dimension=0, tiled=True)[0]
                )
        return (jnp.concatenate(outs, axis=0),)

    def sum_far(state):
        low, high, over_a, over_b, own = state
        return swap(low, "b"), swap(high, "a"), over_a, over_b, own

    def sum_near(state, *others):
        low, high, over_a, over_b, own = state
        half = low.shape[0]
        low = after(low, *others)
        over_a = lax.dynamic_update_slice(over_a, over_a[:half] + low, (0, 0))
        over_b = lax.dynamic_update_slice(over_b, over_b[half:] + high, (half, 0))
        return own, swap(over_a, "a"), swap(over_b, "b"), (over_a, over_b)

    def sum_z(state, *others):
        own, got_a, got_b, _ = state
        parts = cut_sum(at_z, seq, own, after(got_a, *others), got_b)
        return [parts[0]] + [z_shift(parts[step], step) for step in range(1, seq)]

    def sum_three(state, *others):
        own, got_a, got_b, _ = state
        return (own.astype(f32) + after(got_a, *others).astype(f32) + got_b.astype(f32)).astype(bf16)

    def sum_plain(state):
        (total,) = state
        cut = total.reshape(total.shape[0], seq, -1).transpose(1, 0, 2)
        return [
            z_shift(lax.dynamic_index_in_dim(cut, (at_z + step) % seq, 0, keepdims=False), step)
            for step in range(seq)
        ]

    def sum_end(parts, shards, *others):
        owned = sum(after(part, *others).astype(f32) for part in parts)
        results = []
        start = 0
        for shard in shards:
            results.append(owned[start : start + shard.shape[1]].T)
            start += shard.shape[1]
        return results

    gain_skip = norm_gains[: 2 * width]
    gain_one = norm_gains[2 * width : 3 * width]
    gain_two = norm_gains[3 * width : 4 * width]
    gain_three = norm_gains[4 * width :]

    skip_set = [skip_weight]
    pair_set = [query_key_weight, value_weight, shift_weight]
    self_set = [self_output, cross_query, cross_output]
    memory_set = [cross_memory]
    up_set = [up_weight]
    down_set = [down_weight]
    skip_flip, pair_flip, self_flip, memory_flip, up_flip, down_flip = (
        flip(one) for one in (skip_set, pair_set, self_set, memory_set, up_set, down_set)
    )
    if square:
        skip_sent = z_send(skip_flip)
        lanes = down_weight.shape[0] // seq
        cross_flip = jnp.concatenate(
            [
                jnp.pad(one, ((0, 0), (0, lanes - one.shape[1])))
                for one in (self_flip, memory_flip)
            ],
            axis=0,
        )
        cross_flip = after(cross_flip, pair_flip)
        up_padded = jnp.pad(up_flip, ((0, 0), (0, lanes - up_flip.shape[1])))
        slabs = [down_flip[:, i * lanes : (i + 1) * lanes] for i in range(seq)]
        mlp_flip = jnp.concatenate([up_padded] + slabs, axis=0)
        pair_sent = lax.all_gather(pair_flip, "z", axis=0, tiled=False)
        cross_sent = lax.all_gather(cross_flip, "z", axis=0, tiled=False)
        skip_piece = z_piece(skip_sent)
        skip_near = hop_one(skip_piece)
        skip_half = halves(*skip_near)
        skip_far = hop_two(*skip_half)
        pair_piece = join_gathered(after(pair_sent, *skip_half))
        pair_near = hop_one(pair_piece)
        skip_far = after_all(skip_far, pair_piece)
        skip_mine = (skip_piece,) + skip_near + skip_far
        skip_other = to_core(skip_mine)
        (skip_t,) = whole_of(skip_mine, skip_other, skip_set)
        joined = jnp.concatenate(
            [
                inputs.reshape(tokens, width).T,
                skipped.reshape(tokens, width).T,
            ],
            axis=0,
        ).astype(f32)
        level_zero = norm_gain(joined, gain_skip).astype(bf16)
        start_zero = dot(skip_t, level_zero).astype(bf16)
        zero_sent = to_latent(start_zero.T.reshape(inputs.shape))
        pair_near = after_all(pair_near, start_zero)
        pair_half = halves(*pair_near)
        pair_far = hop_two(*pair_half)
        self_piece, memory_piece = join_two(
            after(cross_sent, *pair_half), self_flip.shape, memory_flip.shape
        )
        pair_far = after_all(pair_far, self_piece)
        pair_mine = (pair_piece,) + pair_near + pair_far
        pair_other = to_core(pair_mine)
        self_near = hop_one(self_piece)
        memory_near = hop_one(memory_piece)
        stream_zero = after(zero_sent, *pair_far).T.astype(f32)
        mlp_sent = lax.all_gather(after(mlp_flip, zero_sent), "z", axis=0, tiled=False)
        pair_t, value_t, shift_t = whole_of(pair_mine, pair_other, pair_set)
    else:
        chip_both = to_latent(jnp.concatenate([inputs, skipped], axis=-1))
        joined = chip_both.T.astype(f32)
        level_zero = norm_gain(joined, gain_skip).astype(bf16)
        chip_text = to_latent(text_rows).T
        chip_grad = to_latent(cotangent).T
        (skip_t,) = gather_plain(z_piece(z_send(skip_flip)), skip_set)
        pair_t, value_t, shift_t = gather_plain(z_piece(z_send(pair_flip)), pair_set)
        self_t, cq_t, cout_t = gather_plain(z_piece(z_send(self_flip)), self_set)
        (memory_t,) = gather_plain(z_piece(z_send(memory_flip)), memory_set)
        (up_t,) = gather_plain(z_piece(z_send(up_flip)), up_set)
        (down_t,) = gather_plain(z_piece(z_send(down_flip)), down_set)
        stream_zero = dot(skip_t, level_zero)

    quarter = HD // 4
    frequency = jnp.power(10000.0, -jnp.arange(quarter, dtype=f32) / quarter)
    position = jnp.concatenate(
        [
            (at_c * lat_count + (slot - step) % lat_count) * local_rows
            + jnp.arange(local_rows, dtype=jnp.int32)
            for step in range(lat_count)
        ]
    )
    row_angle = (position // GRID).astype(f32)[None, :] * frequency[:, None]
    col_angle = (position % GRID).astype(f32)[None, :] * frequency[:, None]
    tables = (jnp.cos(row_angle), jnp.sin(row_angle), jnp.cos(col_angle), jnp.sin(col_angle))

    def prepare(flat):
        cube = flat.reshape(H, HD, flat.shape[-1])
        return rotate(normalize(cube, 1), tables).reshape(flat.shape)

    cond_pair = (condition, swap(condition, "c"))
    same_core = at_z // lat_count == at_c
    cond_two = jnp.where(same_core, cond_pair[0], cond_pair[1])
    chip_cond = lax.dynamic_index_in_dim(cond_two, slot, 0, keepdims=False)
    shift = dot(shift_t, jax.nn.silu(chip_cond.astype(f32)).astype(bf16)[:, None], NN)[:, 0]

    level_one = shifted_norm(stream_zero, gain_one, shift).astype(bf16)
    pair_proj = dot(pair_t, level_one)
    value_proj = dot(value_t, level_one).astype(bf16)
    query_flat = pair_proj[:width]
    key_flat = pair_proj[width:]
    query = prepare(query_flat).astype(bf16)
    key = prepare(key_flat).astype(bf16)
    keys = [key, swap(key, "c")]
    values = [value_proj, swap(value_proj, "c")]
    query_next = query
    if square:
        self_near = after_all(self_near, query)
        self_half = halves(*self_near)
        self_far = hop_two(*self_half)
        query_next = after(query, *self_half)
    attended, self_inverse = attend(query_next, keys, values)
    attended_next = attended
    if square:
        all_plane = ("a", "b", "c")
        up_piece, down_piece = unpack(
            after(mlp_sent, attended),
            seq,
            up_flip.shape[1],
            (up_flip.shape[0], down_flip.shape[0]),
        )
        slice_rows = up_weight.shape[1]
        down_blocks = [
            lax.dynamic_slice_in_dim(down_piece, places[rank] * slice_rows, slice_rows, 1)
            for rank in range(8)
        ]
        text_padded = jnp.pad(text_rows, ((0, 0), (0, 0), (0, width - text_rows.shape[2])))
        mixed = to_latent(after(jnp.concatenate([cotangent, text_padded], axis=1), query))
        mixed = mixed.reshape(lat_count, -1, width)
        attended_next = after(attended, up_piece)
        down_sent = exchange(down_blocks)
        memory_near = after_all(memory_near, attended)
        memory_half = halves(*memory_near)
        memory_far = hop_two(*memory_half)
        self_far = after_all(self_far, *memory_half)
        self_mine = (self_piece,) + self_near + self_far
        self_other = to_core(self_mine)
        memory_far = after_all(memory_far, *self_far)
        memory_mine = (memory_piece,) + memory_near + memory_far
        memory_other = to_core(memory_mine)
        self_t, cq_t, cout_t = whole_of(self_mine, self_other, self_set)
        (memory_t,) = whole_of(memory_mine, memory_other, memory_set)
        mixed = after(mixed, *memory_far)
        chip_text = mixed[:, local_rows:, : text_rows.shape[2]].reshape(-1, text_rows.shape[2]).T
    stream_one = stream_zero + dot(self_t, attended_next)
    level_two = norm_gain(stream_one, gain_two).astype(bf16)
    cross_proj = dot(cq_t, level_two)
    cross = head_norm(cross_proj).astype(bf16)
    memory_proj = dot(memory_t, chip_text)
    memory_key_flat = memory_proj[:width]
    memory_key = head_norm(memory_key_flat).astype(bf16)
    memory_value = memory_proj[width:].astype(bf16)
    text_keys = [memory_key, swap(memory_key, "c")]
    text_values = [memory_value, swap(memory_value, "c")]
    cross_next = cross
    if square:
        chip_grad = mixed[:, :local_rows].reshape(-1, width).T
        grad_all = lax.all_gather(chip_grad, all_plane, axis=0, tiled=False)
        cross_next = after(cross, chip_grad)
    crossed, cross_inverse = attend(cross_next, text_keys, text_values)
    stream_two = stream_one + dot(cout_t, crossed)
    level_three = norm_gain(stream_two, gain_three).astype(bf16)
    def with_other(values):
        return values, swap(values, "c")

    one_pair = with_other(level_one)
    attended_pair = with_other(attended)
    two_pair = with_other(level_two)
    text_pair = with_other(chip_text)
    crossed_pair = with_other(crossed)
    if square:
        zero_pair = with_other(level_zero)
        swapped = [
            pair[1]
            for pair in (one_pair, attended_pair, two_pair, text_pair, crossed_pair, zero_pair)
        ]
        up_slice = after(up_piece, *swapped)
        three_all = lax.all_gather(
            after(level_three, grad_all), all_plane, axis=0, tiled=False
        )
        down_slice = stack_by_device([after(part, level_three) for part in down_sent])
        hidden, activated = mlp_call(
            mlp_up_kernel,
            "mlp_up",
            [up_slice],
            [three_all],
            [(slice_rows, f32), (slice_rows, bf16)],
        )
    else:
        hidden = dot(up_t, level_three)
        activated = gelu_tanh(hidden).astype(bf16)

    if square:
        grad_hidden, part = mlp_call(
            mlp_back_kernel,
            "mlp_back",
            [down_slice.T, up_slice.T],
            [grad_all, hidden],
            [(slice_rows, bf16), (width, bf16)],
        )
        grad_level_three = lax.psum_scatter(part, all_plane, scatter_dimension=0, tiled=True)[0]
        down_grad = mlp_call(
            mlp_outer_kernel,
            "mlp_outer",
            [],
            [after(grad_all, part), activated],
            [],
            (width, slice_rows),
        )
        down_parts = exchange(
            [
                lax.dynamic_slice_in_dim(
                    down_grad, places[rank] * (width // 8), width // 8, 0
                )
                for rank in range(8)
            ]
        )
        up_grad = mlp_call(
            mlp_outer_kernel,
            "mlp_outer",
            [],
            [after(grad_hidden, down_grad), three_all],
            [],
            (slice_rows, width),
        )
        (out_part,) = mlp_call(
            mlp_down_kernel,
            "mlp_down",
            [down_slice],
            [after(activated, up_grad)],
            [(width, bf16)],
        )
        down_whole = stack_by_device([after(part, out_part) for part in down_parts])
        mlp_cut = pack(up_grad, down_whole, seq, lanes)
        grad_level_three = after(grad_level_three, mlp_cut).astype(f32)
    else:
        grad_act = dot(down_t, chip_grad, TN)
        _, gelu_pull = jax.vjp(gelu_tanh, hidden)
        grad_hidden = gelu_pull(grad_act)[0].astype(bf16)
        down_outer = outer_of((with_other(activated), [with_other(chip_grad)]))
        up_outer = outer_of((with_other(level_three), [with_other(grad_hidden)]))
        grad_level_three = dot(up_t, grad_hidden, TN)
        zero_pair = with_other(level_zero)
    _, pull_three = jax.vjp(norm_gain, stream_two, gain_three)
    grad_from_three, grad_gain_three = pull_three(grad_level_three)
    grad_stream_two = chip_grad.astype(f32) + grad_from_three
    cross_back = grad_stream_two.astype(bf16)
    grad_crossed = dot(cout_t, cross_back, TN).astype(bf16)
    grad_cross, grad_tk, grad_tv = attend_back(
        cross, grad_crossed, crossed, cross_inverse, text_keys, text_values
    )
    grad_memory_key = grad_tk[0] + swap(grad_tk[1], "c").astype(f32)
    grad_memory_value = grad_tv[0] + swap(grad_tv[1], "c").astype(f32)
    _, pull_memory = jax.vjp(head_norm, memory_key_flat)
    grad_memory_proj = jnp.concatenate(
        [pull_memory(grad_memory_key)[0], grad_memory_value], axis=0
    ).astype(bf16)
    _, pull_cq = jax.vjp(head_norm, cross_proj)
    grad_cq_flat = pull_cq(grad_cross)[0].astype(bf16)
    if square:
        def spread(values):
            cube = values.reshape(seq, -1, values.shape[1])
            cube = jnp.pad(cube, ((0, 0), (0, width // seq - cube.shape[1]), (0, 0)))
            return cube.reshape(width, -1)

        cross_outer = outer_of(
            (crossed_pair, [with_other(cross_back)]),
            (two_pair, [with_other(grad_cq_flat)]),
            (tuple(spread(text) for text in text_pair), [with_other(grad_memory_proj)]),
        )
        cross_sum = sum_far(cross_outer)
    else:
        cross_outer = outer_of(
            (crossed_pair, [with_other(cross_back)]), (two_pair, [with_other(grad_cq_flat)])
        )
        memory_outer = outer_of((text_pair, [with_other(grad_memory_proj)]))
    grad_level_two = dot(cq_t, grad_cq_flat, TN)
    _, pull_two = jax.vjp(norm_gain, stream_one, gain_two)
    grad_from_two, grad_gain_two = pull_two(grad_level_two)
    grad_stream_one = grad_stream_two + grad_from_two
    self_back = grad_stream_one.astype(bf16)
    grad_attended = dot(
        self_t, after(self_back, cross_outer[0]), TN
    ).astype(bf16)
    grad_q, grad_k, grad_v = attend_back(
        query, grad_attended, attended, self_inverse, keys, values
    )
    if square:
        cross_sum = sum_near(cross_sum, grad_q)
        out_sum = lax.psum_scatter(
            after(out_part, grad_level_three), all_plane, scatter_dimension=0, tiled=True
        )[0]
        blended = (stream_two + after(out_sum, grad_q).astype(f32)).astype(bf16)
        mlp_sum = lax.psum_scatter(
            after(mlp_cut, grad_level_three), "z", scatter_dimension=0, tiled=True
        )[0]
        grad_q = after(grad_q, blended, *cross_sum[3])
    grad_key = grad_k[0] + swap(grad_k[1], "c").astype(f32)
    grad_value_proj = (grad_v[0] + swap(grad_v[1], "c").astype(f32)).astype(bf16)
    _, pull_query = jax.vjp(prepare, query_flat)
    _, pull_key = jax.vjp(prepare, key_flat)
    grad_pair_proj = jnp.concatenate([pull_query(grad_q)[0], pull_key(grad_key)[0]], axis=0).astype(
        bf16
    )
    first_outer = outer_of(
        (attended_pair, [with_other(self_back)]),
        (one_pair, [with_other(grad_value_proj), with_other(grad_pair_proj)]),
    )
    if square:
        first_sum = sum_far(first_outer)
        cross_total = sum_three(cross_sum, first_outer[0])
        early = [cross_total, mlp_sum]
    else:
        early = []
        blended = (stream_two + dot(down_t, activated)).astype(bf16)
    grad_text_rows = dot(grad_memory_proj, memory_t, TN).astype(bf16)
    text_width = text_rows.shape[2]
    back = jnp.concatenate(
        [
            blended.T.reshape(lat_count, -1, width),
            jnp.pad(grad_text_rows, ((0, 0), (0, width - text_width))).reshape(
                lat_count, -1, width
            ),
        ],
        axis=1,
    )
    back = from_latent(back.reshape(-1, width), first_outer[0])
    blended_out = back[:, :local_rows]
    grad_text = back[:, local_rows:, :text_width].astype(f32)
    grad_pair_next = after(grad_pair_proj, first_outer[0])
    grad_level_one = dot(pair_t, grad_pair_next, TN) + dot(value_t, grad_value_proj, TN)
    _, pull_one = jax.vjp(shifted_norm, stream_zero, gain_one, shift)
    grad_from_one, grad_gain_one, grad_shift_part = pull_one(grad_level_one)
    skip_back = (grad_stream_one + grad_from_one).astype(bf16)
    if square:
        first_sum = sum_near(first_sum, skip_back)
        skip_sent = after(skip_back, back, *early).T
        skip_back_rows = from_latent(skip_sent, *first_sum[3]).reshape(tokens, width)
        own_back, other_back = with_other(skip_back_rows.T)
        own_sum, got_a, got_b, _ = first_sum
        stacked = stack_sum(
            seq, (cross_total,), (own_sum, after(got_a, skip_back_rows), got_b)
        )
        both_sum = [lax.psum_scatter(stacked, "z", scatter_dimension=0, tiled=True)[0]]
        skip_outer = outer_of((zero_pair, [(after(own_back, stacked), other_back)]))
        skip_sum = sum_far(skip_outer)
        skip_back_rows = after(skip_back_rows, skip_outer[0])
    else:
        skip_outer = outer_of((zero_pair, [with_other(skip_back)]))
        skip_back_rows = from_latent(skip_back.T).reshape(tokens, width)
    grad_level_zero = dot(skip_back_rows, skip_t, NN)
    if square:
        skip_sum = sum_near(skip_sum, grad_level_zero)
        late = skip_sum[3][0]
        up_rows, up_part = up_weight.shape[1], up_weight.shape[0]
        mlp_sum = after(mlp_sum, late).astype(f32)
        grad_up = mlp_sum[:up_rows, :up_part].T
        grad_down = (
            mlp_sum[up_rows:]
            .reshape(slice_rows // lanes, cores, -1, lanes)
            .transpose(1, 0, 3, 2)
            .reshape(cores * slice_rows, -1)
        )
        skip_sum = sum_z(skip_sum, late)
        late = skip_sum[0]
        grad_cout, grad_cq, grad_memory, grad_self, grad_value, grad_pair = sum_end(
            both_sum,
            [
                cross_output,
                cross_query,
                cross_memory,
                self_output,
                value_weight,
                query_key_weight,
            ],
            late,
        )
        grad_memory = grad_memory[: cross_memory.shape[0]]
        (grad_skip_w,) = sum_end(skip_sum, skip_set, grad_pair)
    else:
        (grad_down,) = sum_end(sum_plain(down_outer), down_set)
        (grad_up,) = sum_end(sum_plain(up_outer), up_set)
        grad_cout, grad_cq = sum_end(sum_plain(cross_outer), [cross_output, cross_query])
        (grad_memory,) = sum_end(sum_plain(memory_outer), memory_set)
        grad_self, grad_value, grad_pair = sum_end(
            sum_plain(first_outer), [self_output, value_weight, query_key_weight]
        )
        (grad_skip_w,) = sum_end(sum_plain(skip_outer), skip_set)

    joined_rows = jnp.concatenate([inputs, skipped], axis=-1).astype(f32).reshape(tokens, -1)
    _, pull_zero = jax.vjp(norm_gain_rows, joined_rows, gain_skip)
    grad_joined, grad_gain_skip = pull_zero(grad_level_zero)
    grad_input = grad_joined[:, :width].reshape(inputs.shape)
    grad_skipped = grad_joined[:, width:].reshape(inputs.shape)
    small = jnp.concatenate(
        [grad_shift_part, grad_gain_skip, grad_gain_one, grad_gain_two, grad_gain_three]
    ).reshape(-1, width)
    if square:
        small = jnp.concatenate([after(small, late), condition.astype(f32)], axis=0)
        held = jnp.zeros((8,) + small.shape, f32)
        for rank in range(8):
            arrived = to_rank(small, rank) if rank else small
            held = lax.dynamic_update_slice(held, arrived[None], (places[rank], 0, 0))
        shift_plane = held[:, 0].reshape(plane, cores, width).sum(axis=1)
        gain_plane = sum(held[i, 1:-lat_count] for i in range(8))
        cond_rows = held[:, -lat_count:].reshape(-1, width)
        columns = z_order(z_send(jnp.concatenate([gain_plane, shift_plane], axis=0)))
        gain_rows = len(gain_plane)
        grad_gains = sum(column[:gain_rows] for column in columns).reshape(-1)
        shift_grads = jnp.stack([column[gain_rows:] for column in columns], axis=1)
        shift_grads = shift_grads.reshape(-1, width)
    else:
        cond_rows = gather_rows(condition, ("c", "b", "a")).astype(f32)
        grad_gains = lax.psum(small[1:], ("a", "b", "c", "z")).reshape(-1)
        shift_grads = lax.all_gather(lax.psum(small[:1], "c"), ("a", "b", "z"), axis=0, tiled=True)
    cond_act = jax.nn.silu(cond_rows).astype(bf16)
    block_in, block_out = shift_weight.shape
    cond_block = lax.dynamic_slice_in_dim(cond_act, at_z * block_in, block_in, 1).astype(f32)
    own_columns = ((at_a * inner + at_b) * cores + at_c) * block_out
    grad_shift = jnp.dot(
        cond_block.T,
        lax.dynamic_slice_in_dim(shift_grads, own_columns, block_out, 1),
        precision=lax.Precision.HIGHEST,
    )

    return (
        blended_out,
        grad_input,
        grad_skipped,
        grad_text,
        grad_gains,
        grad_skip_w,
        grad_shift,
        grad_pair,
        grad_value,
        grad_self,
        grad_cq,
        grad_memory,
        grad_cout,
        grad_up,
        grad_down,
    )


def solution(mesh):
    dp, seq = mesh.shape["dp"], mesh.shape["seq"]
    inner, cores = 2, 2
    sizes = (dp // (inner * cores), inner, cores, seq)
    split = Mesh(mesh.devices.reshape(sizes), ("a", "b", "c", "z"))
    rows = P(("a", "b", "c"), "z", None)
    blocks = P("z", ("a", "b", "c"))
    return jax.shard_map(
        functools.partial(on_device, sizes),
        mesh=split,
        in_specs=(rows, rows, rows, P(("a", "b", "c"), None), rows, P()) + (blocks,) * 10,
        out_specs=(rows, rows, rows, rows, P()) + (blocks,) * 10,
        check_vma=False,
    )
```

```python
import functools
import math

import jax
import jax.numpy as jnp
from jax import lax
from jax.experimental import pallas as pl
from jax.experimental.pallas import tpu as pltpu
from jax.sharding import Mesh
from jax.sharding import PartitionSpec as P

H = 16
HD = 88
GRID = 32
PAIR = 2 * HD

epsilon = 1e-06
SCALE = HD ** (-0.5)
SCALE_LOG2 = SCALE * math.log2(math.e)

f32 = jnp.float32
bf16 = jnp.bfloat16


def normalize(values, axis):
    center = values - jnp.mean(values, axis=axis, keepdims=True)
    spread = jnp.mean(center * center, axis=axis, keepdims=True)
    return center * lax.rsqrt(spread + epsilon)


def norm_gain(values, gain_vec):
    return normalize(values, 0) * gain_vec[:, None]


def shifted_norm(values, gain_vec, offset):
    return normalize(values, 0) * gain_vec[:, None] + offset[:, None]


def norm_gain_rows(values, gain_vec):
    return normalize(values, -1) * gain_vec


def gelu_tanh(values):
    return jax.nn.gelu(values, approximate=True)


def head_norm(flat):
    return normalize(flat.reshape(H, HD, flat.shape[-1]), 1).reshape(flat.shape)


def rotate(per_head, tables):
    row_cos, row_sin, col_cos, col_sin = tables
    quarter = per_head.shape[1] // 4
    part_one = per_head[:, :quarter]
    part_two = per_head[:, quarter : 2 * quarter]
    part_three = per_head[:, 2 * quarter : 3 * quarter]
    part_four = per_head[:, 3 * quarter :]
    return jnp.concatenate(
        [
            part_one * row_cos - part_two * row_sin,
            part_two * row_cos + part_one * row_sin,
            part_three * col_cos - part_four * col_sin,
            part_four * col_cos + part_three * col_sin,
        ],
        axis=1,
    )


def dot(a, b, dims=((1,), (0,))):
    return lax.dot_general(a, b, (dims, ((), ())), preferred_element_type=f32)


NN = ((1,), (0,))
TN = ((0,), (0,))
NT = ((1,), (1,))


def heads_of(ref):
    pair = ref[...].astype(f32)
    return pair[:HD].astype(bf16), pair[HD:].astype(bf16)


def attend_kernel(blocks, *refs):
    q_ref = refs[0]
    k_refs = refs[1 : 1 + blocks]
    v_refs = refs[1 + blocks : 1 + 2 * blocks]
    o_ref, inv_ref = refs[1 + 2 * blocks :]
    q_heads = heads_of(q_ref)
    k_heads = [heads_of(r) for r in k_refs]
    v_heads = [heads_of(r) for r in v_refs]
    outs = []
    for i in range(2):
        total = None
        summed = None
        for k_pair, v_pair in zip(k_heads, v_heads):
            scores = dot(k_pair[i], q_heads[i], TN)
            probs = jnp.exp2(scores * SCALE_LOG2)
            part_sum = jnp.sum(probs, axis=0, keepdims=True)
            part = dot(v_pair[i], probs.astype(bf16), NN)
            total = part if total is None else total + part
            summed = part_sum if summed is None else summed + part_sum
        inverse = 1.0 / summed
        outs.append(total * inverse)
        inv_ref[0, i : i + 1, :] = inverse
    o_ref[...] = jnp.concatenate(outs, axis=0).astype(bf16)


def attend(query, keys, values):
    blocks = len(keys)
    tokens = query.shape[1]
    per_key = keys[0].shape[1]
    spec_q = pl.BlockSpec((PAIR, tokens), lambda h: (h, 0))
    spec_k = pl.BlockSpec((PAIR, per_key), lambda h: (h, 0))
    return pl.pallas_call(
        functools.partial(attend_kernel, blocks),
        grid=(H // 2,),
        in_specs=[spec_q] + [spec_k] * (2 * blocks),
        out_specs=[spec_q, pl.BlockSpec((1, 2, tokens), lambda h: (h, 0, 0))],
        out_shape=[
            jax.ShapeDtypeStruct((H * HD, tokens), bf16),
            jax.ShapeDtypeStruct((H // 2, 2, tokens), f32),
        ],
        compiler_params=pltpu.CompilerParams(vmem_limit_bytes=48 * 2**20),
        cost_estimate=pl.CostEstimate(
            flops=2 * 2 * H * 128 * tokens * per_key * blocks,
            bytes_accessed=2 * H * HD * (3 * tokens + 2 * per_key * blocks),
            transcendentals=H * tokens * per_key * blocks,
        ),
        name="attend",
    )(query, *keys, *values)


def attend_back_kernel(blocks, *refs):
    q_ref, g_ref, o_ref, inv_ref = refs[:4]
    k_refs = refs[4 : 4 + blocks]
    v_refs = refs[4 + blocks : 4 + 2 * blocks]
    dq_ref = refs[4 + 2 * blocks]
    dk_refs = refs[5 + 2 * blocks : 5 + 3 * blocks]
    dv_refs = refs[5 + 3 * blocks : 5 + 4 * blocks]
    q_heads = heads_of(q_ref)
    g_heads = heads_of(g_ref)
    gated = g_ref[...].astype(f32) * o_ref[...].astype(f32)
    k_heads = [heads_of(r) for r in k_refs]
    v_heads = [heads_of(r) for r in v_refs]
    grad_queries = []
    grad_keys = [[] for _ in range(blocks)]
    grad_values = [[] for _ in range(blocks)]
    for i in range(2):
        row_dot = jnp.sum(gated[i * HD : (i + 1) * HD], axis=0, keepdims=True)
        inverse = inv_ref[0, i : i + 1, :]
        grad_q = None
        for b in range(blocks):
            k_one, v_one = k_heads[b][i], v_heads[b][i]
            scores = dot(k_one, q_heads[i], TN)
            exact = jnp.exp2(scores * SCALE_LOG2) * inverse
            grad_probs = dot(v_one, g_heads[i], TN)
            grad_scores = (exact * (grad_probs - row_dot)).astype(bf16)
            part = dot(k_one, grad_scores, NN)
            grad_q = part if grad_q is None else grad_q + part
            grad_keys[b].append(dot(q_heads[i], grad_scores, NT) * SCALE)
            grad_values[b].append(dot(g_heads[i], exact.astype(bf16), NT))
        grad_queries.append(grad_q * SCALE)
    dq_ref[...] = jnp.concatenate(grad_queries, axis=0)
    for b in range(blocks):
        dk_refs[b][...] = jnp.concatenate(grad_keys[b], axis=0).astype(dk_refs[b].dtype)
        dv_refs[b][...] = jnp.concatenate(grad_values[b], axis=0).astype(dv_refs[b].dtype)


def attend_back(query, grad, out, inverse, keys, values):
    blocks = len(keys)
    tokens = query.shape[1]
    per_key = keys[0].shape[1]
    spec_q = pl.BlockSpec((PAIR, tokens), lambda h: (h, 0))
    spec_k = pl.BlockSpec((PAIR, per_key), lambda h: (h, 0))
    shapes_k = [jax.ShapeDtypeStruct((H * HD, per_key), kind) for kind in (f32, bf16)]
    outs = pl.pallas_call(
        functools.partial(attend_back_kernel, blocks),
        grid=(H // 2,),
        in_specs=[spec_q] * 3
        + [pl.BlockSpec((1, 2, tokens), lambda h: (h, 0, 0))]
        + [spec_k] * (2 * blocks),
        out_specs=[spec_q] + [spec_k] * (2 * blocks),
        out_shape=[jax.ShapeDtypeStruct((H * HD, tokens), f32)] + shapes_k * 2,
        compiler_params=pltpu.CompilerParams(vmem_limit_bytes=56 * 2**20),
        cost_estimate=pl.CostEstimate(
            flops=5 * 2 * H * 128 * tokens * per_key * blocks,
            bytes_accessed=2 * H * HD * (6 * tokens + 6 * per_key * blocks),
            transcendentals=H * tokens * per_key * blocks,
        ),
        name="attend_back",
    )(query, grad, out, inverse, *keys, *values)
    return outs[0], outs[1 : 1 + blocks], outs[1 + blocks :]


def assemble_kernel(heights, layout, *refs):
    count = len(layout)
    place_ref = refs[0]
    pieces = refs[1 : 1 + count]
    wholes = refs[1 + count : 1 + count + len(heights)]
    held = refs[1 + count + len(heights) : -2]
    sem_in, sem_out = refs[-2:]
    loads = [
        pltpu.make_async_copy(piece, room, sem_in.at[i])
        for i, (piece, room) in enumerate(zip(pieces, held))
    ]
    for load in loads:
        load.start()
    stores = []
    for load, room, (rank, low, high) in zip(loads, held, layout):
        load.wait()
        top = 0
        for height, whole in zip(heights, wholes):
            begin, end = max(low, top), min(high, top + height)
            if begin < end:
                row = pl.multiple_of(place_ref[rank] * height, 16) + (begin - top)
                store = pltpu.make_async_copy(
                    room.at[pl.ds(begin - low, end - begin)],
                    whole.at[pl.ds(row, end - begin)],
                    sem_out.at[len(stores)],
                )
                store.start()
                stores.append(store)
            top += height
    for store in stores:
        store.wait()


def assemble(pieces, layout, heights, places):
    width = pieces[0].shape[1]
    total = sum(heights)
    return pl.pallas_call(
        functools.partial(assemble_kernel, heights, layout),
        in_specs=[pl.BlockSpec(memory_space=pltpu.SMEM)]
        + [pl.BlockSpec(memory_space=pl.ANY)] * len(pieces),
        out_specs=[pl.BlockSpec(memory_space=pl.ANY)] * len(heights),
        out_shape=[jax.ShapeDtypeStruct((8 * height, width), bf16) for height in heights],
        scratch_shapes=[pltpu.VMEM(piece.shape, bf16) for piece in pieces]
        + [
            pltpu.SemaphoreType.DMA((len(pieces),)),
            pltpu.SemaphoreType.DMA((len(pieces) * len(heights),)),
        ],
        compiler_params=pltpu.CompilerParams(vmem_limit_bytes=24 * 2**20),
        cost_estimate=pl.CostEstimate(
            flops=0, bytes_accessed=2 * 2 * 8 * total * width, transcendentals=0
        ),
        name="assemble",
    )(places, *pieces)


def outer_kernel(heights, sharing, half, place_ref, *refs):
    count = len(heights)
    outs = 5 if half else 1
    dy_refs = refs[: 2 * count]
    x_refs = refs[2 * count : -outs]
    if half:
        low_ref, high_ref, over_a_ref, over_b_ref, own_ref = refs[-outs:]

    def put(rank, top, block):
        if not half:
            refs[-1][rank, top : top + block.shape[0], :] = block
            return
        if rank < 3:
            (own_ref, over_b_ref, over_a_ref)[rank][top : top + block.shape[0], :] = block
            return
        end = top + block.shape[0]
        if top < half:
            low_ref[top : min(end, half), :] = block[: min(end, half) - top]
        if end > half:
            high_ref[max(top, half) - half : end - half, :] = block[max(top, half) - top :]

    top = 0
    for i, (height, x_index) in enumerate(zip(heights, sharing)):
        step = 4 if height <= 176 else 2 if height <= 352 else 1
        for start in range(0, 4, step):
            total = None
            for core in range(2):
                chosen = [
                    dy_refs[2 * i + core][
                        pl.ds(pl.multiple_of(place_ref[rank] * height, 16), height), :
                    ]
                    for rank in range(start, start + step)
                ]
                lhs = chosen[0] if step == 1 else jnp.concatenate(chosen, axis=0)
                part = dot(lhs, x_refs[2 * x_index + core][...], NT)
                total = part if total is None else total + part
            total = total.astype(bf16)
            for n in range(step):
                put(start + n, top, total[n * height : (n + 1) * height])
        top += height


def outer_blocks(places, groups, blocks, split):
    x_pairs = [x_pair for x_pair, _ in groups]
    dy_pairs = [dy for _, group in groups for dy in group]
    sharing = [i for i, (_, group) in enumerate(groups) for _ in group]
    heights = [dy[0].shape[0] // blocks for dy in dy_pairs]
    rows = sum(heights)
    half = rows // 32 * 16 if split else 0
    tokens = dy_pairs[0][0].shape[1]
    width = x_pairs[0][0].shape[0]
    cut = next(c for c in (1408, 1536, 512, 128) if width % c == 0)
    once = pl.Buffered(1)
    dy_specs = [
        pl.BlockSpec(dy.shape, lambda i, place: (0, 0), pipeline_mode=once)
        for pair in dy_pairs
        for dy in pair
    ]
    x_buffers = {"pipeline_mode": once} if cut == width else {}
    x_specs = [
        pl.BlockSpec((cut, x.shape[1]), lambda i, place: (i, 0), **x_buffers)
        for pair in x_pairs
        for x in pair
    ]
    sizes = (half, rows - half, rows, rows, rows)
    if split:
        out_specs = [pl.BlockSpec((size, cut), lambda i, place: (0, i)) for size in sizes]
        out_shape = [jax.ShapeDtypeStruct((size, width), bf16) for size in sizes]
    else:
        out_specs = [pl.BlockSpec((4, rows, cut), lambda i, place: (0, 0, i))]
        out_shape = [jax.ShapeDtypeStruct((4, rows, width), bf16)]
    return pl.pallas_call(
        functools.partial(outer_kernel, heights, sharing, half),
        grid_spec=pltpu.PrefetchScalarGridSpec(
            num_scalar_prefetch=1,
            grid=(width // cut,),
            in_specs=dy_specs + x_specs,
            out_specs=out_specs,
        ),
        out_shape=out_shape,
        compiler_params=pltpu.CompilerParams(vmem_limit_bytes=56 * 2**20),
        cost_estimate=pl.CostEstimate(
            flops=2 * 2 * 4 * rows * width * tokens,
            bytes_accessed=2 * (2 * tokens * (8 * rows + width) + 4 * rows * width),
            transcendentals=0,
        ),
        name="outer_blocks",
    )(places, *[dy for pair in dy_pairs for dy in pair], *[x for pair in x_pairs for x in pair])


def cut_kernel(seq, z_ref, *refs):
    term_refs, out_refs, held = refs[: -seq - 1], refs[-seq - 1 : -1], refs[-1]
    at_z = z_ref[0]
    rows, width = term_refs[0].shape
    part = width // seq

    def chunk(i, _):
        at = pl.ds(pl.multiple_of(i * 16, 16), 16)
        total = term_refs[0][at, :]
        if len(term_refs) > 1:
            total = sum(ref[at, :].astype(f32) for ref in term_refs).astype(bf16)
        for j in range(seq):
            held[j, at, :] = total[:, j * part : (j + 1) * part]
        return 0

    lax.fori_loop(0, rows // 16, chunk, 0)
    for step in range(seq):
        out_refs[step][...] = held[lax.rem(at_z + step, seq)]


def cut_sum(at_z, seq, *terms):
    rows, width = terms[0].shape
    return pl.pallas_call(
        functools.partial(cut_kernel, seq),
        in_specs=[pl.BlockSpec(memory_space=pltpu.SMEM)]
        + [pl.BlockSpec(memory_space=pltpu.VMEM)] * len(terms),
        out_specs=[pl.BlockSpec(memory_space=pltpu.VMEM)] * seq,
        out_shape=[jax.ShapeDtypeStruct((rows, width // seq), bf16)] * seq,
        scratch_shapes=[pltpu.VMEM((seq, rows, width // seq), bf16)],
        compiler_params=pltpu.CompilerParams(vmem_limit_bytes=32 * 2**20),
        cost_estimate=pl.CostEstimate(
            flops=2 * rows * width, bytes_accessed=8 * rows * width, transcendentals=0
        ),
        name="cut_sum",
    )(at_z.reshape(1), *terms)


def join_kernel(seq, z_ref, *refs):
    part_refs, out_ref, held = refs[:seq], refs[seq], refs[seq + 1]
    at_z = z_ref[0]
    rows, width = out_ref.shape
    for step in range(seq):
        held[lax.rem(at_z + seq - step, seq)] = part_refs[step][...]

    def chunk(i, _):
        at = pl.ds(pl.multiple_of(i * 16, 16), 16)
        out_ref[at, :] = jnp.concatenate([held[j, at, :] for j in range(seq)], axis=1)
        return 0

    lax.fori_loop(0, rows // 16, chunk, 0)


def join_parts(at_z, parts):
    seq = len(parts)
    rows, part = parts[0].shape
    return pl.pallas_call(
        functools.partial(join_kernel, seq),
        in_specs=[pl.BlockSpec(memory_space=pltpu.SMEM)]
        + [pl.BlockSpec(memory_space=pltpu.VMEM)] * seq,
        out_specs=pl.BlockSpec(memory_space=pltpu.VMEM),
        out_shape=jax.ShapeDtypeStruct((rows, seq * part), bf16),
        scratch_shapes=[pltpu.VMEM((seq, rows, part), bf16)],
        compiler_params=pltpu.CompilerParams(vmem_limit_bytes=32 * 2**20),
        cost_estimate=pl.CostEstimate(
            flops=0, bytes_accessed=4 * seq * rows * part, transcendentals=0
        ),
        name="join_parts",
    )(at_z.reshape(1), *parts)


def join_gathered_kernel(gathered_ref, out_ref):
    seq = gathered_ref.shape[0]

    def chunk(i, _):
        at = pl.ds(pl.multiple_of(i * 16, 16), 16)
        out_ref[at, :] = jnp.concatenate([gathered_ref[j, at, :] for j in range(seq)], axis=1)
        return 0

    lax.fori_loop(0, out_ref.shape[0] // 16, chunk, 0)


def join_gathered(gathered):
    seq, rows, part = gathered.shape
    return pl.pallas_call(
        join_gathered_kernel,
        in_specs=[pl.BlockSpec(memory_space=pltpu.VMEM)],
        out_specs=pl.BlockSpec(memory_space=pltpu.VMEM),
        out_shape=jax.ShapeDtypeStruct((rows, seq * part), bf16),
        compiler_params=pltpu.CompilerParams(vmem_limit_bytes=32 * 2**20),
        cost_estimate=pl.CostEstimate(
            flops=0, bytes_accessed=4 * seq * rows * part, transcendentals=0
        ),
        name="join_gathered",
    )(gathered)


def stack_kernel(counts, *refs):
    term_refs, out_ref = refs[:-1], refs[-1]
    seq, _, part = out_ref.shape
    top = 0
    first = 0
    for count in counts:
        group = term_refs[first : first + count]
        rows = group[0].shape[0]

        def chunk(i, _, group=group, top=top):
            at = pl.ds(pl.multiple_of(i * 16, 16), 16)
            total = group[0][at, :]
            if len(group) > 1:
                total = sum(ref[at, :].astype(f32) for ref in group).astype(bf16)
            to = pl.ds(pl.multiple_of(top + i * 16, 16), 16)
            for j in range(seq):
                out_ref[j, to, :] = total[:, j * part : (j + 1) * part]
            return 0

        lax.fori_loop(0, rows // 16, chunk, 0)
        top += rows
        first += count


def stack_sum(seq, *groups):
    terms = [term for group in groups for term in group]
    rows, width = sum(group[0].shape[0] for group in groups), terms[0].shape[1]
    return pl.pallas_call(
        functools.partial(stack_kernel, [len(group) for group in groups]),
        in_specs=[pl.BlockSpec(memory_space=pltpu.VMEM)] * len(terms),
        out_specs=pl.BlockSpec(memory_space=pltpu.VMEM),
        out_shape=jax.ShapeDtypeStruct((seq, rows, width // seq), bf16),
        compiler_params=pltpu.CompilerParams(vmem_limit_bytes=32 * 2**20),
        cost_estimate=pl.CostEstimate(
            flops=2 * rows * width, bytes_accessed=8 * rows * width, transcendentals=0
        ),
        name="stack_sum",
    )(*terms)


def gelu_slope(x):
    scale = math.sqrt(2.0 / math.pi)
    bend = 0.044715
    curve = jnp.tanh(scale * (x + bend * x * x * x))
    return 0.5 * (1.0 + curve) + 0.5 * x * (1.0 - curve * curve) * scale * (1.0 + 3.0 * bend * x * x)


def mlp_up_kernel(up_ref, u_ref, hidden_ref, act_ref):
    hidden = dot(up_ref[...], u_ref[0], NN)
    hidden_ref[0] = hidden
    act_ref[0] = gelu_tanh(hidden).astype(bf16)


def mlp_down_kernel(down_ref, act_ref, out_ref):
    out_ref[0] = dot(down_ref[...], act_ref[0], NN).astype(bf16)


def mlp_back_kernel(down_flip_ref, up_flip_ref, grad_ref, hidden_ref, dh_ref, du_ref):
    grad_act = dot(down_flip_ref[...], grad_ref[0], NN)
    grad_hidden = (grad_act * gelu_slope(hidden_ref[0])).astype(bf16)
    dh_ref[0] = grad_hidden
    du_ref[0] = dot(up_flip_ref[...], grad_hidden, NN).astype(bf16)


def mlp_outer_kernel(a_ref, b_ref, out_ref, total_ref):
    step = pl.program_id(0)

    @pl.when(step == 0)
    def _():
        total_ref[...] = jnp.zeros_like(total_ref)

    total_ref[...] += dot(a_ref[0], b_ref[0], NT)

    @pl.when(step == pl.num_programs(0) - 1)
    def _():
        out_ref[...] = total_ref[...].astype(bf16)


def by_device(shape):
    return pl.BlockSpec((1,) + shape, lambda i: (i, 0, 0))


def kept(shape):
    return pl.BlockSpec(shape, lambda i: (0, 0))


def mlp_call(kernel, name, held, streams, outs, whole=None):
    count, _, tokens = streams[0].shape
    params = pltpu.CompilerParams(vmem_limit_bytes=48 * 2**20)
    flops = 2 * count * tokens * sum(x.shape[0] * x.shape[1] for x in held)
    moved = sum(x.size * 2 for x in streams) + sum(count * r * tokens * 3 for r, _ in outs)
    if whole:
        flops = 2 * count * tokens * whole[0] * whole[1]
        out_specs, out_shape = kept(whole), jax.ShapeDtypeStruct(whole, bf16)
        scratch = [pltpu.VMEM(whole, f32)]
    else:
        out_specs = [by_device((rows, tokens)) for rows, _ in outs]
        out_shape = [jax.ShapeDtypeStruct((count, rows, tokens), kind) for rows, kind in outs]
        scratch = []
    return pl.pallas_call(
        kernel,
        grid=(count,),
        in_specs=[kept(x.shape) for x in held] + [by_device(x.shape[1:]) for x in streams],
        out_specs=out_specs,
        out_shape=out_shape,
        scratch_shapes=scratch,
        compiler_params=params,
        cost_estimate=pl.CostEstimate(flops=flops, bytes_accessed=moved, transcendentals=0),
        name=name,
    )(*held, *streams)


def join_two_kernel(gathered_ref, first_ref, second_ref):
    seq = gathered_ref.shape[0]
    top = 0
    for out_ref in (first_ref, second_ref):
        rows, part = out_ref.shape[0], out_ref.shape[1] // seq

        def chunk(i, _, top=top, part=part, out_ref=out_ref):
            at = pl.ds(pl.multiple_of(i * 16, 16), 16)
            source = pl.ds(pl.multiple_of(top + i * 16, 16), 16)
            out_ref[at, :] = jnp.concatenate(
                [gathered_ref[j, source, :part] for j in range(seq)], axis=1
            )
            return 0

        lax.fori_loop(0, rows // 16, chunk, 0)
        top += rows


def join_two(gathered, first, second):
    seq = gathered.shape[0]
    shapes = [(rows, seq * part) for rows, part in (first, second)]
    return pl.pallas_call(
        join_two_kernel,
        in_specs=[pl.BlockSpec(memory_space=pltpu.VMEM)],
        out_specs=[pl.BlockSpec(memory_space=pltpu.VMEM)] * 2,
        out_shape=[jax.ShapeDtypeStruct(shape, bf16) for shape in shapes],
        compiler_params=pltpu.CompilerParams(vmem_limit_bytes=32 * 2**20),
        cost_estimate=pl.CostEstimate(
            flops=0, bytes_accessed=4 * gathered.size, transcendentals=0
        ),
        name="join_two",
    )(gathered)


def unpack_kernel(wide, tall, packed_ref, up_ref, down_ref):
    seq = packed_ref.shape[0]
    up_rows, down_rows = tall
    slabs = (packed_ref.shape[1] - up_rows) // down_rows

    def chunk(i, _):
        at = pl.ds(pl.multiple_of(i * 16, 16), 16)
        up_ref[at, :] = jnp.concatenate([packed_ref[z, at, :wide] for z in range(seq)], axis=1)
        return 0

    lax.fori_loop(0, up_rows // 16, chunk, 0)
    lanes = packed_ref.shape[2]
    for z in range(seq):
        for slab in range(slabs):
            left = (z * slabs + slab) * lanes
            top = up_rows + slab * down_rows
            down_ref[:, left : left + lanes] = packed_ref[z, top : top + down_rows, :]


def unpack(packed, seq, wide, tall):
    devices, rows, lanes = packed.shape
    blocks = devices // seq
    up_rows, down_rows = tall
    down_width = seq * lanes * ((rows - up_rows) // down_rows)
    return pl.pallas_call(
        functools.partial(unpack_kernel, wide, tall),
        grid=(blocks,),
        in_specs=[pl.BlockSpec((seq, rows, lanes), lambda p: (p, 0, 0))],
        out_specs=[
            pl.BlockSpec((up_rows, seq * wide), lambda p: (p, 0)),
            pl.BlockSpec((down_rows, down_width), lambda p: (p, 0)),
        ],
        out_shape=[
            jax.ShapeDtypeStruct((blocks * up_rows, seq * wide), bf16),
            jax.ShapeDtypeStruct((blocks * down_rows, down_width), bf16),
        ],
        compiler_params=pltpu.CompilerParams(vmem_limit_bytes=40 * 2**20),
        cost_estimate=pl.CostEstimate(
            flops=0, bytes_accessed=4 * devices * rows * lanes, transcendentals=0
        ),
        name="unpack",
    )(packed)


def pack_kernel(up_ref, down_ref, out_ref):
    seq, _, lanes = out_ref.shape
    up_rows, up_width = up_ref.shape
    part = up_width // seq
    down_rows, down_width = down_ref.shape
    block = down_rows // seq

    def chunk(i, _):
        at = pl.ds(pl.multiple_of(i * 16, 16), 16)
        rows = up_ref[at, :]
        fill = jnp.zeros((16, lanes - part), rows.dtype)
        for z in range(seq):
            out_ref[z, at, :] = jnp.concatenate(
                [rows[:, z * part : (z + 1) * part], fill], axis=1
            )
        return 0

    lax.fori_loop(0, up_rows // 16, chunk, 0)
    for z in range(seq):
        for slab in range(down_width // lanes):
            top = up_rows + slab * block
            out_ref[z, top : top + block, :] = down_ref[
                z * block : (z + 1) * block, slab * lanes : (slab + 1) * lanes
            ]


def pack(up_grad, down_grad, seq, lanes):
    rows = up_grad.shape[0] + down_grad.shape[0] // seq * (down_grad.shape[1] // lanes)
    return pl.pallas_call(
        pack_kernel,
        in_specs=[pl.BlockSpec(memory_space=pltpu.VMEM)] * 2,
        out_specs=pl.BlockSpec(memory_space=pltpu.VMEM),
        out_shape=jax.ShapeDtypeStruct((seq, rows, lanes), bf16),
        compiler_params=pltpu.CompilerParams(vmem_limit_bytes=32 * 2**20),
        cost_estimate=pl.CostEstimate(
            flops=0, bytes_accessed=4 * seq * rows * lanes, transcendentals=0
        ),
        name="pack",
    )(up_grad, down_grad)


def after(value, *others):
    return lax.optimization_barrier((value,) + others)[0]


SWAP = ((0, 1), (1, 0))


def swap(values, axis):
    return lax.ppermute(values, axis, SWAP)


def on_device(
    sizes,
    inputs,
    skipped,
    text_rows,
    condition,
    cotangent,
    norm_gains,
    skip_weight,
    shift_weight,
    query_key_weight,
    value_weight,
    self_output,
    cross_query,
    cross_memory,
    cross_output,
    up_weight,
    down_weight,
):
    outer, inner, cores, seq = sizes
    plane = outer * inner
    square = outer == 2 and inner == 2
    lat_count, local_rows, width = inputs.shape
    text_local = text_rows.shape[1]
    at_a = lax.axis_index("a")
    at_b = lax.axis_index("b")
    at_c = lax.axis_index("c")
    at_z = lax.axis_index("z")
    tokens = lat_count * local_rows

    def route(step):
        return [
            (
                core * seq + z,
                (z // lat_count) * seq + core * lat_count + (z % lat_count + step) % lat_count,
            )
            for core in range(cores)
            for z in range(seq)
        ]

    slot = at_z % lat_count

    def to_latent(values):
        parts = []
        for step in range(lat_count):
            chosen = lax.dynamic_index_in_dim(
                values, (slot + step) % lat_count, 0, keepdims=False
            )
            parts.append(lax.ppermute(chosen, ("c", "z"), route(step)))
        return jnp.concatenate(parts, axis=0)

    def from_latent(rows, *others):
        height = rows.shape[0] // lat_count
        parts = []
        for step in range(lat_count):
            back = [(target, source) for source, target in route(step)]
            parts.append(
                lax.ppermute(rows[step * height : (step + 1) * height], ("c", "z"), back)
            )
        parts = [after(part, *others) for part in parts]
        stacked = jnp.stack(parts + parts)
        return lax.dynamic_slice_in_dim(stacked, (lat_count - slot) % lat_count, lat_count, 0)

    places = jnp.stack(
        [
            ((at_a + da) % outer * inner + (at_b + db) % inner) * cores + (at_c + dc) % cores
            for dc in range(2)
            for da in range(2)
            for db in range(2)
        ]
    ).astype(jnp.int32)
    here = {"a": at_a, "b": at_b, "c": at_c}

    def z_shift(values, step):
        return lax.ppermute(values, "z", [(z, (z + step) % seq) for z in range(seq)])

    def z_send(values):
        return [values] + [z_shift(values, step) for step in range(1, seq)]

    def z_order(arrived):
        blocks = []
        for z in range(seq):
            block = arrived[0]
            for step in range(1, seq):
                block = jnp.where(at_z == (z + step) % seq, arrived[step], block)
            blocks.append(block)
        return blocks

    def z_piece(arrived, *others):
        arrived = [after(part, *others) for part in arrived]
        if square:
            return join_parts(at_z, arrived)
        return jnp.concatenate(z_order(arrived), axis=1)

    def flip(shards):
        return jnp.concatenate([shard.T for shard in shards], axis=0)

    def gather_rows(values, axes):
        if not square:
            return lax.all_gather(values, axes[::-1], axis=0, tiled=True)
        for axis in axes:
            other = swap(values, axis)
            lower = here[axis] == 0
            values = jnp.concatenate(
                [jnp.where(lower, values, other), jnp.where(lower, other, values)], axis=0
            )
        return values

    def to_rank(values, rank):
        axes = tuple(axis for axis, bit in (("c", 4), ("a", 2), ("b", 1)) if rank & bit)
        axes = tuple(axis for axis in ("a", "b", "c") if axis in axes)
        last = 2 ** len(axes) - 1
        return lax.ppermute(values, axes, [(i, last - i) for i in range(last + 1)])

    def exchange(blocks):
        return [blocks[0]] + [to_rank(blocks[rank], rank) for rank in range(1, 8)]

    def stack_by_device(blocks):
        rows = blocks[0].shape[0]
        layout = tuple((rank, 0, rows) for rank in range(8))
        return assemble(tuple(blocks), layout, [rows], places)[0]

    def hop_one(piece):
        return swap(piece, "b"), swap(piece, "a")

    def halves(over_b, over_a):
        half = over_b.shape[0] // 32 * 16
        return over_b[:half], over_a[half:]

    def hop_two(low, high):
        return swap(low, "a"), swap(high, "b")

    def after_all(parts, *others):
        return tuple(lax.optimization_barrier(tuple(parts) + others)[: len(parts)])

    def to_core(parts):
        return tuple(swap(part, "c") for part in parts)

    def whole_of(mine, others, shards):
        rows = mine[0].shape[0]
        half = mine[3].shape[0]
        spans = ((0, 0, rows), (1, 0, rows), (2, 0, rows), (3, 0, half), (3, half, rows))
        layout = spans + tuple((rank + 4, begin, end) for rank, begin, end in spans)
        return assemble(mine + others, layout, [shard.shape[1] for shard in shards], places)

    def gather_plain(piece, shards):
        heights = [shard.shape[1] for shard in shards]
        starts = [sum(heights[:i]) for i in range(len(heights))]
        return [
            lax.all_gather(piece[s : s + h], ("a", "b", "c"), axis=0, tiled=True)
            for s, h in zip(starts, heights)
        ]

    in_order = jnp.arange(4, dtype=jnp.int32) * cores + at_c

    def outer_of(*groups, split=True):
        if square:
            return outer_blocks(
                places[:4] if split else in_order, groups, plane * cores, split
            )
        outs = []
        for x_pair, dy_pairs in groups:
            for dy_pair in dy_pairs:
                total = 0.0
                for dy, x in zip(dy_pair, x_pair):
                    cube = dy.reshape(plane, cores, -1, dy.shape[1])
                    mine = lax.dynamic_index_in_dim(cube, at_c, 1, keepdims=False)
                    total = total + dot(mine.reshape(-1, dy.shape[1]), x, NT)
                cube = total.astype(bf16).reshape(plane, -1, x_pair[0].shape[0])
                outs.append(
                    lax.psum_scatter(cube, ("a", "b"), scatter_dimension=0, tiled=True)[0]
                )
        return (jnp.concatenate(outs, axis=0),)

    def sum_far(state):
        low, high, over_a, over_b, own = state
        return swap(low, "b"), swap(high, "a"), over_a, over_b, own

    def sum_near(state, *others):
        low, high, over_a, over_b, own = state
        half = low.shape[0]
        low = after(low, *others)
        over_a = lax.dynamic_update_slice(over_a, over_a[:half] + low, (0, 0))
        over_b = lax.dynamic_update_slice(over_b, over_b[half:] + high, (half, 0))
        return own, swap(over_a, "a"), swap(over_b, "b"), (over_a, over_b)

    def sum_z(state, *others):
        own, got_a, got_b, _ = state
        parts = cut_sum(at_z, seq, own, after(got_a, *others), got_b)
        return [parts[0]] + [z_shift(parts[step], step) for step in range(1, seq)]

    def sum_three(state, *others):
        own, got_a, got_b, _ = state
        return (own.astype(f32) + after(got_a, *others).astype(f32) + got_b.astype(f32)).astype(bf16)

    def sum_plain(state):
        (total,) = state
        cut = total.reshape(total.shape[0], seq, -1).transpose(1, 0, 2)
        return [
            z_shift(lax.dynamic_index_in_dim(cut, (at_z + step) % seq, 0, keepdims=False), step)
            for step in range(seq)
        ]

    def sum_end(parts, shards, *others):
        owned = sum(after(part, *others).astype(f32) for part in parts)
        results = []
        start = 0
        for shard in shards:
            results.append(owned[start : start + shard.shape[1]].T)
            start += shard.shape[1]
        return results

    gain_skip = norm_gains[: 2 * width]
    gain_one = norm_gains[2 * width : 3 * width]
    gain_two = norm_gains[3 * width : 4 * width]
    gain_three = norm_gains[4 * width :]

    skip_set = [skip_weight]
    pair_set = [query_key_weight, value_weight, shift_weight]
    self_set = [self_output, cross_query, cross_output]
    memory_set = [cross_memory]
    up_set = [up_weight]
    down_set = [down_weight]
    skip_flip, pair_flip, self_flip, memory_flip, up_flip, down_flip = (
        flip(one) for one in (skip_set, pair_set, self_set, memory_set, up_set, down_set)
    )
    if square:
        skip_sent = z_send(skip_flip)
        lanes = down_weight.shape[0] // seq
        cross_flip = jnp.concatenate(
            [
                jnp.pad(one, ((0, 0), (0, lanes - one.shape[1])))
                for one in (self_flip, memory_flip)
            ],
            axis=0,
        )
        cross_flip = after(cross_flip, pair_flip)
        up_padded = jnp.pad(up_flip, ((0, 0), (0, lanes - up_flip.shape[1])))
        slabs = [down_flip[:, i * lanes : (i + 1) * lanes] for i in range(seq)]
        mlp_flip = jnp.concatenate([up_padded] + slabs, axis=0)
        pair_sent = lax.all_gather(pair_flip, "z", axis=0, tiled=False)
        cross_sent = lax.all_gather(cross_flip, "z", axis=0, tiled=False)
        skip_piece = z_piece(skip_sent)
        skip_near = hop_one(skip_piece)
        skip_half = halves(*skip_near)
        skip_far = hop_two(*skip_half)
        pair_piece = join_gathered(after(pair_sent, *skip_half))
        pair_near = hop_one(pair_piece)
        skip_far = after_all(skip_far, pair_piece)
        skip_mine = (skip_piece,) + skip_near + skip_far
        skip_other = to_core(skip_mine)
        (skip_t,) = whole_of(skip_mine, skip_other, skip_set)
        joined = jnp.concatenate(
            [
                inputs.reshape(tokens, width).T,
                skipped.reshape(tokens, width).T,
            ],
            axis=0,
        ).astype(f32)
        level_zero = norm_gain(joined, gain_skip).astype(bf16)
        start_zero = dot(skip_t, level_zero).astype(bf16)
        zero_sent = to_latent(start_zero.T.reshape(inputs.shape))
        pair_near = after_all(pair_near, start_zero)
        pair_half = halves(*pair_near)
        pair_far = hop_two(*pair_half)
        self_piece, memory_piece = join_two(
            after(cross_sent, *pair_half), self_flip.shape, memory_flip.shape
        )
        pair_far = after_all(pair_far, self_piece)
        pair_mine = (pair_piece,) + pair_near + pair_far
        pair_other = to_core(pair_mine)
        self_near = hop_one(self_piece)
        memory_near = hop_one(memory_piece)
        stream_zero = after(zero_sent, *pair_far).T.astype(f32)
        mlp_sent = lax.all_gather(after(mlp_flip, zero_sent), "z", axis=0, tiled=False)
        pair_t, value_t, shift_t = whole_of(pair_mine, pair_other, pair_set)
    else:
        chip_both = to_latent(jnp.concatenate([inputs, skipped], axis=-1))
        joined = chip_both.T.astype(f32)
        level_zero = norm_gain(joined, gain_skip).astype(bf16)
        chip_text = to_latent(text_rows).T
        chip_grad = to_latent(cotangent).T
        (skip_t,) = gather_plain(z_piece(z_send(skip_flip)), skip_set)
        pair_t, value_t, shift_t = gather_plain(z_piece(z_send(pair_flip)), pair_set)
        self_t, cq_t, cout_t = gather_plain(z_piece(z_send(self_flip)), self_set)
        (memory_t,) = gather_plain(z_piece(z_send(memory_flip)), memory_set)
        (up_t,) = gather_plain(z_piece(z_send(up_flip)), up_set)
        (down_t,) = gather_plain(z_piece(z_send(down_flip)), down_set)
        stream_zero = dot(skip_t, level_zero)

    quarter = HD // 4
    frequency = jnp.power(10000.0, -jnp.arange(quarter, dtype=f32) / quarter)
    position = jnp.concatenate(
        [
            (at_c * lat_count + (slot - step) % lat_count) * local_rows
            + jnp.arange(local_rows, dtype=jnp.int32)
            for step in range(lat_count)
        ]
    )
    row_angle = (position // GRID).astype(f32)[None, :] * frequency[:, None]
    col_angle = (position % GRID).astype(f32)[None, :] * frequency[:, None]
    tables = (jnp.cos(row_angle), jnp.sin(row_angle), jnp.cos(col_angle), jnp.sin(col_angle))

    def prepare(flat):
        cube = flat.reshape(H, HD, flat.shape[-1])
        return rotate(normalize(cube, 1), tables).reshape(flat.shape)

    cond_pair = (condition, swap(condition, "c"))
    same_core = at_z // lat_count == at_c
    cond_two = jnp.where(same_core, cond_pair[0], cond_pair[1])
    chip_cond = lax.dynamic_index_in_dim(cond_two, slot, 0, keepdims=False)
    shift = dot(shift_t, jax.nn.silu(chip_cond.astype(f32)).astype(bf16)[:, None], NN)[:, 0]

    level_one = shifted_norm(stream_zero, gain_one, shift).astype(bf16)
    pair_proj = dot(pair_t, level_one)
    value_proj = dot(value_t, level_one).astype(bf16)
    query_flat = pair_proj[:width]
    key_flat = pair_proj[width:]
    query = prepare(query_flat).astype(bf16)
    key = prepare(key_flat).astype(bf16)
    keys = [key, swap(key, "c")]
    values = [value_proj, swap(value_proj, "c")]
    query_next = query
    if square:
        self_near = after_all(self_near, query)
        self_half = halves(*self_near)
        self_far = hop_two(*self_half)
        query_next = after(query, *self_half)
    attended, self_inverse = attend(query_next, keys, values)
    attended_next = attended
    if square:
        all_plane = ("a", "b", "c")
        up_piece, down_piece = unpack(
            after(mlp_sent, attended),
            seq,
            up_flip.shape[1],
            (up_flip.shape[0], down_flip.shape[0]),
        )
        slice_rows = up_weight.shape[1]
        down_blocks = [
            lax.dynamic_slice_in_dim(down_piece, places[rank] * slice_rows, slice_rows, 1)
            for rank in range(8)
        ]
        text_padded = jnp.pad(text_rows, ((0, 0), (0, 0), (0, width - text_rows.shape[2])))
        mixed = to_latent(after(jnp.concatenate([cotangent, text_padded], axis=1), query))
        mixed = mixed.reshape(lat_count, -1, width)
        attended_next = after(attended, up_piece)
        down_sent = exchange(down_blocks)
        memory_near = after_all(memory_near, attended)
        memory_half = halves(*memory_near)
        memory_far = hop_two(*memory_half)
        self_far = after_all(self_far, *memory_half)
        self_mine = (self_piece,) + self_near + self_far
        self_other = to_core(self_mine)
        memory_far = after_all(memory_far, *self_far)
        memory_mine = (memory_piece,) + memory_near + memory_far
        memory_other = to_core(memory_mine)
        self_t, cq_t, cout_t = whole_of(self_mine, self_other, self_set)
        (memory_t,) = whole_of(memory_mine, memory_other, memory_set)
        mixed = after(mixed, *memory_far)
        chip_text = mixed[:, local_rows:, : text_rows.shape[2]].reshape(-1, text_rows.shape[2]).T
    stream_one = stream_zero + dot(self_t, attended_next)
    level_two = norm_gain(stream_one, gain_two).astype(bf16)
    cross_proj = dot(cq_t, level_two)
    cross = head_norm(cross_proj).astype(bf16)
    memory_proj = dot(memory_t, chip_text)
    memory_key_flat = memory_proj[:width]
    memory_key = head_norm(memory_key_flat).astype(bf16)
    memory_value = memory_proj[width:].astype(bf16)
    text_keys = [memory_key, swap(memory_key, "c")]
    text_values = [memory_value, swap(memory_value, "c")]
    cross_next = cross
    if square:
        chip_grad = mixed[:, :local_rows].reshape(-1, width).T
        grad_all = lax.all_gather(chip_grad, all_plane, axis=0, tiled=False)
        cross_next = after(cross, chip_grad)
    crossed, cross_inverse = attend(cross_next, text_keys, text_values)
    stream_two = stream_one + dot(cout_t, crossed)
    level_three = norm_gain(stream_two, gain_three).astype(bf16)
    def with_other(values):
        return values, swap(values, "c")

    one_pair = with_other(level_one)
    attended_pair = with_other(attended)
    two_pair = with_other(level_two)
    text_pair = with_other(chip_text)
    crossed_pair = with_other(crossed)
    if square:
        zero_pair = with_other(level_zero)
        swapped = [
            pair[1]
            for pair in (one_pair, attended_pair, two_pair, text_pair, crossed_pair, zero_pair)
        ]
        up_slice = after(up_piece, *swapped)
        three_all = lax.all_gather(
            after(level_three, grad_all), all_plane, axis=0, tiled=False
        )
        down_slice = stack_by_device([after(part, level_three) for part in down_sent])
        hidden, activated = mlp_call(
            mlp_up_kernel,
            "mlp_up",
            [up_slice],
            [three_all],
            [(slice_rows, f32), (slice_rows, bf16)],
        )
    else:
        hidden = dot(up_t, level_three)
        activated = gelu_tanh(hidden).astype(bf16)

    if square:
        grad_hidden, part = mlp_call(
            mlp_back_kernel,
            "mlp_back",
            [down_slice.T, up_slice.T],
            [grad_all, hidden],
            [(slice_rows, bf16), (width, bf16)],
        )
        grad_level_three = lax.psum_scatter(part, all_plane, scatter_dimension=0, tiled=True)[0]
        down_grad = mlp_call(
            mlp_outer_kernel,
            "mlp_outer",
            [],
            [after(grad_all, part), activated],
            [],
            (width, slice_rows),
        )
        down_parts = exchange(
            [
                lax.dynamic_slice_in_dim(
                    down_grad, places[rank] * (width // 8), width // 8, 0
                )
                for rank in range(8)
            ]
        )
        up_grad = mlp_call(
            mlp_outer_kernel,
            "mlp_outer",
            [],
            [after(grad_hidden, down_grad), three_all],
            [],
            (slice_rows, width),
        )
        (out_part,) = mlp_call(
            mlp_down_kernel,
            "mlp_down",
            [down_slice],
            [after(activated, up_grad)],
            [(width, bf16)],
        )
        down_whole = stack_by_device([after(part, out_part) for part in down_parts])
        mlp_cut = pack(up_grad, down_whole, seq, lanes)
        grad_level_three = after(grad_level_three, mlp_cut).astype(f32)
    else:
        grad_act = dot(down_t, chip_grad, TN)
        _, gelu_pull = jax.vjp(gelu_tanh, hidden)
        grad_hidden = gelu_pull(grad_act)[0].astype(bf16)
        down_outer = outer_of((with_other(activated), [with_other(chip_grad)]))
        up_outer = outer_of((with_other(level_three), [with_other(grad_hidden)]))
        grad_level_three = dot(up_t, grad_hidden, TN)
        zero_pair = with_other(level_zero)
    _, pull_three = jax.vjp(norm_gain, stream_two, gain_three)
    grad_from_three, grad_gain_three = pull_three(grad_level_three)
    grad_stream_two = chip_grad.astype(f32) + grad_from_three
    cross_back = grad_stream_two.astype(bf16)
    grad_crossed = dot(cout_t, cross_back, TN).astype(bf16)
    grad_cross, grad_tk, grad_tv = attend_back(
        cross, grad_crossed, crossed, cross_inverse, text_keys, text_values
    )
    grad_memory_key = grad_tk[0] + swap(grad_tk[1], "c").astype(f32)
    grad_memory_value = grad_tv[0] + swap(grad_tv[1], "c").astype(f32)
    _, pull_memory = jax.vjp(head_norm, memory_key_flat)
    grad_memory_proj = jnp.concatenate(
        [pull_memory(grad_memory_key)[0], grad_memory_value], axis=0
    ).astype(bf16)
    _, pull_cq = jax.vjp(head_norm, cross_proj)
    grad_cq_flat = pull_cq(grad_cross)[0].astype(bf16)
    if square:
        def spread(values):
            cube = values.reshape(seq, -1, values.shape[1])
            cube = jnp.pad(cube, ((0, 0), (0, width // seq - cube.shape[1]), (0, 0)))
            return cube.reshape(width, -1)

        cross_outer = outer_of(
            (crossed_pair, [with_other(cross_back)]),
            (two_pair, [with_other(grad_cq_flat)]),
            (tuple(spread(text) for text in text_pair), [with_other(grad_memory_proj)]),
        )
        cross_sum = sum_far(cross_outer)
    else:
        cross_outer = outer_of(
            (crossed_pair, [with_other(cross_back)]), (two_pair, [with_other(grad_cq_flat)])
        )
        memory_outer = outer_of((text_pair, [with_other(grad_memory_proj)]))
    grad_level_two = dot(cq_t, grad_cq_flat, TN)
    _, pull_two = jax.vjp(norm_gain, stream_one, gain_two)
    grad_from_two, grad_gain_two = pull_two(grad_level_two)
    grad_stream_one = grad_stream_two + grad_from_two
    self_back = grad_stream_one.astype(bf16)
    grad_attended = dot(
        self_t, after(self_back, cross_outer[0]), TN
    ).astype(bf16)
    grad_q, grad_k, grad_v = attend_back(
        query, grad_attended, attended, self_inverse, keys, values
    )
    if square:
        cross_sum = sum_near(cross_sum, grad_q)
        out_sum = lax.psum_scatter(
            after(out_part, grad_level_three), all_plane, scatter_dimension=0, tiled=True
        )[0]
        blended = (stream_two + after(out_sum, grad_q).astype(f32)).astype(bf16)
        mlp_sum = lax.psum_scatter(
            after(mlp_cut, grad_level_three), "z", scatter_dimension=0, tiled=True
        )[0]
        grad_q = after(grad_q, blended, *cross_sum[3])
    grad_key = grad_k[0] + swap(grad_k[1], "c").astype(f32)
    grad_value_proj = (grad_v[0] + swap(grad_v[1], "c").astype(f32)).astype(bf16)
    _, pull_query = jax.vjp(prepare, query_flat)
    _, pull_key = jax.vjp(prepare, key_flat)
    grad_pair_proj = jnp.concatenate([pull_query(grad_q)[0], pull_key(grad_key)[0]], axis=0).astype(
        bf16
    )
    first_outer = outer_of(
        (attended_pair, [with_other(self_back)]),
        (one_pair, [with_other(grad_value_proj), with_other(grad_pair_proj)]),
    )
    if square:
        first_sum = sum_far(first_outer)
        cross_total = sum_three(cross_sum, first_outer[0])
        early = [cross_total, mlp_sum]
    else:
        early = []
        blended = (stream_two + dot(down_t, activated)).astype(bf16)
    grad_text_rows = dot(grad_memory_proj, memory_t, TN).astype(bf16)
    text_width = text_rows.shape[2]
    back = jnp.concatenate(
        [
            blended.T.reshape(lat_count, -1, width),
            jnp.pad(grad_text_rows, ((0, 0), (0, width - text_width))).reshape(
                lat_count, -1, width
            ),
        ],
        axis=1,
    )
    back = from_latent(back.reshape(-1, width), first_outer[0])
    blended_out = back[:, :local_rows]
    grad_text = back[:, local_rows:, :text_width].astype(f32)
    grad_pair_next = after(grad_pair_proj, first_outer[0])
    grad_level_one = dot(pair_t, grad_pair_next, TN) + dot(value_t, grad_value_proj, TN)
    _, pull_one = jax.vjp(shifted_norm, stream_zero, gain_one, shift)
    grad_from_one, grad_gain_one, grad_shift_part = pull_one(grad_level_one)
    skip_back = (grad_stream_one + grad_from_one).astype(bf16)
    if square:
        first_sum = sum_near(first_sum, skip_back)
        skip_sent = after(skip_back, back, *early).T
        skip_back_rows = from_latent(skip_sent, *first_sum[3]).reshape(tokens, width)
        own_back, other_back = with_other(skip_back_rows.T)
        own_sum, got_a, got_b, _ = first_sum
        stacked = stack_sum(
            seq, (cross_total,), (own_sum, after(got_a, skip_back_rows), got_b)
        )
        both_sum = [lax.psum_scatter(stacked, "z", scatter_dimension=0, tiled=True)[0]]
        skip_outer = outer_of((zero_pair, [(after(own_back, stacked), other_back)]))
        skip_sum = sum_far(skip_outer)
        skip_back_rows = after(skip_back_rows, skip_outer[0])
    else:
        skip_outer = outer_of((zero_pair, [with_other(skip_back)]))
        skip_back_rows = from_latent(skip_back.T).reshape(tokens, width)
    grad_level_zero = dot(skip_back_rows, skip_t, NN)
    if square:
        skip_sum = sum_near(skip_sum, grad_level_zero)
        late = skip_sum[3][0]
        up_rows, up_part = up_weight.shape[1], up_weight.shape[0]
        mlp_sum = after(mlp_sum, late).astype(f32)
        grad_up = mlp_sum[:up_rows, :up_part].T
        grad_down = (
            mlp_sum[up_rows:]
            .reshape(slice_rows // lanes, cores, -1, lanes)
            .transpose(1, 0, 3, 2)
            .reshape(cores * slice_rows, -1)
        )
        skip_sum = sum_z(skip_sum, late)
        late = skip_sum[0]
        grad_cout, grad_cq, grad_memory, grad_self, grad_value, grad_pair = sum_end(
            both_sum,
            [
                cross_output,
                cross_query,
                cross_memory,
                self_output,
                value_weight,
                query_key_weight,
            ],
            late,
        )
        grad_memory = grad_memory[: cross_memory.shape[0]]
        (grad_skip_w,) = sum_end(skip_sum, skip_set, grad_pair)
    else:
        (grad_down,) = sum_end(sum_plain(down_outer), down_set)
        (grad_up,) = sum_end(sum_plain(up_outer), up_set)
        grad_cout, grad_cq = sum_end(sum_plain(cross_outer), [cross_output, cross_query])
        (grad_memory,) = sum_end(sum_plain(memory_outer), memory_set)
        grad_self, grad_value, grad_pair = sum_end(
            sum_plain(first_outer), [self_output, value_weight, query_key_weight]
        )
        (grad_skip_w,) = sum_end(sum_plain(skip_outer), skip_set)

    joined_rows = jnp.concatenate([inputs, skipped], axis=-1).astype(f32).reshape(tokens, -1)
    _, pull_zero = jax.vjp(norm_gain_rows, joined_rows, gain_skip)
    grad_joined, grad_gain_skip = pull_zero(grad_level_zero)
    grad_input = grad_joined[:, :width].reshape(inputs.shape)
    grad_skipped = grad_joined[:, width:].reshape(inputs.shape)
    small = jnp.concatenate(
        [grad_shift_part, grad_gain_skip, grad_gain_one, grad_gain_two, grad_gain_three]
    ).reshape(-1, width)
    if square:
        small = jnp.concatenate([after(small, late), condition.astype(f32)], axis=0)
        held = jnp.zeros((8,) + small.shape, f32)
        for rank in range(8):
            arrived = to_rank(small, rank) if rank else small
            held = lax.dynamic_update_slice(held, arrived[None], (places[rank], 0, 0))
        shift_plane = held[:, 0].reshape(plane, cores, width).sum(axis=1)
        gain_plane = sum(held[i, 1:-lat_count] for i in range(8))
        cond_rows = held[:, -lat_count:].reshape(-1, width)
        sums = after(jnp.concatenate([gain_plane, shift_plane], axis=0), *skip_sum)
        columns = z_order(z_send(sums))
        gain_rows = len(gain_plane)
        grad_gains = sum(column[:gain_rows] for column in columns).reshape(-1)
        shift_grads = jnp.stack([column[gain_rows:] for column in columns], axis=1)
        shift_grads = shift_grads.reshape(-1, width)
    else:
        cond_rows = gather_rows(condition, ("c", "b", "a")).astype(f32)
        grad_gains = lax.psum(small[1:], ("a", "b", "c", "z")).reshape(-1)
        shift_grads = lax.all_gather(lax.psum(small[:1], "c"), ("a", "b", "z"), axis=0, tiled=True)
    cond_act = jax.nn.silu(cond_rows).astype(bf16)
    block_in, block_out = shift_weight.shape
    cond_block = lax.dynamic_slice_in_dim(cond_act, at_z * block_in, block_in, 1).astype(f32)
    own_columns = ((at_a * inner + at_b) * cores + at_c) * block_out
    grad_shift = jnp.dot(
        cond_block.T,
        lax.dynamic_slice_in_dim(shift_grads, own_columns, block_out, 1),
        precision=lax.Precision.HIGHEST,
    )

    return (
        blended_out,
        grad_input,
        grad_skipped,
        grad_text,
        grad_gains,
        grad_skip_w,
        grad_shift,
        grad_pair,
        grad_value,
        grad_self,
        grad_cq,
        grad_memory,
        grad_cout,
        grad_up,
        grad_down,
    )


def solution(mesh):
    dp, seq = mesh.shape["dp"], mesh.shape["seq"]
    inner, cores = 2, 2
    sizes = (dp // (inner * cores), inner, cores, seq)
    split = Mesh(mesh.devices.reshape(sizes), ("a", "b", "c", "z"))
    rows = P(("a", "b", "c"), "z", None)
    blocks = P("z", ("a", "b", "c"))
    return jax.shard_map(
        functools.partial(on_device, sizes),
        mesh=split,
        in_specs=(rows, rows, rows, P(("a", "b", "c"), None), rows, P()) + (blocks,) * 10,
        out_specs=(rows, rows, rows, rows, P()) + (blocks,) * 10,
        check_vma=False,
    )
```
